128 devices in a mesh: section: 2 (over core), dp: 64 (over z, y, x).
Axes of the slice: x: 4, y: 4, z: 4, core: 2. Of those that a mesh axis runs over, the one named last changes fastest.
Arguments:
- tokens: bfloat16 [2, 128, 256, 512], P(None, 'dp'), may hold values from -6 to 6
- lengths: int32 [2, 128], P(None, 'dp'), may hold values from 32 to 256, as said below
- out_cotangent: bfloat16 [2, 128, 256, 512], P(None, 'dp'), may hold values from -6 to 6
- pos_table: bfloat16 [2, 256, 512], P('section'), may hold values from -3 to 3
- w_qkv: bfloat16 [2, 512, 1536], P('section'), may hold values from -0.25 to 0.25
- w_out: bfloat16 [2, 512, 512], P('section'), may hold values from -1 to 1
- b_out: bfloat16 [2, 512], P('section'), may hold values from -2 to 2
- norm1_gain: bfloat16 [2, 512], P('section'), may hold values from 0.25 to 1.75
- norm1_bias: bfloat16 [2, 512], P('section'), may hold values from -2 to 2
- w_up: bfloat16 [2, 512, 2048], P('section'), may hold values from -0.25 to 0.25
- b_up: bfloat16 [2, 2048], P('section'), may hold values from -3 to 3
- w_down: bfloat16 [2, 2048, 512], P('section'), may hold values from -0.125 to 0.125
- b_down: bfloat16 [2, 512], P('section'), may hold values from -2 to 2
- norm2_gain: bfloat16 [2, 512], P('section'), may hold values from 0.25 to 1.75
- norm2_bias: bfloat16 [2, 512], P('section'), may hold values from -2 to 2
Outputs:
- output: bfloat16 [2, 128, 256, 512], P('section', 'dp')
- input_grad: bfloat16 [2, 128, 256, 512], P('section', 'dp')
- grad_pos_table: float32 [2, 256, 512], P('section')
- grad_w_qkv: float32 [2, 512, 1536], P('section')
- grad_w_out: float32 [2, 512, 512], P('section')
- grad_b_out: float32 [2, 512], P('section')
- grad_norm1_gain: float32 [2, 512], P('section')
- grad_norm1_bias: float32 [2, 512], P('section')
- grad_w_up: float32 [2, 512, 2048], P('section')
- grad_b_up: float32 [2, 2048], P('section')
- grad_w_down: float32 [2, 2048, 512], P('section')
- grad_b_down: float32 [2, 512], P('section')
- grad_norm2_gain: float32 [2, 512], P('section')
- grad_norm2_bias: float32 [2, 512], P('section')
The draws below stay inside these ranges and needn't reach their ends.
Inputs may be any that keep to these rules, and one draw needn't show every extreme that they name: `lengths`: some window has all 256 characters in use in every draw.
All inputs are finite; a program needn't handle non-finite values.
Results may differ from the reference program's by a relative error of at most 0.02.
Values may be sent and summed in bfloat16 or wider, within the bound.
No kernel may reach another device: no remote copies, remote signals or barrier semaphores. Data moves between devices by JAX's collectives and lax.ppermute only.
A program may use at most 192 MiB of HBM per device.

```python
import jax
import jax.numpy as jnp
from jax import lax

D = 512
HEADS = 8
FF = 2048
HEAD_DIM = 64
WIN = 256
MB = 2
WINDOWS = 128
LAYERS = 2


def draw_lengths(key, part):
    key = jax.random.fold_in(key, 7)
    first_key, second_key = jax.random.split(key)
    shorter = jax.random.randint(first_key, (MB, WINDOWS), WIN // 8, WIN + 1)
    is_full = jax.random.randint(second_key, (MB, WINDOWS), 0, 5) < 3
    chosen = jnp.where(is_full, WIN, shorter)
    return chosen.at[0, 0].set(WIN).astype(jnp.int32)


def block_scale(rng, extent, pieces, least, top_value):
    def one(axis_at, blocks):
        heights = jax.random.uniform(jax.random.fold_in(jax.random.fold_in(rng, 6), axis_at), (blocks,), jnp.float32, least / len(pieces), top_value / len(pieces))
        return jnp.repeat(jnp.exp(heights), extent[axis_at] // blocks).reshape((-1,) + (1,) * (len(extent) - axis_at - 1))

    loudness = one(*pieces[0])
    for cut in pieces[1:]:
        loudness = loudness * one(*cut)
    return loudness


def centred(stream_key, extent, scale, limit, cuts=(), held_as=jnp.bfloat16):
    values = jax.random.normal(stream_key, extent, jnp.float32) * scale
    if len(cuts) > 0:
        values = block_scale(stream_key, extent, cuts, -0.22, 0.18) * values
    return jnp.clip(values, min=-limit, max=limit).astype(held_as)


def setup_inputs(seed: int = 0) -> dict:
    seeds = jax.random.split(jax.random.key(seed), 16)
    return {
        "tokens": centred(seeds[0], (MB, WINDOWS, WIN, D), 1.0, 6.0, ((1, 64),)),
        "lengths": draw_lengths(jax.random.fold_in(seeds[15], 71), 0),
        "out_cotangent": centred(seeds[2], (MB, WINDOWS, WIN, D), 1.0, 6.0, ((1, 64),)),
        "pos_table": centred(seeds[3], (LAYERS, WIN, D), 0.5, 3.0, ((0, 2),)),
        "w_qkv": centred(seeds[4], (LAYERS, D, 3 * D), D ** -0.5, 0.25, ((0, 2),)),
        "w_out": centred(seeds[5], (LAYERS, D, D), (D // 16) ** -0.5, 1.0, ((0, 2),)),
        "b_out": centred(seeds[6], (LAYERS, D), 0.3, 2.0, ((0, 2),)),
        "norm1_gain": jnp.clip(1.0 + 0.15 * jax.random.normal(seeds[7], (LAYERS, D), jnp.float32), 0.25, 1.75).astype(jnp.bfloat16),
        "norm1_bias": centred(seeds[8], (LAYERS, D), 0.3, 2.0, ((0, 2),)),
        "w_up": centred(seeds[9], (LAYERS, D, FF), D ** -0.5, 0.25, ((0, 2),)),
        "b_up": centred(seeds[10], (LAYERS, FF), 0.5, 3.0, ((0, 2),)),
        "w_down": centred(seeds[11], (LAYERS, FF, D), FF ** -0.5, 0.125, ((0, 2),)),
        "b_down": centred(seeds[12], (LAYERS, D), 0.3, 2.0, ((0, 2),)),
        "norm2_gain": jnp.clip(1.0 + 0.15 * jax.random.normal(seeds[13], (LAYERS, D), jnp.float32), 0.25, 1.75).astype(jnp.bfloat16),
        "norm2_bias": centred(seeds[14], (LAYERS, D), 0.3, 2.0, ((0, 2),)),
    }


@jax.custom_vjp
def low(v):
    return lax.optimization_barrier(v.astype(jnp.bfloat16)).astype(jnp.float32)

@jax.custom_vjp
def low_back(v):
    return v

def low_keep(v):
    return (low(v), None)

def low_pass(kept, grad):
    return (grad,)

def back_keep(v):
    return (v, None)

def back_low(kept, grad):
    return (low(grad),)
low.defvjp(low_keep, low_pass)
low_back.defvjp(back_keep, back_low)

def matmul(left_side, right_side):
    return jnp.einsum('...i,ij->...j', left_side, right_side, precision=lax.Precision.HIGHEST)

def normalize(entries):
    center = entries - lax.optimization_barrier(jnp.mean(entries, -1, keepdims=True))
    return center * lax.rsqrt(lax.optimization_barrier(jnp.mean(center * center, -1, keepdims=True)) + 1e-05)

def allowed(lengths_now, window):
    places = jnp.arange(window)
    causal = places[None, :] <= places[:, None]
    inside = places[None, None, None, :] < lengths_now[:, None, None, None]
    return causal[None, None] & inside

def apply_layer(stream, lengths_now, weights):
    position, w_qkv, w_out, b_out, gain_one, shift_one, w_up, b_up, w_down, b_down, gain_two, shift_two = weights
    window_count, window, model_width = stream.shape
    hidden = stream + position
    project = low_back(low(matmul(low(hidden), w_qkv)))
    query_rows = project[..., :model_width].reshape(window_count, window, HEADS, HEAD_DIM)
    key_rows = project[..., model_width:2 * model_width].reshape(window_count, window, HEADS, HEAD_DIM)
    value_rows = project[..., 2 * model_width:].reshape(window_count, window, HEADS, HEAD_DIM)
    scores = jnp.einsum('wqhe,wkhe->whqk', query_rows, key_rows, precision=lax.Precision.HIGHEST)
    scores = low_back(scores * HEAD_DIM ** (-0.5))
    scores = jnp.where(allowed(lengths_now, window), scores, -1e+30)
    raised = jnp.exp(scores - lax.optimization_barrier(jnp.max(scores, -1, keepdims=True)))
    soft_weights = raised / lax.optimization_barrier(jnp.sum(raised, -1, keepdims=True))
    mixed_heads = jnp.einsum('whqk,wkhe->wqhe', low(soft_weights), value_rows, precision=lax.Precision.HIGHEST)
    mixed_heads = low_back(low(mixed_heads)).reshape(window_count, window, model_width)
    branch = low_back(matmul(mixed_heads, w_out) + b_out)
    after_attn = normalize(hidden + branch) * gain_one + shift_one
    up_value = low_back(matmul(low(after_attn), w_up) + b_up)
    outcome = low_back(matmul(low(jax.nn.gelu(up_value, approximate=True)), w_down) + b_down)
    return normalize(after_attn + outcome) * gain_two + shift_two

def reference(tokens, lengths, out_cotangent, pos_table, w_qkv, w_out, b_out, norm1_gain, norm1_bias, w_up, b_up, w_down, b_down, norm2_gain, norm2_bias):
    params = tuple((entry.astype(jnp.float32) for entry in (pos_table, w_qkv, w_out, b_out, norm1_gain, norm1_bias, w_up, b_up, w_down, b_down, norm2_gain, norm2_bias)))

    def network(stream, lengths_now, weights):
        for layer_no in range(LAYERS):
            stream = apply_layer(stream, lengths_now, tuple((entry[layer_no] for entry in weights)))
            if layer_no + 1 < LAYERS:
                stream = low_back(low(stream))
        return stream

    def one_batch(totals, sliced):
        batch_tokens, lengths_now, cotangent = sliced
        keep_rows = (jnp.arange(WIN)[None, :] < lengths_now[:, None]).astype(jnp.float32)[..., None]
        result, pullback = jax.vjp(lambda stream, weights: network(stream, lengths_now, weights), batch_tokens.astype(jnp.float32), params)
        grad_tokens, grad_params = pullback(cotangent.astype(jnp.float32) * keep_rows)
        totals = tuple((running + addition for running, addition in zip(totals, grad_params)))
        return (totals, ((result * keep_rows).astype(jnp.bfloat16), grad_tokens.astype(jnp.bfloat16)))
    zeros_init = tuple((jnp.zeros(entry.shape, jnp.float32) for entry in params))
    totals, (output, input_grad) = lax.scan(one_batch, zeros_init, (tokens, lengths, out_cotangent))
    return (output, input_grad, totals[0], totals[1], totals[2], totals[3], totals[4], totals[5], totals[6], totals[7], totals[8], totals[9], totals[10], totals[11])
```

```python
import jax
import jax.numpy as jnp
from jax import lax
from jax.experimental import pallas as pl
from jax.experimental.pallas import tpu as pltpu
from jax.sharding import Mesh, PartitionSpec as P

HEADS = 8
D = 512
FF = 2048
WIN = 256
ROWS = 512
F32 = jnp.float32
BF16 = jnp.bfloat16
VMEM_LIMIT = 60 * 1024 * 1024

ANY = pl.BlockSpec(memory_space=pl.ANY)
VM = pl.BlockSpec(memory_space=pltpu.VMEM)
SM = pl.BlockSpec(memory_space=pltpu.SMEM)
PARAMS = pltpu.CompilerParams(vmem_limit_bytes=VMEM_LIMIT)


def nn(a, b):
    return lax.dot_general(a, b, (((1,), (0,)), ((), ())), preferred_element_type=F32)


def nt(a, b):
    return lax.dot_general(a, b, (((1,), (1,)), ((), ())), preferred_element_type=F32)


def tn(a, b):
    return lax.dot_general(a, b, (((0,), (0,)), ((), ())), preferred_element_type=F32)


def start_pick(near, mine, other, dst, sem):
    @pl.when(near)
    def _():
        pltpu.make_async_copy(mine, dst, sem).start()

    @pl.when(jnp.logical_not(near))
    def _():
        pltpu.make_async_copy(other, dst, sem).start()


def wait_for(src, dst, sem):
    pltpu.make_async_copy(src, dst, sem).wait()


def normalize(v):
    center = v - jnp.mean(v, -1, keepdims=True)
    inverse = lax.rsqrt(jnp.mean(center * center, -1, keepdims=True) + 1e-05)
    return center * inverse, inverse


def norm_backward(e, normed, inverse, gain):
    scaled = e * gain
    return inverse * (
        scaled
        - jnp.mean(scaled, -1, keepdims=True)
        - normed * jnp.mean(scaled * normed, -1, keepdims=True)
    )


def gelu_pair(v):
    c = 0.7978845608028654
    sq = v * v
    t = jnp.tanh(v * (c + (c * 0.044715) * sq))
    half = 0.5 + 0.5 * t
    slope = half + (0.5 * v) * (1.0 - t * t) * (c + (3.0 * c * 0.044715) * sq)
    return v * half, slope


def attn_fwd_kernel(
    layer,
    sec_ref,
    len_ref,
    stream_in,
    pos_m,
    pos_o,
    wq_m,
    wq_o,
    wo_m,
    wo_o,
    vec_m,
    vec_o,
    project_ref,
    probs_ref,
    mixed_ref,
    sum_one_ref,
    stream,
    pos,
    wq,
    wo,
    vec,
    hidden,
    mask,
    sems,
):
    sec = sec_ref[0]
    near = sec == layer
    src = stream_in.at[sec] if layer == 0 else stream_in
    first = pltpu.make_async_copy(src, stream, sems.at[0])
    first.start()
    start_pick(near, pos_m.at[0], pos_o.at[0], pos, sems.at[1])
    start_pick(near, wq_m.at[0], wq_o.at[0], wq, sems.at[2])
    start_pick(near, vec_m, vec_o, vec, sems.at[4])
    start_pick(near, wo_m.at[0], wo_o.at[0], wo, sems.at[3])
    rows = lax.broadcasted_iota(jnp.int32, (WIN, WIN), 0)
    cols = lax.broadcasted_iota(jnp.int32, (WIN, WIN), 1)
    for w in range(2):
        inside = (cols <= rows) & (cols < len_ref[sec, w])
        mask[w] = jnp.where(inside, 0.0, -1e30)
    first.wait()
    wait_for(pos_m.at[0], pos, sems.at[1])
    place = pos[...].astype(F32)
    for w in range(2):
        hidden[w * WIN : (w + 1) * WIN, :] = stream[w].astype(F32) + place
    hidden_low = hidden[...].astype(BF16)
    wait_for(wq_m.at[0], wq, sems.at[2])
    for c in range(3):
        project_ref[:, c * D : (c + 1) * D] = nn(hidden_low, wq[:, c * D : (c + 1) * D]).astype(
            BF16
        )
    lanes = lax.broadcasted_iota(jnp.int32, (WIN, 128), 1)

    def attend(step, carry):
        w = step // 4
        p = step % 4
        at_row = pl.ds(pl.multiple_of(w * WIN, WIN), WIN)
        at = pl.multiple_of(p * 128, 128)
        q2 = project_ref[at_row, pl.ds(at, 128)] * jnp.asarray(0.125, BF16)
        k2 = project_ref[at_row, pl.ds(pl.multiple_of(D + p * 128, 128), 128)]
        v2 = project_ref[at_row, pl.ds(pl.multiple_of(2 * D + p * 128, 128), 128)]
        blocked = mask[w]
        parts = []
        for h in range(2):
            own = (lanes >= 64) if h else (lanes < 64)
            qm = jnp.where(own, q2, jnp.zeros_like(q2))
            scores = nt(qm, k2) + blocked
            raised = jnp.exp(scores - jnp.max(scores, -1, keepdims=True))
            soft = (raised * (1.0 / jnp.sum(raised, -1, keepdims=True))).astype(BF16)
            probs_ref[step * 2 + h] = soft
            parts.append(nn(soft, v2))
        mixed_ref[at_row, pl.ds(at, 128)] = jnp.where(lanes < 64, parts[0], parts[1]).astype(BF16)
        return carry

    lax.fori_loop(0, 8, attend, 0)
    wait_for(wo_m.at[0], wo, sems.at[3])
    wait_for(vec_m, vec, sems.at[4])
    sum_one_ref[...] = hidden[...] + (nn(mixed_ref[...], wo[...]) + vec[0:1, :].astype(F32))


def ffn_fwd_kernel(
    layer,
    sec_ref,
    len_ref,
    wu_m,
    wu_o,
    wd_m,
    wd_o,
    vec_m,
    vec_o,
    sum_one_ref,
    low_ref,
    active_ref,
    slope_ref,
    sum_two_ref,
    out_ref,
    wu,
    wd,
    vec,
    acc,
    sems,
):
    sec = sec_ref[0]
    near = sec == layer
    start_pick(near, vec_m, vec_o, vec, sems.at[2])
    start_pick(near, wu_m.at[0], wu_o.at[0], wu, sems.at[0])
    start_pick(near, wd_m.at[0], wd_o.at[0], wd, sems.at[1])
    normed, _ = normalize(sum_one_ref[...])
    wait_for(vec_m, vec, sems.at[2])
    small = vec[...].astype(F32)
    after = normed * small[1:2] + small[2:3]
    acc[...] = after
    low = after.astype(BF16)
    low_ref[...] = low
    wait_for(wu_m.at[0], wu, sems.at[0])
    wait_for(wd_m.at[0], wd, sems.at[1])
    for c in range(4):
        block = slice(c * D, (c + 1) * D)
        value = nn(low, wu[:, block]) + small[6 + c : 7 + c]
        active, slope = gelu_pair(value)
        active = active.astype(BF16)
        active_ref[:, block] = active
        slope_ref[:, block] = slope.astype(BF16)
        acc[...] += nn(active, wd[block, :])
    sum_two = acc[...] + small[3:4]
    sum_two_ref[...] = sum_two
    normed, _ = normalize(sum_two)
    result = normed * small[4:5] + small[5:6]
    for w in range(2):
        part = result[w * WIN : (w + 1) * WIN]
        if layer == 1:
            at_row = lax.broadcasted_iota(jnp.int32, (WIN, D), 0)
            part = jnp.where(at_row < len_ref[sec, w], part, 0.0)
        out_ref[w] = part.astype(BF16)


def sds(shape, dtype):
    return jax.ShapeDtypeStruct(shape, dtype)


def attn_forward(layer, sec, lengths, stream, mine, other):
    args = [sec, lengths, stream]
    for i in (0, 1, 2, 5):
        args += [mine[i], other[i]]

    def body(*refs):
        attn_fwd_kernel(layer, *refs)

    return pl.pallas_call(
        body,
        out_shape=[
            sds((ROWS, 3 * D), BF16),
            sds((16, WIN, WIN), BF16),
            sds((ROWS, D), BF16),
            sds((ROWS, D), F32),
        ],
        in_specs=[SM, SM] + [ANY] * (len(args) - 2),
        out_specs=[VM] * 4,
        scratch_shapes=[
            pltpu.VMEM((2, WIN, D), BF16),
            pltpu.VMEM((WIN, D), BF16),
            pltpu.VMEM((D, 3 * D), BF16),
            pltpu.VMEM((D, D), BF16),
            pltpu.VMEM((16, D), BF16),
            pltpu.VMEM((ROWS, D), F32),
            pltpu.VMEM((2, WIN, WIN), F32),
            pltpu.SemaphoreType.DMA((5,)),
        ],
        compiler_params=PARAMS,
        cost_estimate=pl.CostEstimate(
            flops=4_000_000_000, bytes_accessed=10_000_000, transcendentals=1_000_000
        ),
        name=f"attention_forward_{layer}",
    )(*args)


def ffn_forward(layer, sec, lengths, sum_one, mine, other):
    args = [sec, lengths]
    for i in (3, 4, 5):
        args += [mine[i], other[i]]
    args += [sum_one]

    def body(*refs):
        ffn_fwd_kernel(layer, *refs)

    return pl.pallas_call(
        body,
        out_shape=[
            sds((ROWS, D), BF16),
            sds((ROWS, FF), BF16),
            sds((ROWS, FF), BF16),
            sds((ROWS, D), F32),
            sds((2, WIN, D), BF16),
        ],
        in_specs=[SM, SM] + [ANY] * 6 + [VM],
        out_specs=[VM] * 5,
        scratch_shapes=[
            pltpu.VMEM((D, FF), BF16),
            pltpu.VMEM((FF, D), BF16),
            pltpu.VMEM((16, D), BF16),
            pltpu.VMEM((ROWS, D), F32),
            pltpu.SemaphoreType.DMA((3,)),
        ],
        compiler_params=PARAMS,
        cost_estimate=pl.CostEstimate(
            flops=4_000_000_000, bytes_accessed=10_000_000, transcendentals=1_000_000
        ),
        name=f"ffn_forward_{layer}",
    )(*args)


def fwd_layer(layer, sec, lengths, stream, mine, other):
    first = attn_forward(layer, sec, lengths, stream, mine, other)
    return list(first) + list(ffn_forward(layer, sec, lengths, first[3], mine, other))


def ffn_kernel(
    layer,
    sec_ref,
    len_ref,
    up_in,
    wu_m,
    wu_o,
    wd_m,
    wd_o,
    vec_m,
    vec_o,
    low_ref,
    active_ref,
    slope_ref,
    sum_two_ref,
    grad_after_ref,
    keep_ref,
    send_ref,
    small_ref,
    arriving,
    wu,
    wd,
    vec,
    acc,
    grads,
    sems,
    osems,
):
    sec = sec_ref[0]
    near = sec == layer
    src = up_in.at[sec] if layer == 1 else up_in
    first = pltpu.make_async_copy(src, arriving, sems.at[0])
    first.start()
    start_pick(near, vec_m, vec_o, vec, sems.at[1])
    start_pick(near, wd_m.at[0], wd_o.at[0], wd, sems.at[2])
    start_pick(near, wu_m.at[0], wu_o.at[0], wu, sems.at[3])
    normed, inverse = normalize(sum_two_ref[...])
    first.wait()
    parts = []
    for w in range(2):
        part = arriving[w].astype(F32)
        if layer == 1:
            at_row = lax.broadcasted_iota(jnp.int32, (WIN, D), 0)
            part = jnp.where(at_row < len_ref[sec, w], part, 0.0)
        parts.append(part)
    e = jnp.concatenate(parts, 0)
    wait_for(vec_m, vec, sems.at[1])
    gain = vec[4:5, :].astype(F32)
    small_ref[...] = jnp.zeros_like(small_ref)
    small_ref[1:2, :] = jnp.sum(e * normed, 0, keepdims=True)
    small_ref[2:3, :] = jnp.sum(e, 0, keepdims=True)
    grad_sum = norm_backward(e, normed, inverse, gain)
    acc[...] = grad_sum
    grad_low = grad_sum.astype(BF16)
    small_ref[0:1, :] = jnp.sum(grad_low.astype(F32), 0, keepdims=True)
    wait_for(wd_m.at[0], wd, sems.at[2])
    wait_for(wu_m.at[0], wu, sems.at[3])
    for c in range(4):
        block = slice(c * D, (c + 1) * D)
        grad_up = nt(grad_low, wd[block, :]) * slope_ref[:, block].astype(F32)
        grad_up = grad_up.astype(BF16)
        small_ref[3 + c : 4 + c, :] = jnp.sum(grad_up.astype(F32), 0, keepdims=True)
        acc[...] += nt(grad_up, wu[:, block])
        grad_wu = tn(low_ref[...], grad_up).astype(BF16)
        grad_wd = tn(active_ref[:, block], grad_low).astype(BF16)
        for k in range(4):
            at = slice((c * 4 + k) * D, (c * 4 + k + 1) * D)
            grads[0, at, :] = grad_wu[:, k * 128 : (k + 1) * 128]
            grads[1, at, :] = grad_wd[:, k * 128 : (k + 1) * 128]
    kept = pltpu.make_async_copy(grads.at[sec], keep_ref, osems.at[0])
    sent = pltpu.make_async_copy(grads.at[1 - sec], send_ref, osems.at[1])
    kept.start()
    sent.start()
    grad_after_ref[...] = acc[...]
    kept.wait()
    sent.wait()


def ffn_back(layer, sec, lengths, arriving, mine, other, kept):
    args = [sec, lengths, arriving]
    for i in (3, 4, 5):
        args += [mine[i], other[i]]
    args += list(kept[4:8])

    def body(*refs):
        ffn_kernel(layer, *refs)

    return pl.pallas_call(
        body,
        out_shape=[
            sds((ROWS, D), F32),
            sds((8192, 128), BF16),
            sds((8192, 128), BF16),
            sds((8, D), F32),
        ],
        in_specs=[SM, SM] + [ANY] * 7 + [VM] * 4,
        out_specs=[VM, ANY, ANY, VM],
        scratch_shapes=[
            pltpu.VMEM((2, WIN, D), BF16),
            pltpu.VMEM((D, FF), BF16),
            pltpu.VMEM((FF, D), BF16),
            pltpu.VMEM((16, D), BF16),
            pltpu.VMEM((ROWS, D), F32),
            pltpu.VMEM((2, 8192, 128), BF16),
            pltpu.SemaphoreType.DMA((4,)),
            pltpu.SemaphoreType.DMA((2,)),
        ],
        compiler_params=PARAMS,
        cost_estimate=pl.CostEstimate(
            flops=5_000_000_000, bytes_accessed=20_000_000, transcendentals=0
        ),
        name=f"ffn_backward_{layer}",
    )(*args)


def attn_kernel(
    layer,
    sec_ref,
    grad_after_ref,
    stream_in,
    pos_m,
    pos_o,
    wq_m,
    wq_o,
    wo_m,
    wo_o,
    vec_m,
    vec_o,
    project_ref,
    probs_ref,
    mixed_ref,
    sum_one_ref,
    small_in,
    grad_low_ref,
    keep_ref,
    send_ref,
    stream,
    pos,
    wq,
    wo,
    vec,
    total,
    grad_mixed,
    grad_project,
    grads,
    sems,
    osems,
):
    sec = sec_ref[0]
    near = sec == layer
    start_pick(near, wo_m.at[0], wo_o.at[0], wo, sems.at[0])
    start_pick(near, vec_m, vec_o, vec, sems.at[1])
    start_pick(near, wq_m.at[0], wq_o.at[0], wq, sems.at[2])
    start_pick(near, pos_m.at[0], pos_o.at[0], pos, sems.at[3])
    src = stream_in.at[sec] if layer == 0 else stream_in
    last = pltpu.make_async_copy(src, stream, sems.at[4])
    last.start()
    normed, inverse = normalize(sum_one_ref[...])
    e = grad_after_ref[...]
    wait_for(vec_m, vec, sems.at[1])
    gain = vec[1:2, :].astype(F32)
    row_norm = jnp.sum(e * normed, 0, keepdims=True)
    row_shift = jnp.sum(e, 0, keepdims=True)
    grad_sum = norm_backward(e, normed, inverse, gain)
    total[...] = grad_sum
    branch = grad_sum.astype(BF16)
    row_out = jnp.sum(branch.astype(F32), 0, keepdims=True)
    rows = jnp.concatenate([row_out, row_norm, row_shift], 0)
    rows = jnp.concatenate([rows, jnp.zeros((5, D), F32), small_in[...]], 0).astype(BF16)
    wait_for(wo_m.at[0], wo, sems.at[0])
    grad_mixed[...] = nt(branch, wo[...]).astype(BF16)
    grad_out = tn(mixed_ref[...], branch).astype(BF16)
    for c in range(4):
        lanes_at = slice(c * 128, (c + 1) * 128)
        grads[1, 2048 + c * D : 2048 + (c + 1) * D, :] = grad_out[:, lanes_at]
        for half in range(2):
            grads[half, 4608 + c * 16 : 4608 + (c + 1) * 16, :] = rows[:, lanes_at]
    for half in range(2):
        grads[half, 4672:5120, :] = jnp.zeros((448, 128), BF16)
    lanes = lax.broadcasted_iota(jnp.int32, (WIN, 128), 1)

    def attend(step, carry):
        w = step // 4
        p = step % 4
        at_row = pl.ds(pl.multiple_of(w * WIN, WIN), WIN)
        at = pl.ds(pl.multiple_of(p * 128, 128), 128)
        at_k = pl.ds(pl.multiple_of(D + p * 128, 128), 128)
        at_v = pl.ds(pl.multiple_of(2 * D + p * 128, 128), 128)
        q2 = project_ref[at_row, at] * jnp.asarray(0.125, BF16)
        k2 = project_ref[at_row, at_k]
        v2 = project_ref[at_row, at_v]
        g2 = grad_mixed[at_row, at]
        grad_q = []
        grad_k = []
        grad_v = []
        for h in range(2):
            own = (lanes >= 64) if h else (lanes < 64)
            none = jnp.zeros_like(q2)
            gm = jnp.where(own, g2, none)
            qm = jnp.where(own, q2, none)
            soft_low = probs_ref[step * 2 + h]
            soft = soft_low.astype(F32)
            product = soft * nt(gm, v2)
            grad_scores = (product - soft * jnp.sum(product, -1, keepdims=True)).astype(BF16)
            grad_q.append(nn(grad_scores, k2))
            grad_k.append(tn(grad_scores, qm))
            grad_v.append(tn(soft_low, gm))
        first_half = lanes < 64
        grad_project[at_row, at] = (
            jnp.where(first_half, grad_q[0], grad_q[1]) * 0.125
        ).astype(BF16)
        grad_project[at_row, at_k] = (grad_k[0] + grad_k[1]).astype(BF16)
        grad_project[at_row, at_v] = (grad_v[0] + grad_v[1]).astype(BF16)
        return carry

    lax.fori_loop(0, 8, attend, 0)
    last.wait()
    wait_for(pos_m.at[0], pos, sems.at[3])
    place = pos[...].astype(F32)
    hidden_low = jnp.concatenate(
        [(stream[w].astype(F32) + place).astype(BF16) for w in range(2)], 0
    )
    wait_for(wq_m.at[0], wq, sems.at[2])
    for j in range(3):
        block = slice(j * D, (j + 1) * D)
        part = grad_project[:, block]
        total[...] += nt(part, wq[:, block])
        grad_w = tn(hidden_low, part).astype(BF16)
        half, base = ((0, 0), (0, 2048), (1, 0))[j]
        for c in range(4):
            grads[half, base + c * D : base + (c + 1) * D, :] = grad_w[:, c * 128 : (c + 1) * 128]
    for w in range(2):
        grad_low_ref[w] = total[w * WIN : (w + 1) * WIN, :].astype(BF16)
    grad_pos = (total[0:WIN, :] + total[WIN : 2 * WIN, :]).astype(BF16)
    for half in range(2):
        for c in range(4):
            grads[half, 4096 + c * 128 : 4096 + (c + 1) * 128, :] = grad_pos[
                half * 128 : (half + 1) * 128, c * 128 : (c + 1) * 128
            ]
    kept = pltpu.make_async_copy(grads.at[sec], keep_ref, osems.at[0])
    sent = pltpu.make_async_copy(grads.at[1 - sec], send_ref, osems.at[1])
    kept.start()
    sent.start()
    kept.wait()
    sent.wait()


def attn_back(layer, sec, grad_after, stream, mine, other, kept, small):
    args = [sec, grad_after, stream]
    for i in (0, 1, 2, 5):
        args += [mine[i], other[i]]
    args += [kept[0], kept[1], kept[2], kept[3], small]

    def body(*refs):
        attn_kernel(layer, *refs)

    return pl.pallas_call(
        body,
        out_shape=[
            sds((2, WIN, D), BF16),
            sds((5120, 128), BF16),
            sds((5120, 128), BF16),
        ],
        in_specs=[SM, VM] + [ANY] * 9 + [VM] * 5,
        out_specs=[VM, ANY, ANY],
        scratch_shapes=[
            pltpu.VMEM((2, WIN, D), BF16),
            pltpu.VMEM((WIN, D), BF16),
            pltpu.VMEM((D, 3 * D), BF16),
            pltpu.VMEM((D, D), BF16),
            pltpu.VMEM((16, D), BF16),
            pltpu.VMEM((ROWS, D), F32),
            pltpu.VMEM((ROWS, D), BF16),
            pltpu.VMEM((ROWS, 3 * D), BF16),
            pltpu.VMEM((2, 5120, 128), BF16),
            pltpu.SemaphoreType.DMA((5,)),
            pltpu.SemaphoreType.DMA((2,)),
        ],
        compiler_params=PARAMS,
        cost_estimate=pl.CostEstimate(
            flops=4_000_000_000, bytes_accessed=15_000_000, transcendentals=0
        ),
        name=f"attention_backward_{layer}",
    )(*args)


def pack_vectors(b_out, gain_one, shift_one, b_down, gain_two, shift_two, b_up):
    def body(*refs):
        out = refs[-1]
        rows = [ref[...].astype(F32) for ref in refs[:6]]
        wide = refs[6][...].astype(F32)
        rows += [wide[:, c * D : (c + 1) * D] for c in range(4)]
        rows += [jnp.zeros((6, D), F32)]
        out[...] = jnp.concatenate(rows, 0).astype(BF16)

    return pl.pallas_call(
        body,
        out_shape=sds((16, D), BF16),
        in_specs=[VM] * 7,
        out_specs=VM,
        name="pack_vectors",
    )(b_out, gain_one, shift_one, b_down, gain_two, shift_two, b_up)


CHUNK = 208


def unpack_kernel(
    got, pos_ref, wq_ref, wo_ref, bo_ref, g1_ref, s1_ref, wu_ref, bu_ref, wd_ref, bd_ref, g2_ref, s2_ref
):
    for block in range(16):
        for r in range(4):
            dev = block * 4 + r
            at = slice(r * 128, (r + 1) * 128)
            wu_ref[0, at, block * 128 : (block + 1) * 128] = got[dev, 0:128, :].astype(F32)
            down = slice((block // 4) * D + r * 128, (block // 4) * D + (r + 1) * 128)
            lane = slice((block % 4) * 128, (block % 4 + 1) * 128)
            wd_ref[0, down, lane] = got[dev, CHUNK : CHUNK + 128, :].astype(F32)

    def piece(half, row):
        dev, off = row // 80, row % 80
        base = half * CHUNK + 128 + off
        return got[dev, base : base + 16, :].astype(F32)

    for c in range(4):
        lane = slice(c * 128, (c + 1) * 128)
        for i in range(32):
            at = slice(i * 16, (i + 1) * 16)
            row = c * D + i * 16
            wq_ref[0, at, c * 128 : (c + 1) * 128] = piece(0, row)
            wq_ref[0, at, D + c * 128 : D + (c + 1) * 128] = piece(0, 2048 + row)
            wq_ref[0, at, 2 * D + c * 128 : 2 * D + (c + 1) * 128] = piece(1, row)
            wo_ref[0, at, lane] = piece(1, 2048 + row)
        for i in range(8):
            for half in range(2):
                at = slice(half * 128 + i * 16, half * 128 + (i + 1) * 16)
                pos_ref[0, at, lane] = piece(half, 4096 + c * 128 + i * 16)
        small = piece(0, 4608 + c * 16)
        for ref, row in (
            (bo_ref, 0),
            (g1_ref, 1),
            (s1_ref, 2),
            (bd_ref, 8),
            (g2_ref, 9),
            (s2_ref, 10),
        ):
            ref[:, lane] = small[row : row + 1]
        for j in range(4):
            bu_ref[:, j * D + c * 128 : j * D + (c + 1) * 128] = small[11 + j : 12 + j]


def unpack(got):
    return pl.pallas_call(
        unpack_kernel,
        out_shape=[
            sds((1, WIN, D), F32),
            sds((1, D, 3 * D), F32),
            sds((1, D, D), F32),
            sds((1, D), F32),
            sds((1, D), F32),
            sds((1, D), F32),
            sds((1, D, FF), F32),
            sds((1, FF), F32),
            sds((1, FF, D), F32),
            sds((1, D), F32),
            sds((1, D), F32),
            sds((1, D), F32),
        ],
        in_specs=[VM],
        out_specs=[VM] * 12,
        compiler_params=PARAMS,
        name="unpack_gradients",
    )(got)


def swap(value):
    return lax.ppermute(value, "section", [(0, 1), (1, 0)])


def scatter_sum(value, rows):
    parts = lax.all_to_all(value.reshape(64, rows, 128), "dp", 0, 0, tiled=True)
    return jnp.sum(parts.astype(F32), 0).astype(BF16)


def shards(
    tokens,
    lengths,
    out_cotangent,
    pos_table,
    w_qkv,
    w_out,
    b_out,
    norm1_gain,
    norm1_bias,
    w_up,
    b_up,
    w_down,
    b_down,
    norm2_gain,
    norm2_bias,
):
    section = lax.axis_index("section")
    sec = section.astype(jnp.int32).reshape(1)
    vec = pack_vectors(b_out, norm1_gain, norm1_bias, b_down, norm2_gain, norm2_bias, b_up)
    mine = (pos_table, w_qkv, w_out, w_up, w_down, vec)
    other = tuple(swap(entry) for entry in mine)
    first = attn_forward(0, sec, lengths, tokens, mine, other)
    kept_0 = list(first) + list(ffn_forward(0, sec, lengths, first[3], mine, other))
    stream = kept_0[8]
    first = attn_forward(1, sec, lengths, stream, mine, other)
    kept_1 = list(first) + list(ffn_forward(1, sec, lengths, first[3], mine, other))
    output = kept_1[8]
    scattered = []
    arriving = out_cotangent
    for layer, kept, source in ((1, kept_1, stream), (0, kept_0, tokens)):
        after, ffn_keep, ffn_send, small = ffn_back(
            layer, sec, lengths, arriving, mine, other, kept
        )
        ffn_got = swap(ffn_send)
        arriving, att_keep, att_send = attn_back(
            layer, sec, after, source, mine, other, kept, small
        )
        att_got = swap(att_send)
        ffn_part = scatter_sum(ffn_keep + ffn_got, 128)
        att_part = scatter_sum(att_keep + att_got, 80)
        scattered.append(jnp.concatenate([ffn_part, att_part], 0))
    last, early = scattered
    is_first = section == 0
    own = jnp.where(is_first, early, last)
    partner = swap(jnp.where(is_first, last, early))
    chunk = jnp.concatenate(
        [jnp.where(is_first, own, partner), jnp.where(is_first, partner, own)], 0
    )
    gathered = lax.all_gather(chunk, "dp", axis=0, tiled=False)
    return (output[None], arriving[None]) + tuple(unpack(gathered))


def solution(mesh):
    placed = (
        P(None, "dp", None, None),
        P(None, "dp"),
        P(None, "dp", None, None),
        P("section", None, None),
        P("section", None, None),
        P("section", None, None),
        P("section", None),
        P("section", None),
        P("section", None),
        P("section", None, None),
        P("section", None),
        P("section", None, None),
        P("section", None),
        P("section", None),
        P("section", None),
    )
    return jax.shard_map(
        shards,
        mesh=mesh,
        in_specs=placed,
        out_specs=(
            P("section", "dp", None, None),
            P("section", "dp", None, None),
            P("section", None, None),
            P("section", None, None),
            P("section", None, None),
            P("section", None),
            P("section", None),
            P("section", None),
            P("section", None, None),
            P("section", None),
            P("section", None, None),
            P("section", None),
            P("section", None),
            P("section", None),
        ),
        check_vma=False,
    )
```

```python
import jax
import jax.numpy as jnp
from jax import lax
from jax.experimental import pallas as pl
from jax.experimental.pallas import tpu as pltpu
from jax.sharding import Mesh, PartitionSpec as P

HEADS = 8
D = 512
FF = 2048
WIN = 256
ROWS = 512
F32 = jnp.float32
BF16 = jnp.bfloat16
VMEM_LIMIT = 24 * 1024 * 1024

ANY = pl.BlockSpec(memory_space=pltpu.HBM)
VM = pl.BlockSpec(memory_space=pltpu.VMEM)
SM = pl.BlockSpec(memory_space=pltpu.SMEM)
PARAMS = pltpu.CompilerParams(vmem_limit_bytes=VMEM_LIMIT)
SLIGHT = pl.CostEstimate(flops=1000, bytes_accessed=1000, transcendentals=0)
HEAVY = pl.CostEstimate(flops=35_000_000_000, bytes_accessed=1000, transcendentals=0)
WIDE = pltpu.CompilerParams(vmem_limit_bytes=40 * 1024 * 1024)
FFN_PART = 128
ATT_PART = 80
CHUNK = FFN_PART + ATT_PART
WAY = ((16, 4, 1), (1, 16, 4))


def nn(a, b):
    return lax.dot_general(a, b, (((1,), (0,)), ((), ())), preferred_element_type=F32)


def nt(a, b):
    return lax.dot_general(a, b, (((1,), (1,)), ((), ())), preferred_element_type=F32)


def tn(a, b):
    return lax.dot_general(a, b, (((0,), (0,)), ((), ())), preferred_element_type=F32)


def start_pick(near, mine, other, dst, sem):
    @pl.when(near)
    def _():
        pltpu.make_async_copy(mine, dst, sem).start()

    @pl.when(jnp.logical_not(near))
    def _():
        pltpu.make_async_copy(other, dst, sem).start()


def wait_for(src, dst, sem):
    pltpu.make_async_copy(src, dst, sem).wait()


def normalize(v):
    center = v - jnp.mean(v, -1, keepdims=True)
    inverse = lax.rsqrt(jnp.mean(center * center, -1, keepdims=True) + 1e-05)
    return center * inverse, inverse


def norm_backward(e, normed, inverse, gain):
    scaled = e * gain
    return inverse * (
        scaled
        - jnp.mean(scaled, -1, keepdims=True)
        - normed * jnp.mean(scaled * normed, -1, keepdims=True)
    )


def gelu_pair(v):
    c = 0.7978845608028654
    sq = v * v
    t = jnp.tanh(v * (c + (c * 0.044715) * sq))
    half = 0.5 + 0.5 * t
    slope = half + (0.5 * v) * (1.0 - t * t) * (c + (3.0 * c * 0.044715) * sq)
    return v * half, slope


def attn_fwd_kernel(
    layer,
    sec_ref,
    stream_in,
    pos_m,
    pos_o,
    wq_m,
    wq_o,
    wo_m,
    wo_o,
    project_ref,
    probs_ref,
    mixed_ref,
    sum_one_ref,
    stream,
    pos,
    wq,
    wo,
    hidden,
    mask,
    sems,
):
    sec = sec_ref[0]
    near = sec == layer
    src = stream_in.at[sec] if layer == 0 else stream_in
    first = pltpu.make_async_copy(src, stream, sems.at[0])
    first.start()
    start_pick(near, pos_m.at[0], pos_o.at[0], pos, sems.at[1])
    start_pick(near, wq_m.at[0], wq_o.at[0], wq, sems.at[2])
    start_pick(near, wo_m.at[0], wo_o.at[0], wo, sems.at[3])
    rows = lax.broadcasted_iota(jnp.int32, (WIN, WIN), 0)
    cols = lax.broadcasted_iota(jnp.int32, (WIN, WIN), 1)
    for w in range(2):
        inside = (cols <= rows) & (cols < sec_ref[2 + 2 * sec + w])
        mask[w] = jnp.where(inside, 0.0, -1e30)
    first.wait()
    wait_for(pos_m.at[0], pos, sems.at[1])
    place = pos[...].astype(F32)
    for w in range(2):
        hidden[w * WIN : (w + 1) * WIN, :] = stream[w].astype(F32) + place
    hidden_low = hidden[...].astype(BF16)
    wait_for(wq_m.at[0], wq, sems.at[2])
    for c in range(3):
        project_ref[:, c * D : (c + 1) * D] = nn(hidden_low, wq[:, c * D : (c + 1) * D]).astype(
            BF16
        )
    lanes = lax.broadcasted_iota(jnp.int32, (WIN, 128), 1)

    def attend(step, carry):
        w = step // 4
        p = step % 4
        at_row = pl.ds(pl.multiple_of(w * WIN, WIN), WIN)
        at = pl.multiple_of(p * 128, 128)
        q2 = project_ref[at_row, pl.ds(at, 128)] * jnp.asarray(0.125, BF16)
        k2 = project_ref[at_row, pl.ds(pl.multiple_of(D + p * 128, 128), 128)]
        v2 = project_ref[at_row, pl.ds(pl.multiple_of(2 * D + p * 128, 128), 128)]
        blocked = mask[w]
        parts = []
        for h in range(2):
            own = (lanes >= 64) if h else (lanes < 64)
            qm = jnp.where(own, q2, jnp.zeros_like(q2))
            scores = nt(qm, k2) + blocked
            raised = jnp.exp(scores - jnp.max(scores, -1, keepdims=True))
            soft = (raised * (1.0 / jnp.sum(raised, -1, keepdims=True))).astype(BF16)
            probs_ref[step * 2 + h] = soft
            parts.append(nn(soft, v2))
        mixed_ref[at_row, pl.ds(at, 128)] = jnp.where(lanes < 64, parts[0], parts[1]).astype(BF16)
        return carry

    lax.fori_loop(0, 8, attend, 0)
    wait_for(wo_m.at[0], wo, sems.at[3])
    sum_one_ref[...] = hidden[...] + nn(mixed_ref[...], wo[...])


def ffn_fwd_kernel(
    layer,
    sec_ref,
    wu_m,
    wu_o,
    wd_m,
    wd_o,
    vec_m,
    vec_o,
    sum_one_ref,
    low_ref,
    active_ref,
    slope_ref,
    sum_two_ref,
    out_ref,
    wu,
    wd,
    vec,
    acc,
    sems,
):
    sec = sec_ref[0]
    near = sec == layer
    start_pick(near, vec_m, vec_o, vec, sems.at[2])
    start_pick(near, wu_m.at[0], wu_o.at[0], wu, sems.at[0])
    start_pick(near, wd_m.at[0], wd_o.at[0], wd, sems.at[1])
    wait_for(vec_m, vec, sems.at[2])
    small = vec[...].astype(F32)
    normed, _ = normalize(sum_one_ref[...] + small[0:1])
    after = normed * small[1:2] + small[2:3]
    acc[...] = after
    low = after.astype(BF16)
    low_ref[...] = low
    wait_for(wu_m.at[0], wu, sems.at[0])
    wait_for(wd_m.at[0], wd, sems.at[1])
    for c in range(4):
        block = slice(c * D, (c + 1) * D)
        value = nn(low, wu[:, block]) + small[6 + c : 7 + c]
        active, slope = gelu_pair(value)
        active = active.astype(BF16)
        active_ref[:, block] = active
        slope_ref[:, block] = slope.astype(BF16)
        acc[...] += nn(active, wd[block, :])
    sum_two = acc[...] + small[3:4]
    sum_two_ref[...] = sum_two
    normed, _ = normalize(sum_two)
    result = normed * small[4:5] + small[5:6]
    for w in range(2):
        part = result[w * WIN : (w + 1) * WIN]
        if layer == 1:
            at_row = lax.broadcasted_iota(jnp.int32, (WIN, D), 0)
            part = jnp.where(at_row < sec_ref[2 + 2 * sec + w], part, 0.0)
        out_ref[w] = part.astype(BF16)


def sds(shape, dtype):
    return jax.ShapeDtypeStruct(shape, dtype)


def attn_forward(layer, sec, stream, mine, other):
    args = [sec, stream]
    for i in (0, 1, 2):
        args += [mine[i], other[i]]

    def body(*refs):
        attn_fwd_kernel(layer, *refs)

    return pl.pallas_call(
        body,
        out_shape=[
            sds((ROWS, 3 * D), BF16),
            sds((16, WIN, WIN), BF16),
            sds((ROWS, D), BF16),
            sds((ROWS, D), F32),
        ],
        in_specs=[SM] + [ANY] * (len(args) - 1),
        out_specs=[VM] * 4,
        scratch_shapes=[
            pltpu.VMEM((2, WIN, D), BF16),
            pltpu.VMEM((WIN, D), BF16),
            pltpu.VMEM((D, 3 * D), BF16),
            pltpu.VMEM((D, D), BF16),
            pltpu.VMEM((ROWS, D), F32),
            pltpu.VMEM((2, WIN, WIN), F32),
            pltpu.SemaphoreType.DMA((4,)),
        ],
        compiler_params=PARAMS,
        cost_estimate=HEAVY,
        name=f"attention_forward_{layer}",
    )(*args)


def ffn_forward(layer, sec, sum_one, mine, other):
    args = [sec]
    for i in (3, 4, 5):
        args += [mine[i], other[i]]
    args += [sum_one]

    def body(*refs):
        ffn_fwd_kernel(layer, *refs)

    return pl.pallas_call(
        body,
        out_shape=[
            sds((ROWS, D), BF16),
            sds((ROWS, FF), BF16),
            sds((ROWS, FF), BF16),
            sds((ROWS, D), F32),
            sds((2, WIN, D), BF16),
        ],
        in_specs=[SM] + [ANY] * 6 + [VM],
        out_specs=[VM] * 5,
        scratch_shapes=[
            pltpu.VMEM((D, FF), BF16),
            pltpu.VMEM((FF, D), BF16),
            pltpu.VMEM((16, D), BF16),
            pltpu.VMEM((ROWS, D), F32),
            pltpu.SemaphoreType.DMA((3,)),
        ],
        compiler_params=PARAMS,
        cost_estimate=HEAVY,
        name=f"ffn_forward_{layer}",
    )(*args)


def ffn_kernel(
    layer,
    sec_ref,
    up_in,
    wu_m,
    wu_o,
    wd_m,
    wd_o,
    vec_m,
    vec_o,
    low_ref,
    active_ref,
    slope_ref,
    sum_two_ref,
    grad_after_ref,
    small_ref,
    grads,
    send_ref,
    arriving,
    wu,
    wd,
    vec,
    acc,
    sems,
):
    sec = sec_ref[0]
    near = sec == layer
    src = up_in.at[sec] if layer == 1 else up_in
    first = pltpu.make_async_copy(src, arriving, sems.at[0])
    first.start()
    start_pick(near, vec_m, vec_o, vec, sems.at[1])
    start_pick(near, wd_m.at[0], wd_o.at[0], wd, sems.at[2])
    start_pick(near, wu_m.at[0], wu_o.at[0], wu, sems.at[3])
    normed, inverse = normalize(sum_two_ref[...])
    first.wait()
    parts = []
    for w in range(2):
        part = arriving[w].astype(F32)
        if layer == 1:
            at_row = lax.broadcasted_iota(jnp.int32, (WIN, D), 0)
            part = jnp.where(at_row < sec_ref[2 + 2 * sec + w], part, 0.0)
        parts.append(part)
    e = jnp.concatenate(parts, 0)
    wait_for(vec_m, vec, sems.at[1])
    gain = vec[4:5, :].astype(F32)
    small_ref[...] = jnp.zeros_like(small_ref)
    small_ref[1:2, :] = jnp.sum(e * normed, 0, keepdims=True)
    small_ref[2:3, :] = jnp.sum(e, 0, keepdims=True)
    grad_sum = norm_backward(e, normed, inverse, gain)
    acc[...] = grad_sum
    grad_low = grad_sum.astype(BF16)
    small_ref[0:1, :] = jnp.sum(grad_low.astype(F32), 0, keepdims=True)
    wait_for(wd_m.at[0], wd, sems.at[2])
    wait_for(wu_m.at[0], wu, sems.at[3])
    for c in range(4):
        block = slice(c * D, (c + 1) * D)
        grad_up = nt(grad_low, wd[block, :]) * slope_ref[:, block].astype(F32)
        grad_up = grad_up.astype(BF16)
        small_ref[3 + c : 4 + c, :] = jnp.sum(grad_up.astype(F32), 0, keepdims=True)
        acc[...] += nt(grad_up, wu[:, block])
        grad_wu = tn(low_ref[...], grad_up).astype(BF16)
        grad_wd = tn(active_ref[:, block], grad_low).astype(BF16)
        for k in range(4):
            at = slice((c * 4 + k) * D, (c * 4 + k + 1) * D)
            grads[0, at, :] = grad_wu[:, k * 128 : (k + 1) * 128]
            grads[1, at, :] = grad_wd[:, k * 128 : (k + 1) * 128]
        at = slice(c * 2048, (c + 1) * 2048)
        send_ref[at, :] = grads[1 - sec, at, :]
    grad_after_ref[...] = acc[...]


def ffn_back(layer, sec, arriving, mine, other, kept):
    args = [sec, arriving]
    for i in (3, 4, 5):
        args += [mine[i], other[i]]
    args += list(kept[4:8])

    def body(*refs):
        ffn_kernel(layer, *refs)

    return pl.pallas_call(
        body,
        out_shape=[
            sds((ROWS, D), F32),
            sds((8, D), F32),
            sds((2, 8192, 128), BF16),
            sds((8192, 128), BF16),
        ],
        in_specs=[SM] + [ANY] * 7 + [VM] * 4,
        out_specs=[VM] * 4,
        scratch_shapes=[
            pltpu.VMEM((2, WIN, D), BF16),
            pltpu.VMEM((D, FF), BF16),
            pltpu.VMEM((FF, D), BF16),
            pltpu.VMEM((16, D), BF16),
            pltpu.VMEM((ROWS, D), F32),
            pltpu.SemaphoreType.DMA((4,)),
        ],
        compiler_params=PARAMS,
        cost_estimate=HEAVY,
        name=f"ffn_backward_{layer}",
    )(*args)


def out_kernel(
    layer,
    sec_ref,
    wo_m,
    wo_o,
    vec_m,
    vec_o,
    grad_after_ref,
    sum_one_ref,
    mixed_ref,
    small_in,
    grad_sum_ref,
    grad_mixed_ref,
    grad_out_ref,
    rows_ref,
    wo,
    vec,
    sems,
):
    near = sec_ref[0] == layer
    start_pick(near, vec_m, vec_o, vec, sems.at[1])
    start_pick(near, wo_m.at[0], wo_o.at[0], wo, sems.at[0])
    wait_for(vec_m, vec, sems.at[1])
    small = vec[...].astype(F32)
    normed, inverse = normalize(sum_one_ref[...] + small[0:1])
    e = grad_after_ref[...]
    row_norm = jnp.sum(e * normed, 0, keepdims=True)
    row_shift = jnp.sum(e, 0, keepdims=True)
    grad_sum = norm_backward(e, normed, inverse, small[1:2])
    grad_sum_ref[...] = grad_sum
    branch = grad_sum.astype(BF16)
    row_out = jnp.sum(branch.astype(F32), 0, keepdims=True)
    rows = jnp.concatenate([row_out, row_norm, row_shift, jnp.zeros((5, D), F32)], 0)
    rows_ref[...] = jnp.concatenate([rows, small_in[...]], 0).astype(BF16)
    wait_for(wo_m.at[0], wo, sems.at[0])
    grad_mixed_ref[...] = nt(branch, wo[...]).astype(BF16)
    grad_out_ref[...] = tn(mixed_ref[...], branch).astype(BF16)


def out_back(layer, sec, grad_after, mine, other, kept, small):
    args = [sec]
    for i in (2, 5):
        args += [mine[i], other[i]]
    args += [grad_after, kept[3], kept[2], small]

    def body(*refs):
        out_kernel(layer, *refs)

    return pl.pallas_call(
        body,
        out_shape=[
            sds((ROWS, D), F32),
            sds((ROWS, D), BF16),
            sds((D, D), BF16),
            sds((16, D), BF16),
        ],
        in_specs=[SM] + [ANY] * 4 + [VM] * 4,
        out_specs=[VM] * 4,
        scratch_shapes=[
            pltpu.VMEM((D, D), BF16),
            pltpu.VMEM((16, D), BF16),
            pltpu.SemaphoreType.DMA((2,)),
        ],
        compiler_params=PARAMS,
        cost_estimate=HEAVY,
        name=f"projection_backward_{layer}",
    )(*args)


def attn_kernel(
    layer,
    sec_ref,
    stream_in,
    pos_m,
    pos_o,
    wq_m,
    wq_o,
    project_ref,
    probs_ref,
    grad_sum_ref,
    grad_mixed_ref,
    grad_out_ref,
    rows_ref,
    grad_low_ref,
    grads,
    send_ref,
    stream,
    pos,
    wq,
    total,
    grad_project,
    sems,
):
    sec = sec_ref[0]
    near = sec == layer
    start_pick(near, wq_m.at[0], wq_o.at[0], wq, sems.at[0])
    start_pick(near, pos_m.at[0], pos_o.at[0], pos, sems.at[1])
    src = stream_in.at[sec] if layer == 0 else stream_in
    last = pltpu.make_async_copy(src, stream, sems.at[2])
    last.start()
    for c in range(4):
        lanes_at = slice(c * 128, (c + 1) * 128)
        grads[1, 2048 + c * D : 2048 + (c + 1) * D, :] = grad_out_ref[:, lanes_at]
        for half in range(2):
            grads[half, 4608 + c * 16 : 4608 + (c + 1) * 16, :] = rows_ref[:, lanes_at]
    for half in range(2):
        grads[half, 4672:5120, :] = jnp.zeros((448, 128), BF16)
    lanes = lax.broadcasted_iota(jnp.int32, (WIN, 128), 1)

    def attend(step, carry):
        w = step // 4
        p = step % 4
        at_row = pl.ds(pl.multiple_of(w * WIN, WIN), WIN)
        at = pl.ds(pl.multiple_of(p * 128, 128), 128)
        at_k = pl.ds(pl.multiple_of(D + p * 128, 128), 128)
        at_v = pl.ds(pl.multiple_of(2 * D + p * 128, 128), 128)
        q2 = project_ref[at_row, at] * jnp.asarray(0.125, BF16)
        k2 = project_ref[at_row, at_k]
        v2 = project_ref[at_row, at_v]
        g2 = grad_mixed_ref[at_row, at]
        grad_q = []
        grad_k = []
        grad_v = []
        for h in range(2):
            own = (lanes >= 64) if h else (lanes < 64)
            none = jnp.zeros_like(q2)
            gm = jnp.where(own, g2, none)
            qm = jnp.where(own, q2, none)
            soft_low = probs_ref[step * 2 + h]
            soft = soft_low.astype(F32)
            product = soft * nt(gm, v2)
            grad_scores = (product - soft * jnp.sum(product, -1, keepdims=True)).astype(BF16)
            grad_q.append(nn(grad_scores, k2))
            grad_k.append(tn(grad_scores, qm))
            grad_v.append(tn(soft_low, gm))
        first_half = lanes < 64
        grad_project[at_row, at] = (
            jnp.where(first_half, grad_q[0], grad_q[1]) * 0.125
        ).astype(BF16)
        grad_project[at_row, at_k] = (grad_k[0] + grad_k[1]).astype(BF16)
        grad_project[at_row, at_v] = (grad_v[0] + grad_v[1]).astype(BF16)
        return carry

    lax.fori_loop(0, 8, attend, 0)
    last.wait()
    wait_for(pos_m.at[0], pos, sems.at[1])
    place = pos[...].astype(F32)
    hidden_low = jnp.concatenate(
        [(stream[w].astype(F32) + place).astype(BF16) for w in range(2)], 0
    )
    wait_for(wq_m.at[0], wq, sems.at[0])
    total[...] = grad_sum_ref[...]
    for j in range(3):
        block = slice(j * D, (j + 1) * D)
        part = grad_project[:, block]
        total[...] += nt(part, wq[:, block])
        grad_w = tn(hidden_low, part).astype(BF16)
        half, base = ((0, 0), (0, 2048), (1, 0))[j]
        for c in range(4):
            grads[half, base + c * D : base + (c + 1) * D, :] = grad_w[:, c * 128 : (c + 1) * 128]
    for w in range(2):
        grad_low_ref[w] = total[w * WIN : (w + 1) * WIN, :].astype(BF16)
    grad_pos = (total[0:WIN, :] + total[WIN : 2 * WIN, :]).astype(BF16)
    for half in range(2):
        for c in range(4):
            grads[half, 4096 + c * 128 : 4096 + (c + 1) * 128, :] = grad_pos[
                half * 128 : (half + 1) * 128, c * 128 : (c + 1) * 128
            ]
    send_ref[...] = grads[1 - sec]


def attn_back(layer, sec, stream, mine, other, kept, before):
    args = [sec, stream]
    for i in (0, 1):
        args += [mine[i], other[i]]
    args += [kept[0], kept[1]] + list(before)

    def body(*refs):
        attn_kernel(layer, *refs)

    return pl.pallas_call(
        body,
        out_shape=[
            sds((2, WIN, D), BF16),
            sds((2, 5120, 128), BF16),
            sds((5120, 128), BF16),
        ],
        in_specs=[SM] + [ANY] * 5 + [VM] * 6,
        out_specs=[VM] * 3,
        scratch_shapes=[
            pltpu.VMEM((2, WIN, D), BF16),
            pltpu.VMEM((WIN, D), BF16),
            pltpu.VMEM((D, 3 * D), BF16),
            pltpu.VMEM((ROWS, D), F32),
            pltpu.VMEM((ROWS, 3 * D), BF16),
            pltpu.SemaphoreType.DMA((3,)),
        ],
        compiler_params=PARAMS,
        cost_estimate=HEAVY,
        name=f"attention_backward_{layer}",
    )(*args)


def pack_vectors(b_out, gain_one, shift_one, b_down, gain_two, shift_two, b_up):
    def body(*refs):
        out = refs[-1]
        rows = [ref[...].astype(F32) for ref in refs[:6]]
        wide = refs[6][...].astype(F32)
        rows += [wide[:, c * D : (c + 1) * D] for c in range(4)]
        rows += [jnp.zeros((6, D), F32)]
        out[...] = jnp.concatenate(rows, 0).astype(BF16)

    return pl.pallas_call(
        body,
        out_shape=sds((16, D), BF16),
        in_specs=[VM] * 7,
        out_specs=VM,
        name="pack_vectors",
    )(b_out, gain_one, shift_one, b_down, gain_two, shift_two, b_up)


def plain(body, shapes, args, name, specs=None):
    return pl.pallas_call(
        body,
        out_shape=[sds(shape, BF16) for shape in shapes],
        in_specs=specs or [VM] * len(args),
        out_specs=[VM] * len(shapes),
        compiler_params=PARAMS,
        cost_estimate=SLIGHT,
        name=name,
    )(*args)


def stage_order(place_ref):
    first = place_ref[0] == 0
    strides = [jnp.where(first, a, b) for a, b in zip(*WAY)]
    coords = [lax.rem(lax.div(place_ref[1], stride), 4) for stride in strides]

    def owner(*distances):
        return sum(
            lax.rem(coord + r, 4) * stride
            for coord, r, stride in zip(coords, distances, strides)
        )

    return owner


def pair_sum(place, grads, got):
    rows = got.shape[0] // 64

    def body(place_ref, both, two, *outs):
        owner = stage_order(place_ref)
        sec = place_ref[0]
        for third in range(4):
            for second in range(4):
                for first in range(4):
                    dev = owner(first, second, third)
                    src = pl.ds(pl.multiple_of(dev * rows, 16), rows)
                    at = (second * 4 + first) * rows
                    total = both[sec, src, :].astype(F32) + two[src, :].astype(F32)
                    outs[third][at : at + rows, :] = total.astype(BF16)

    return plain(
        body,
        [(16 * rows, 128)] * 4,
        (place, grads, got),
        "sum_of_two_cores",
        [SM, VM, VM],
    )


def add_four(refs, at):
    return sum(ref[at].astype(F32) for ref in refs)


def line_sum(early_ffn, early_att, late_ffn, late_att):
    def body(*refs):
        outs = refs[16:]
        for r in range(4):
            for first in range(4):
                for i in range(4):
                    rows = (FFN_PART, ATT_PART)[i % 2]
                    low = (0, FFN_PART)[i % 2]
                    at = (r * 4 + first) * rows
                    total = add_four(refs[4 * i : 4 * i + 4], (slice(at, at + rows), slice(None)))
                    outs[r][first, i // 2, low : low + rows, :] = total.astype(BF16)

    args = early_ffn + early_att + late_ffn + late_att
    return plain(body, [(4, 2, CHUNK, 128)] * 4, args, "sum_over_line")


def plane_sum(pieces):
    def body(*refs):
        for first in range(4):
            refs[4 + first][...] = add_four(refs[:4], first).astype(BF16)

    return plain(body, [pieces[0].shape[1:]] * 4, pieces, "sum_over_plane")


def cube_sum(place, pieces):
    def body(place_ref, *refs):
        sec = place_ref[0]
        refs[4][...] = add_four(refs[:4], sec).astype(BF16)
        refs[5][...] = add_four(refs[:4], 1 - sec).astype(BF16)

    specs = [SM] + [VM] * 4
    return plain(body, [(CHUNK, 128)] * 2, [place] + pieces, "sum_over_cube", specs)


def unpack_kernel(place_ref, *refs):
    sources, refs = refs[:8], refs[8:]
    pos_ref, wq_ref, wo_ref, bo_ref, g1_ref, s1_ref, wu_ref, bu_ref = refs[:8]
    wd_ref, bd_ref, g2_ref, s2_ref, parts, att, wu, wd, wq, wo, isems, osems = refs[8:]
    sec = place_ref[0]
    loads = []
    for i, ref in enumerate(sources):
        loads.append(pltpu.make_async_copy(ref, parts.at[i], isems.at[i]))
        loads[i].start()
    owner = stage_order(place_ref)
    for i in range(8):
        loads[i].wait()

        def place(step, carry, i=i):
            dev = owner(lax.rem(step, 4), (i % 2) * 2 + lax.div(step, 4), i // 2)
            block = lax.div(dev, 4)
            r = lax.rem(dev, 4)
            lane = pl.ds(pl.multiple_of(block * 128, 128), 128)
            at = pl.ds(pl.multiple_of(r * 128, 128), 128)
            wu[at, lane] = parts[i, step, sec, 0:FFN_PART, :].astype(F32)
            at = pl.ds(pl.multiple_of(lax.div(block, 4) * D + r * 128, 128), 128)
            lane = pl.ds(pl.multiple_of(lax.rem(block, 4) * 128, 128), 128)
            wd[at, lane] = parts[i, step, 1 - sec, 0:FFN_PART, :].astype(F32)
            at = pl.ds(pl.multiple_of(dev * ATT_PART, 16), ATT_PART)
            att[0, at, :] = parts[i, step, sec, FFN_PART:CHUNK, :]
            att[1, at, :] = parts[i, step, 1 - sec, FFN_PART:CHUNK, :]
            return carry

        lax.fori_loop(0, 8, place, 0)
    stores = [
        pltpu.make_async_copy(wu, wu_ref.at[0], osems.at[0]),
        pltpu.make_async_copy(wd, wd_ref.at[0], osems.at[1]),
        pltpu.make_async_copy(wq, wq_ref.at[0], osems.at[2]),
        pltpu.make_async_copy(wo, wo_ref.at[0], osems.at[3]),
    ]
    stores[0].start()
    stores[1].start()
    for c in range(4):
        at = slice(c * D, (c + 1) * D)
        later = slice(2048 + c * D, 2048 + (c + 1) * D)
        wq[:, c * 128 : (c + 1) * 128] = att[0, at, :].astype(F32)
        wq[:, D + c * 128 : D + (c + 1) * 128] = att[0, later, :].astype(F32)
        wq[:, 2 * D + c * 128 : 2 * D + (c + 1) * 128] = att[1, at, :].astype(F32)
    stores[2].start()
    for c in range(4):
        lane = slice(c * 128, (c + 1) * 128)
        wo[:, lane] = att[1, 2048 + c * D : 2048 + (c + 1) * D, :].astype(F32)
        for half in range(2):
            pos_ref[0, half * 128 : (half + 1) * 128, lane] = att[
                half, 4096 + c * 128 : 4096 + (c + 1) * 128, :
            ].astype(F32)
        small = att[0, 4608 + c * 16 : 4608 + (c + 1) * 16, :].astype(F32)
        for ref, row in (
            (bo_ref, 0),
            (g1_ref, 1),
            (s1_ref, 2),
            (bd_ref, 8),
            (g2_ref, 9),
            (s2_ref, 10),
        ):
            ref[:, lane] = small[row : row + 1]
        for j in range(4):
            bu_ref[:, j * D + c * 128 : j * D + (c + 1) * 128] = small[11 + j : 12 + j]
    stores[3].start()
    for store in stores:
        store.wait()


def unpack(place, pieces):
    small = [sds((1, D), F32)] * 3
    return pl.pallas_call(
        unpack_kernel,
        out_shape=[sds((1, WIN, D), F32), sds((1, D, 3 * D), F32), sds((1, D, D), F32)]
        + small
        + [sds((1, D, FF), F32), sds((1, FF), F32), sds((1, FF, D), F32)]
        + small,
        in_specs=[SM] + [VM] * 8,
        out_specs=[VM, ANY, ANY, VM, VM, VM, ANY, VM, ANY, VM, VM, VM],
        scratch_shapes=[
            pltpu.VMEM((8, 8, 2, CHUNK, 128), BF16),
            pltpu.VMEM((2, 64 * ATT_PART, 128), BF16),
            pltpu.VMEM((D, FF), F32),
            pltpu.VMEM((FF, D), F32),
            pltpu.VMEM((D, 3 * D), F32),
            pltpu.VMEM((D, D), F32),
            pltpu.SemaphoreType.DMA((8,)),
            pltpu.SemaphoreType.DMA((4,)),
        ],
        compiler_params=WIDE,
        cost_estimate=SLIGHT,
        name="unpack_gradients",
    )(place, *pieces)


def swap(value):
    return lax.ppermute(value, "section", [(0, 1), (1, 0)])


def from_ahead(value, stage, distance):
    pairs = []
    for section in range(2):
        stride = WAY[section][stage]
        for dst in range(64):
            at = dst // stride % 4
            src = dst + ((at + distance) % 4 - at) * stride
            pairs.append((section * 64 + src, section * 64 + dst))
    return lax.ppermute(value, ("section", "dp"), pairs)


def send_ahead(pieces, stage):
    return [pieces[0]] + [from_ahead(pieces[r], stage, 4 - r) for r in (1, 3, 2)]


def gather(chunk):
    line = jnp.stack([chunk] + [from_ahead(chunk, 0, r) for r in (1, 2, 3)])
    ahead = [from_ahead(line, 1, r) for r in (1, 2, 3)]
    own_a = jnp.concatenate([line, ahead[0]], 0)
    own_b = jnp.concatenate([ahead[1], ahead[2]], 0)
    next_a = from_ahead(own_a, 2, 1)
    prev_b = from_ahead(own_b, 2, 3)
    next_b = from_ahead(own_b, 2, 1)
    prev_a = from_ahead(own_a, 2, 3)
    far_a = from_ahead(next_a, 2, 1)
    far_b = from_ahead(prev_b, 2, 3)
    return own_a, own_b, next_a, next_b, far_a, far_b, prev_a, prev_b


def hold(*values):
    return tuple(pltpu.with_memory_space_constraint(value, pltpu.HBM) for value in values)


def shards(
    tokens,
    lengths,
    out_cotangent,
    pos_table,
    w_qkv,
    w_out,
    b_out,
    norm1_gain,
    norm1_bias,
    w_up,
    b_up,
    w_down,
    b_down,
    norm2_gain,
    norm2_bias,
):
    section = lax.axis_index("section")
    place = jnp.stack([section, lax.axis_index("dp")]).astype(jnp.int32)
    place = jnp.concatenate([place, lengths.reshape(4)])
    vec = pack_vectors(b_out, norm1_gain, norm1_bias, b_down, norm2_gain, norm2_bias, b_up)
    got_qkv = swap(w_qkv)
    got_pos = swap(pos_table)
    got_out = swap(w_out)
    late_up, late_down, got_qkv = lax.optimization_barrier((w_up, w_down, got_qkv))
    mine = hold(pos_table, w_qkv, w_out, w_up, w_down, vec)
    other = hold(got_pos, got_qkv, got_out, swap(late_up), swap(late_down), swap(vec))
    tokens, out_cotangent = hold(tokens, out_cotangent)
    first = attn_forward(0, place, tokens, mine, other)
    kept_0 = list(first) + list(ffn_forward(0, place, first[3], mine, other))
    stream = kept_0[8]
    first = attn_forward(1, place, stream, mine, other)
    kept_1 = list(first) + list(ffn_forward(1, place, first[3], mine, other))
    output = kept_1[8]

    def tie(*values):
        return lax.optimization_barrier(values)

    after, small, ffn_both, ffn_send = ffn_back(
        1, place, out_cotangent, mine, other, kept_1
    )
    ffn_got = swap(ffn_send)
    before = out_back(1, place, after, mine, other, kept_1, small)
    pieces = pair_sum(place, ffn_both, ffn_got)
    before, pieces = tie(before, pieces)
    late_ffn = send_ahead(pieces, 2)
    arriving, att_both, att_send = attn_back(1, place, stream, mine, other, kept_1, before)
    att_got = swap(att_send)
    arriving, late_ffn = tie(arriving, late_ffn)
    after, small, ffn_both, ffn_send = ffn_back(0, place, arriving, mine, other, kept_0)
    pieces = pair_sum(place, att_both, att_got)
    after, pieces = tie(after, pieces)
    late_att = send_ahead(pieces, 2)
    ffn_got = swap(ffn_send)
    before = out_back(0, place, after, mine, other, kept_0, small)
    pieces = pair_sum(place, ffn_both, ffn_got)
    before, pieces = tie(before, pieces)
    early_ffn = send_ahead(pieces, 2)
    arriving, att_both, att_send = attn_back(0, place, tokens, mine, other, kept_0, before)
    att_send, late_att, early_ffn = tie(att_send, late_att, early_ffn)
    early_att = send_ahead(pair_sum(place, att_both, swap(att_send)), 2)
    pieces = line_sum(early_ffn, early_att, late_ffn, late_att)
    pieces = plane_sum(send_ahead(pieces, 1))
    own, others = cube_sum(place, send_ahead(pieces, 0))
    chunk = jnp.stack([own, swap(others)])
    return (output[None], arriving[None]) + tuple(unpack(place, gather(chunk)))


def solution(mesh):
    placed = (
        P(None, "dp", None, None),
        P(None, "dp"),
        P(None, "dp", None, None),
        P("section", None, None),
        P("section", None, None),
        P("section", None, None),
        P("section", None),
        P("section", None),
        P("section", None),
        P("section", None, None),
        P("section", None),
        P("section", None, None),
        P("section", None),
        P("section", None),
        P("section", None),
    )
    return jax.shard_map(
        shards,
        mesh=mesh,
        in_specs=placed,
        out_specs=(
            P("section", "dp", None, None),
            P("section", "dp", None, None),
            P("section", None, None),
            P("section", None, None),
            P("section", None, None),
            P("section", None),
            P("section", None),
            P("section", None),
            P("section", None, None),
            P("section", None),
            P("section", None, None),
            P("section", None),
            P("section", None),
            P("section", None),
        ),
        check_vma=False,
    )
```

```python
import jax
import jax.numpy as jnp
from jax import lax
from jax.experimental import pallas as pl
from jax.experimental.pallas import tpu as pltpu
from jax.sharding import PartitionSpec as P

D = 512
FF = 2048
WIN = 256
ROWS = 512
F32 = jnp.float32
BF16 = jnp.bfloat16

HBM = pl.BlockSpec(memory_space=pltpu.HBM)
VM = pl.BlockSpec(memory_space=pltpu.VMEM)
SM = pl.BlockSpec(memory_space=pltpu.SMEM)
DMA = pltpu.SemaphoreType.DMA
SLIGHT = pl.CostEstimate(flops=1000, bytes_accessed=1000, transcendentals=0)
HEAVY = pl.CostEstimate(flops=35_000_000_000, bytes_accessed=1000, transcendentals=0)
FFN_PART = 128
ATT_PART = 80
CHUNK = FFN_PART + ATT_PART
WAY = ((16, 4, 1), (1, 16, 4))


def limit(mebibytes):
    return pltpu.CompilerParams(vmem_limit_bytes=mebibytes * 1024 * 1024)


def sds(shape, dtype):
    return jax.ShapeDtypeStruct(shape, dtype)


def nn(a, b):
    return lax.dot_general(a, b, (((1,), (0,)), ((), ())), preferred_element_type=F32)


def nt(a, b):
    return lax.dot_general(a, b, (((1,), (1,)), ((), ())), preferred_element_type=F32)


def tn(a, b):
    return lax.dot_general(a, b, (((0,), (0,)), ((), ())), preferred_element_type=F32)


def fetch(near, mine, other, dst, sem):
    @pl.when(near)
    def _():
        pltpu.make_async_copy(mine.at[0], dst, sem).start()

    @pl.when(jnp.logical_not(near))
    def _():
        pltpu.make_async_copy(other.at[0], dst, sem).start()

    return pltpu.make_async_copy(mine.at[0], dst, sem).wait


def copy(src, dst, sem):
    load = pltpu.make_async_copy(src, dst, sem)
    load.start()
    return load.wait


def chosen(near, mine, other):
    return jnp.where(near, mine[...].astype(F32), other[...].astype(F32))


def normalize(v):
    center = v - jnp.mean(v, -1, keepdims=True)
    inverse = lax.rsqrt(jnp.mean(center * center, -1, keepdims=True) + 1e-05)
    return center * inverse, inverse


def norm_backward(e, normed, inverse, gain):
    scaled = e * gain
    return inverse * (
        scaled
        - jnp.mean(scaled, -1, keepdims=True)
        - normed * jnp.mean(scaled * normed, -1, keepdims=True)
    )


def gelu_pair(v):
    c = 0.7978845608028654
    sq = v * v
    t = jnp.tanh(v * (c + (c * 0.044715) * sq))
    half = 0.5 + 0.5 * t
    slope = half + (0.5 * v) * (1.0 - t * t) * (c + (3.0 * c * 0.044715) * sq)
    return v * half, slope


def used(place_ref, window):
    return place_ref[2 + 2 * place_ref[0] + window]


def write_mask(place_ref, mask):
    rows = lax.broadcasted_iota(jnp.int32, (WIN, WIN), 0)
    cols = lax.broadcasted_iota(jnp.int32, (WIN, WIN), 1)
    for w in range(2):
        inside = (cols <= rows) & (cols < used(place_ref, w))
        mask[w] = jnp.where(inside, 0.0, -1e30)


def window_rows(w):
    return slice(w * WIN, (w + 1) * WIN)


def unused_zeroed(place_ref, w, part):
    at_row = lax.broadcasted_iota(jnp.int32, (WIN, D), 0)
    return jnp.where(at_row < used(place_ref, w), part, 0.0)


def project_rows(hidden_low, wq, project):
    for c in range(3):
        at = slice(c * D, (c + 1) * D)
        project[:, at] = nn(hidden_low, wq[:, at]).astype(BF16)


def attend(mask, project, probs, mixed):
    lanes = lax.broadcasted_iota(jnp.int32, (WIN, 128), 1)
    for step in range(8):
        w, p = step // 4, step % 4
        rows = window_rows(w)
        at = [slice(j * D + p * 128, j * D + (p + 1) * 128) for j in range(3)]
        q2 = project[rows, at[0]] * jnp.asarray(0.125, BF16)
        k2 = project[rows, at[1]]
        v2 = project[rows, at[2]]
        blocked = mask[w]
        parts = []
        for h in range(2):
            own = (lanes >= 64) if h else (lanes < 64)
            qm = jnp.where(own, q2, jnp.zeros_like(q2))
            scores = nt(qm, k2) + blocked
            raised = jnp.exp(scores - jnp.max(scores, -1, keepdims=True))
            soft = (raised * (1.0 / jnp.sum(raised, -1, keepdims=True))).astype(BF16)
            probs[step * 2 + h] = soft
            parts.append(nn(soft, v2))
        mixed[rows, at[0]] = jnp.where(lanes < 64, parts[0], parts[1]).astype(BF16)


def attend_back(project, probs, grad_mixed, grad_project):
    lanes = lax.broadcasted_iota(jnp.int32, (WIN, 128), 1)
    for step in range(8):
        w, p = step // 4, step % 4
        rows = window_rows(w)
        at = [slice(j * D + p * 128, j * D + (p + 1) * 128) for j in range(3)]
        q2 = project[rows, at[0]] * jnp.asarray(0.125, BF16)
        k2 = project[rows, at[1]]
        v2 = project[rows, at[2]]
        g2 = grad_mixed[rows, at[0]]
        grad_q, grad_k, grad_v = [], [], []
        for h in range(2):
            own = (lanes >= 64) if h else (lanes < 64)
            none = jnp.zeros_like(q2)
            gm = jnp.where(own, g2, none)
            qm = jnp.where(own, q2, none)
            soft_low = probs[step * 2 + h]
            soft = soft_low.astype(F32)
            product = soft * nt(gm, v2)
            grad_scores = (product - soft * jnp.sum(product, -1, keepdims=True)).astype(BF16)
            grad_q.append(nn(grad_scores, k2))
            grad_k.append(tn(grad_scores, qm))
            grad_v.append(tn(soft_low, gm))
        grad_project[rows, at[0]] = (
            jnp.where(lanes < 64, grad_q[0], grad_q[1]) * 0.125
        ).astype(BF16)
        grad_project[rows, at[1]] = (grad_k[0] + grad_k[1]).astype(BF16)
        grad_project[rows, at[2]] = (grad_v[0] + grad_v[1]).astype(BF16)


def feed(small, sum_one, wu, wd, acc, low_ref, active_ref, slope_ref):
    normed, _ = normalize(sum_one + small[0:1])
    after = normed * small[1:2] + small[2:3]
    acc[...] = after
    low = after.astype(BF16)
    low_ref[...] = low
    for c in range(4):
        block = slice(c * D, (c + 1) * D)
        value = nn(low, wu[:, block]) + small[6 + c : 7 + c]
        active, slope = gelu_pair(value)
        active = active.astype(BF16)
        active_ref[:, block] = active
        slope_ref[:, block] = slope.astype(BF16)
        acc[...] += nn(active, wd[block, :])
    return acc[...] + small[3:4]


def feed_back(
    sec, small, e, sum_two, wu, wd, acc, low_ref, active_ref, slope_ref, small_ref, grads, send
):
    normed, inverse = normalize(sum_two)
    small_ref[...] = jnp.zeros_like(small_ref)
    small_ref[1:2, :] = jnp.sum(e * normed, 0, keepdims=True)
    small_ref[2:3, :] = jnp.sum(e, 0, keepdims=True)
    grad_sum = norm_backward(e, normed, inverse, small[4:5])
    acc[...] = grad_sum
    grad_low = grad_sum.astype(BF16)
    small_ref[0:1, :] = jnp.sum(grad_low.astype(F32), 0, keepdims=True)
    for c in range(4):
        block = slice(c * D, (c + 1) * D)
        grad_up = nt(grad_low, wd[block, :]) * slope_ref[:, block].astype(F32)
        grad_up = grad_up.astype(BF16)
        small_ref[3 + c : 4 + c, :] = jnp.sum(grad_up.astype(F32), 0, keepdims=True)
        acc[...] += nt(grad_up, wu[:, block])
        grad_wu = tn(low_ref[...], grad_up).astype(BF16)
        grad_wd = tn(active_ref[:, block], grad_low).astype(BF16)
        for k in range(4):
            at = slice((c * 4 + k) * D, (c * 4 + k + 1) * D)
            grads[0, at, :] = grad_wu[:, k * 128 : (k + 1) * 128]
            grads[1, at, :] = grad_wd[:, k * 128 : (k + 1) * 128]
        at = slice(c * 2048, (c + 1) * 2048)
        send[at, :] = grads[1 - sec, at, :]


def input_back(
    sec, stream, pos, wq, grad_sum, grad_out, rows, grad_project, total, grads, send
):
    for c in range(4):
        lanes_at = slice(c * 128, (c + 1) * 128)
        grads[1, 2048 + c * D : 2048 + (c + 1) * D, :] = grad_out[:, lanes_at]
        for half in range(2):
            grads[half, 4608 + c * 16 : 4608 + (c + 1) * 16, :] = rows[:, lanes_at]
    for half in range(2):
        grads[half, 4672:5120, :] = jnp.zeros((448, 128), BF16)
    position = pos[...].astype(F32)
    hidden_low = jnp.concatenate(
        [(stream[w].astype(F32) + position).astype(BF16) for w in range(2)], 0
    )
    total[...] = grad_sum[...]
    for j in range(3):
        block = slice(j * D, (j + 1) * D)
        part = grad_project[:, block]
        total[...] += nt(part, wq[:, block])
        grad_w = tn(hidden_low, part).astype(BF16)
        half, base = ((0, 0), (0, 2048), (1, 0))[j]
        for c in range(4):
            grads[half, base + c * D : base + (c + 1) * D, :] = grad_w[:, c * 128 : (c + 1) * 128]
    grad_pos = (total[0:WIN, :] + total[WIN : 2 * WIN, :]).astype(BF16)
    for half in range(2):
        for c in range(4):
            grads[half, 4096 + c * 128 : 4096 + (c + 1) * 128, :] = grad_pos[
                half * 128 : (half + 1) * 128, c * 128 : (c + 1) * 128
            ]
    send[...] = grads[1 - sec]


def first_kernel(
    place_ref,
    tokens,
    pos_m,
    pos_o,
    wq_m,
    wq_o,
    wo_m,
    wo_o,
    project,
    probs,
    mixed,
    sum_one,
    hidden,
    mask,
):
    sec = place_ref[0]
    near = sec == 0
    write_mask(place_ref, mask)
    position = jnp.where(near, pos_m[0].astype(F32), pos_o[0].astype(F32))
    for w in range(2):
        hidden[window_rows(w), :] = tokens[sec, w].astype(F32) + position
    hidden_low = hidden[...].astype(BF16)

    @pl.when(near)
    def _():
        project_rows(hidden_low, wq_m.at[0], project)

    @pl.when(jnp.logical_not(near))
    def _():
        project_rows(hidden_low, wq_o.at[0], project)

    attend(mask, project, probs, mixed)

    @pl.when(near)
    def _():
        sum_one[...] = hidden[...] + nn(mixed[...], wo_m[0])

    @pl.when(jnp.logical_not(near))
    def _():
        sum_one[...] = hidden[...] + nn(mixed[...], wo_o[0])


ATTENTION_KEPT = [
    sds((ROWS, 3 * D), BF16),
    sds((16, WIN, WIN), BF16),
    sds((ROWS, D), BF16),
    sds((ROWS, D), F32),
]
FEED_KEPT = [
    sds((ROWS, D), BF16),
    sds((ROWS, FF), BF16),
    sds((ROWS, FF), BF16),
    sds((ROWS, D), F32),
]
FFN_GRADS = [
    sds((ROWS, D), F32),
    sds((8, D), F32),
    sds((2, 8192, 128), BF16),
    sds((8192, 128), BF16),
]
ATT_GRADS = [sds((2, 5120, 128), BF16), sds((5120, 128), BF16)]


def forward_first(place, tokens, mine, other):
    args = [place, tokens]
    for i in (0, 1, 2):
        args += [mine[i], other[i]]
    return pl.pallas_call(
        first_kernel,
        out_shape=ATTENTION_KEPT,
        in_specs=[SM] + [VM] * 7,
        out_specs=[VM] * 4,
        scratch_shapes=[pltpu.VMEM((ROWS, D), F32), pltpu.VMEM((2, WIN, WIN), F32)],
        compiler_params=limit(20),
        cost_estimate=HEAVY,
        name="forward_attention_0",
    )(*args)


def middle_kernel(
    place_ref,
    cotangent,
    pos_m,
    pos_o,
    wq_m,
    wq_o,
    wo_m,
    wo_o,
    wu_m,
    wu_o,
    wd_m,
    wd_o,
    vec_m,
    vec_o,
    sum_one_0,
    low_0,
    active_0,
    slope_0,
    sum_two_0,
    stream_1,
    project_1,
    probs_1,
    mixed_1,
    sum_one_1,
    output,
    grad_after,
    small_grads,
    grads,
    send,
    arriving,
    pos,
    wq,
    wo,
    wu,
    wd,
    hidden,
    mask,
    acc,
    low_1,
    active_1,
    slope_1,
    sems,
):
    sec = place_ref[0]
    near_0 = sec == 0
    near_1 = sec == 1
    wait_up = fetch(near_0, wu_m, wu_o, wu, sems.at[0])
    wait_down = fetch(near_0, wd_m, wd_o, wd, sems.at[1])
    wait_pos = fetch(near_1, pos_m, pos_o, pos, sems.at[2])
    wait_qkv = fetch(near_1, wq_m, wq_o, wq, sems.at[3])
    wait_out = fetch(near_1, wo_m, wo_o, wo, sems.at[4])
    wait_cotangent = copy(cotangent.at[sec], arriving, sems.at[5])
    write_mask(place_ref, mask)
    small_0 = chosen(near_0, vec_m, vec_o)
    small_1 = chosen(near_1, vec_m, vec_o)
    wait_up()
    wait_down()
    sum_two = feed(small_0, sum_one_0[...], wu, wd, acc, low_0, active_0, slope_0)
    sum_two_0[...] = sum_two
    wait_up = fetch(near_1, wu_m, wu_o, wu, sems.at[0])
    wait_down = fetch(near_1, wd_m, wd_o, wd, sems.at[1])
    wait_pos()
    wait_qkv()
    normed, _ = normalize(sum_two)
    result = (normed * small_0[4:5] + small_0[5:6]).astype(BF16)
    position = pos[...].astype(F32)
    for w in range(2):
        rows = window_rows(w)
        stream_1[w] = result[rows]
        hidden[rows, :] = result[rows].astype(F32) + position
    project_rows(hidden[...].astype(BF16), wq, project_1)
    attend(mask, project_1, probs_1, mixed_1)
    wait_out()
    wait_up()
    wait_down()
    wait_cotangent()
    sum_one = hidden[...] + nn(mixed_1[...], wo[...])
    sum_one_1[...] = sum_one
    sum_two = feed(small_1, sum_one, wu, wd, acc, low_1, active_1, slope_1)
    normed, _ = normalize(sum_two)
    result = normed * small_1[4:5] + small_1[5:6]
    upstream = []
    for w in range(2):
        output[w] = unused_zeroed(place_ref, w, result[window_rows(w)]).astype(BF16)
        upstream.append(unused_zeroed(place_ref, w, arriving[w].astype(F32)))
    e = jnp.concatenate(upstream, 0)
    feed_back(
        sec, small_1, e, sum_two, wu, wd, acc, low_1, active_1, slope_1, small_grads, grads, send
    )
    grad_after[...] = acc[...]


def forward_middle(place, cotangent, mine, other, sum_one):
    args = [place, cotangent]
    for a, b in zip(mine, other):
        args += [a, b]
    return pl.pallas_call(
        middle_kernel,
        out_shape=FEED_KEPT
        + [sds((2, WIN, D), BF16)]
        + ATTENTION_KEPT
        + [sds((2, WIN, D), BF16)]
        + FFN_GRADS,
        in_specs=[SM] + [HBM] * 11 + [VM] * 3,
        out_specs=[VM] * 14,
        scratch_shapes=[
            pltpu.VMEM((2, WIN, D), BF16),
            pltpu.VMEM((WIN, D), BF16),
            pltpu.VMEM((D, 3 * D), BF16),
            pltpu.VMEM((D, D), BF16),
            pltpu.VMEM((D, FF), BF16),
            pltpu.VMEM((FF, D), BF16),
            pltpu.VMEM((ROWS, D), F32),
            pltpu.VMEM((2, WIN, WIN), F32),
            pltpu.VMEM((ROWS, D), F32),
            pltpu.VMEM((ROWS, D), BF16),
            pltpu.VMEM((ROWS, FF), BF16),
            pltpu.VMEM((ROWS, FF), BF16),
            DMA((6,)),
        ],
        compiler_params=limit(MIDDLE_LIMIT),
        cost_estimate=HEAVY,
        name="feed_0_to_feed_backward_1",
    )(*args, sum_one)


MIDDLE_LIMIT = 32


def out_kernel(
    layer,
    place_ref,
    wo_m,
    wo_o,
    vec_m,
    vec_o,
    grad_after,
    sum_one,
    mixed,
    small_in,
    grad_sum_ref,
    grad_mixed,
    grad_out,
    rows_ref,
    wo,
    sem,
):
    near = place_ref[0] == layer
    wait_out = fetch(near, wo_m, wo_o, wo, sem)
    small = chosen(near, vec_m, vec_o)
    normed, inverse = normalize(sum_one[...] + small[0:1])
    e = grad_after[...]
    row_norm = jnp.sum(e * normed, 0, keepdims=True)
    row_shift = jnp.sum(e, 0, keepdims=True)
    grad_sum = norm_backward(e, normed, inverse, small[1:2])
    grad_sum_ref[...] = grad_sum
    branch = grad_sum.astype(BF16)
    row_out = jnp.sum(branch.astype(F32), 0, keepdims=True)
    rows = jnp.concatenate([row_out, row_norm, row_shift, jnp.zeros((5, D), F32)], 0)
    rows_ref[...] = jnp.concatenate([rows, small_in[...]], 0).astype(BF16)
    wait_out()
    grad_mixed[...] = nt(branch, wo[...]).astype(BF16)
    grad_out[...] = tn(mixed[...], branch).astype(BF16)


def out_back(layer, place, mine, other, grad_after, kept, small):
    def body(*refs):
        out_kernel(layer, *refs)

    return pl.pallas_call(
        body,
        out_shape=[
            sds((ROWS, D), F32),
            sds((ROWS, D), BF16),
            sds((D, D), BF16),
            sds((16, D), BF16),
        ],
        in_specs=[SM] + [HBM] * 2 + [VM] * 6,
        out_specs=[VM] * 4,
        scratch_shapes=[pltpu.VMEM((D, D), BF16), DMA],
        compiler_params=limit(16),
        cost_estimate=HEAVY,
        name=f"projection_backward_{layer}",
    )(place, mine[2], other[2], mine[5], other[5], grad_after, kept[3], kept[2], small)


def late_kernel(
    place_ref,
    pos_m,
    pos_o,
    wq_m,
    wq_o,
    wu_m,
    wu_o,
    wd_m,
    wd_o,
    vec_m,
    vec_o,
    stream_1,
    project_1,
    probs_1,
    grad_sum,
    grad_mixed,
    grad_out,
    rows_1,
    low_0,
    active_0,
    slope_0,
    sum_two_0,
    att_grads,
    att_send,
    grad_after,
    small_grads,
    ffn_grads,
    ffn_send,
    pos,
    wq,
    wu,
    wd,
    grad_project,
    total,
    sems,
):
    sec = place_ref[0]
    wait_qkv = fetch(sec == 1, wq_m, wq_o, wq, sems.at[0])
    wait_pos = fetch(sec == 1, pos_m, pos_o, pos, sems.at[1])
    wait_down = fetch(sec == 0, wd_m, wd_o, wd, sems.at[2])
    wait_up = fetch(sec == 0, wu_m, wu_o, wu, sems.at[3])
    small = chosen(sec == 0, vec_m, vec_o)
    attend_back(project_1, probs_1, grad_mixed, grad_project)
    wait_qkv()
    wait_pos()
    wait_down()
    wait_up()
    input_back(
        sec, stream_1, pos, wq, grad_sum, grad_out, rows_1, grad_project, total, att_grads, att_send
    )
    e = total[...].astype(BF16).astype(F32)
    feed_back(
        sec,
        small,
        e,
        sum_two_0[...],
        wu,
        wd,
        total,
        low_0,
        active_0,
        slope_0,
        small_grads,
        ffn_grads,
        ffn_send,
    )
    grad_after[...] = total[...]


def late_back(place, mine, other, stream, attention, before, feed_kept):
    args = [place]
    for i in (0, 1, 3, 4, 5):
        args += [mine[i], other[i]]
    return pl.pallas_call(
        late_kernel,
        out_shape=ATT_GRADS + FFN_GRADS,
        in_specs=[SM] + [HBM] * 8 + [VM] * 13,
        out_specs=[VM] * 6,
        scratch_shapes=[
            pltpu.VMEM((WIN, D), BF16),
            pltpu.VMEM((D, 3 * D), BF16),
            pltpu.VMEM((D, FF), BF16),
            pltpu.VMEM((FF, D), BF16),
            pltpu.VMEM((ROWS, 3 * D), BF16),
            pltpu.VMEM((ROWS, D), F32),
            DMA((4,)),
        ],
        compiler_params=limit(24),
        cost_estimate=HEAVY,
        name="attention_backward_1_and_feed_backward_0",
    )(*args, stream, attention[0], attention[1], *before, *feed_kept)


def last_kernel(
    place_ref,
    tokens,
    pos_m,
    pos_o,
    wq_m,
    wq_o,
    project,
    probs,
    grad_sum,
    grad_mixed,
    grad_out,
    rows,
    grad_low,
    grads,
    send,
    stream,
    pos,
    wq,
    grad_project,
    total,
    sems,
):
    sec = place_ref[0]
    wait_qkv = fetch(sec == 0, wq_m, wq_o, wq, sems.at[0])
    wait_pos = fetch(sec == 0, pos_m, pos_o, pos, sems.at[1])
    wait_stream = copy(tokens.at[sec], stream, sems.at[2])
    attend_back(project, probs, grad_mixed, grad_project)
    wait_qkv()
    wait_pos()
    wait_stream()
    input_back(
        sec, stream, pos, wq, grad_sum, grad_out, rows, grad_project, total, grads, send
    )
    for w in range(2):
        grad_low[w] = total[window_rows(w), :].astype(BF16)


def last_back(place, tokens, mine, other, attention, before):
    args = [place, tokens]
    for i in (0, 1):
        args += [mine[i], other[i]]
    return pl.pallas_call(
        last_kernel,
        out_shape=[sds((2, WIN, D), BF16)] + ATT_GRADS,
        in_specs=[SM] + [HBM] * 5 + [VM] * 6,
        out_specs=[VM] * 3,
        scratch_shapes=[
            pltpu.VMEM((2, WIN, D), BF16),
            pltpu.VMEM((WIN, D), BF16),
            pltpu.VMEM((D, 3 * D), BF16),
            pltpu.VMEM((ROWS, 3 * D), BF16),
            pltpu.VMEM((ROWS, D), F32),
            DMA((3,)),
        ],
        compiler_params=limit(20),
        cost_estimate=HEAVY,
        name="attention_backward_0",
    )(*args, attention[0], attention[1], *before)


def pack_vectors(b_out, gain_one, shift_one, b_down, gain_two, shift_two, b_up):
    def body(*refs):
        out = refs[-1]
        rows = [ref[...].astype(F32) for ref in refs[:6]]
        wide = refs[6][...].astype(F32)
        rows += [wide[:, c * D : (c + 1) * D] for c in range(4)]
        rows += [jnp.zeros((6, D), F32)]
        out[...] = jnp.concatenate(rows, 0).astype(BF16)

    return pl.pallas_call(
        body,
        out_shape=sds((16, D), BF16),
        in_specs=[VM] * 7,
        out_specs=VM,
        name="pack_vectors",
    )(b_out, gain_one, shift_one, b_down, gain_two, shift_two, b_up)


def plain(body, shapes, args, name, specs=None):
    return pl.pallas_call(
        body,
        out_shape=[sds(shape, BF16) for shape in shapes],
        in_specs=specs or [VM] * len(args),
        out_specs=[VM] * len(shapes),
        compiler_params=limit(24),
        cost_estimate=SLIGHT,
        name=name,
    )(*args)


def stage_order(place_ref):
    first = place_ref[0] == 0
    strides = [jnp.where(first, a, b) for a, b in zip(*WAY)]
    coords = [lax.rem(lax.div(place_ref[1], stride), 4) for stride in strides]

    def owner(*distances):
        return sum(
            lax.rem(coord + r, 4) * stride
            for coord, r, stride in zip(coords, distances, strides)
        )

    return owner


def pair_sum(place, *arrays):
    sizes = [got.shape[0] // 64 for got in arrays[1::2]]
    part = sum(sizes)

    def body(place_ref, *refs):
        outs = refs[len(arrays) :]
        owner = stage_order(place_ref)
        sec = place_ref[0]
        for third in range(4):
            for second in range(4):
                for first in range(4):
                    dev = owner(first, second, third)
                    at = (second * 4 + first) * part
                    for i, rows in enumerate(sizes):
                        src = pl.ds(pl.multiple_of(dev * rows, 16), rows)
                        total = refs[2 * i][sec, src, :].astype(F32)
                        total += refs[2 * i + 1][src, :].astype(F32)
                        outs[third][at : at + rows, :] = total.astype(BF16)
                        at += rows

    specs = [SM] + [VM] * len(arrays)
    return plain(body, [(16 * part, 128)] * 4, (place,) + arrays, "sum_of_two_cores", specs)


def add_four(refs, at):
    return sum(ref[at].astype(F32) for ref in refs)


def line_sum(late_ffn, mixed, early_att):
    def body(*refs):
        outs = refs[12:]
        for r in range(4):
            for first in range(4):
                i = r * 4 + first

                def add(source, at, layer, low, rows):
                    total = add_four(refs[source : source + 4], (slice(at, at + rows), slice(None)))
                    outs[r][first, layer, low : low + rows, :] = total.astype(BF16)

                add(0, i * FFN_PART, 1, 0, FFN_PART)
                add(4, i * CHUNK, 0, 0, FFN_PART)
                add(4, i * CHUNK + FFN_PART, 1, FFN_PART, ATT_PART)
                add(8, i * ATT_PART, 0, FFN_PART, ATT_PART)

    args = late_ffn + mixed + early_att
    return plain(body, [(4, 2, CHUNK, 128)] * 4, args, "sum_over_line")


def plane_sum(pieces):
    def body(*refs):
        for first in range(4):
            refs[4 + first][...] = add_four(refs[:4], first).astype(BF16)

    return plain(body, [pieces[0].shape[1:]] * 4, pieces, "sum_over_plane")


def cube_sum(place, pieces):
    def body(place_ref, *refs):
        sec = place_ref[0]
        refs[4][...] = add_four(refs[:4], sec).astype(BF16)
        refs[5][...] = add_four(refs[:4], 1 - sec).astype(BF16)

    specs = [SM] + [VM] * 4
    return plain(body, [(CHUNK, 128)] * 2, [place] + pieces, "sum_over_cube", specs)


def unpack_kernel(place_ref, *refs):
    sources, refs = refs[:8], refs[8:]
    pos_ref, wq_ref, wo_ref, bo_ref, g1_ref, s1_ref, wu_ref, bu_ref = refs[:8]
    wd_ref, bd_ref, g2_ref, s2_ref, parts, att, wu, wd, wq, wo, isems, osems = refs[8:]
    sec = place_ref[0]
    loads = []
    for i, ref in enumerate(sources):
        loads.append(pltpu.make_async_copy(ref, parts.at[i], isems.at[i]))
        loads[i].start()
    owner = stage_order(place_ref)
    for i in range(8):
        loads[i].wait()

        def place(step, carry, i=i):
            dev = owner(lax.rem(step, 4), (i % 2) * 2 + lax.div(step, 4), i // 2)
            block = lax.div(dev, 4)
            r = lax.rem(dev, 4)
            lane = pl.ds(pl.multiple_of(block * 128, 128), 128)
            at = pl.ds(pl.multiple_of(r * 128, 128), 128)
            wu[at, lane] = parts[i, step, sec, 0:FFN_PART, :].astype(F32)
            at = pl.ds(pl.multiple_of(lax.div(block, 4) * D + r * 128, 128), 128)
            lane = pl.ds(pl.multiple_of(lax.rem(block, 4) * 128, 128), 128)
            wd[at, lane] = parts[i, step, 1 - sec, 0:FFN_PART, :].astype(F32)
            at = pl.ds(pl.multiple_of(dev * ATT_PART, 16), ATT_PART)
            att[0, at, :] = parts[i, step, sec, FFN_PART:CHUNK, :]
            att[1, at, :] = parts[i, step, 1 - sec, FFN_PART:CHUNK, :]
            return carry

        lax.fori_loop(0, 8, place, 0)
    stores = [
        pltpu.make_async_copy(wu, wu_ref.at[0], osems.at[0]),
        pltpu.make_async_copy(wd, wd_ref.at[0], osems.at[1]),
        pltpu.make_async_copy(wq, wq_ref.at[0], osems.at[2]),
        pltpu.make_async_copy(wo, wo_ref.at[0], osems.at[3]),
    ]
    stores[0].start()
    stores[1].start()
    for c in range(4):
        at = slice(c * D, (c + 1) * D)
        later = slice(2048 + c * D, 2048 + (c + 1) * D)
        wq[:, c * 128 : (c + 1) * 128] = att[0, at, :].astype(F32)
        wq[:, D + c * 128 : D + (c + 1) * 128] = att[0, later, :].astype(F32)
        wq[:, 2 * D + c * 128 : 2 * D + (c + 1) * 128] = att[1, at, :].astype(F32)
    stores[2].start()
    for c in range(4):
        lane = slice(c * 128, (c + 1) * 128)
        wo[:, lane] = att[1, 2048 + c * D : 2048 + (c + 1) * D, :].astype(F32)
        for half in range(2):
            pos_ref[0, half * 128 : (half + 1) * 128, lane] = att[
                half, 4096 + c * 128 : 4096 + (c + 1) * 128, :
            ].astype(F32)
        small = att[0, 4608 + c * 16 : 4608 + (c + 1) * 16, :].astype(F32)
        for ref, row in (
            (bo_ref, 0),
            (g1_ref, 1),
            (s1_ref, 2),
            (bd_ref, 8),
            (g2_ref, 9),
            (s2_ref, 10),
        ):
            ref[:, lane] = small[row : row + 1]
        for j in range(4):
            bu_ref[:, j * D + c * 128 : j * D + (c + 1) * 128] = small[11 + j : 12 + j]
    stores[3].start()
    for store in stores:
        store.wait()


def unpack(place, pieces):
    small = [sds((1, D), F32)] * 3
    return pl.pallas_call(
        unpack_kernel,
        out_shape=[sds((1, WIN, D), F32), sds((1, D, 3 * D), F32), sds((1, D, D), F32)]
        + small
        + [sds((1, D, FF), F32), sds((1, FF), F32), sds((1, FF, D), F32)]
        + small,
        in_specs=[SM] + [VM] * 8,
        out_specs=[VM, HBM, HBM, VM, VM, VM, HBM, VM, HBM, VM, VM, VM],
        scratch_shapes=[
            pltpu.VMEM((8, 8, 2, CHUNK, 128), BF16),
            pltpu.VMEM((2, 64 * ATT_PART, 128), BF16),
            pltpu.VMEM((D, FF), F32),
            pltpu.VMEM((FF, D), F32),
            pltpu.VMEM((D, 3 * D), F32),
            pltpu.VMEM((D, D), F32),
            DMA((8,)),
            DMA((4,)),
        ],
        compiler_params=limit(40),
        cost_estimate=SLIGHT,
        name="unpack_gradients",
    )(place, *pieces)


def swap(value):
    return lax.ppermute(value, "section", [(0, 1), (1, 0)])


def from_ahead(value, stage, distance):
    pairs = []
    for section in range(2):
        stride = WAY[section][stage]
        for dst in range(64):
            at = dst // stride % 4
            src = dst + ((at + distance) % 4 - at) * stride
            pairs.append((section * 64 + src, section * 64 + dst))
    return lax.ppermute(value, ("section", "dp"), pairs)


def send_ahead(pieces, stage):
    return [pieces[0]] + [from_ahead(pieces[r], stage, 4 - r) for r in (1, 3, 2)]


def gather(chunk):
    line = jnp.stack([chunk] + [from_ahead(chunk, 0, r) for r in (1, 2, 3)])
    ahead = [from_ahead(line, 1, r) for r in (1, 2, 3)]
    own_a = jnp.concatenate([line, ahead[0]], 0)
    own_b = jnp.concatenate([ahead[1], ahead[2]], 0)
    next_a = from_ahead(own_a, 2, 1)
    prev_b = from_ahead(own_b, 2, 3)
    next_b = from_ahead(own_b, 2, 1)
    prev_a = from_ahead(own_a, 2, 3)
    far_a = from_ahead(next_a, 2, 1)
    far_b = from_ahead(prev_b, 2, 3)
    return own_a, own_b, next_a, next_b, far_a, far_b, prev_a, prev_b


def hold(*values):
    return tuple(pltpu.with_memory_space_constraint(value, pltpu.HBM) for value in values)


def shards(
    tokens,
    lengths,
    out_cotangent,
    pos_table,
    w_qkv,
    w_out,
    b_out,
    norm1_gain,
    norm1_bias,
    w_up,
    b_up,
    w_down,
    b_down,
    norm2_gain,
    norm2_bias,
):
    section = lax.axis_index("section")
    place = jnp.stack([section, lax.axis_index("dp")]).astype(jnp.int32)
    place = jnp.concatenate([place, lengths.reshape(4)])
    vec = pack_vectors(b_out, norm1_gain, norm1_bias, b_down, norm2_gain, norm2_bias, b_up)
    got_qkv = swap(w_qkv)
    got_pos = swap(pos_table)
    got_out = swap(w_out)
    late_up, late_down, got_qkv = lax.optimization_barrier((w_up, w_down, got_qkv))
    near = (pos_table, w_qkv, w_out)
    far = (got_pos, got_qkv, got_out)
    mine = hold(pos_table, w_qkv, w_out, w_up, w_down) + (vec,)
    other = hold(got_pos, got_qkv, got_out, swap(late_up), swap(late_down)) + (swap(vec),)
    attention_0 = forward_first(place, tokens, near, far)
    late_tokens, out_cotangent = hold(tokens, out_cotangent)
    middle = forward_middle(place, out_cotangent, mine, other, attention_0[3])
    feed_0, stream, attention_1, output = middle[0:4], middle[4], middle[5:9], middle[9]
    after, small, ffn_both, ffn_send = middle[10:14]

    def tie(*values):
        return lax.optimization_barrier(values)

    ffn_got = swap(ffn_send)
    before = out_back(1, place, mine, other, after, attention_1, small)
    pieces = pair_sum(place, ffn_both, ffn_got)
    before, pieces = tie(before, pieces)
    late_ffn = send_ahead(pieces, 2)
    att_both, att_send, after, small, ffn_both, ffn_send = late_back(
        place, mine, other, stream, attention_1, before, feed_0
    )
    after, late_ffn = tie(after, late_ffn)
    att_got = swap(att_send)
    ffn_got = swap(ffn_send)
    before = out_back(0, place, mine, other, after, attention_0, small)
    pieces = pair_sum(place, ffn_both, ffn_got, att_both, att_got)
    before, pieces = tie(before, pieces)
    mixed = send_ahead(pieces, 2)
    arriving, att_both, att_send = last_back(place, late_tokens, mine, other, attention_0, before)
    att_send, mixed = tie(att_send, mixed)
    early_att = send_ahead(pair_sum(place, att_both, swap(att_send)), 2)
    pieces = line_sum(late_ffn, mixed, early_att)
    pieces = plane_sum(send_ahead(pieces, 1))
    own, others = cube_sum(place, send_ahead(pieces, 0))
    chunk = jnp.stack([own, swap(others)])
    return (output[None], arriving[None]) + tuple(unpack(place, gather(chunk)))


def solution(mesh):
    placed = (
        P(None, "dp", None, None),
        P(None, "dp"),
        P(None, "dp", None, None),
        P("section", None, None),
        P("section", None, None),
        P("section", None, None),
        P("section", None),
        P("section", None),
        P("section", None),
        P("section", None, None),
        P("section", None),
        P("section", None, None),
        P("section", None),
        P("section", None),
        P("section", None),
    )
    return jax.shard_map(
        shards,
        mesh=mesh,
        in_specs=placed,
        out_specs=(
            P("section", "dp", None, None),
            P("section", "dp", None, None),
            P("section", None, None),
            P("section", None, None),
            P("section", None, None),
            P("section", None),
            P("section", None),
            P("section", None),
            P("section", None, None),
            P("section", None),
            P("section", None, None),
            P("section", None),
            P("section", None),
            P("section", None),
        ),
        check_vma=False,
    )
```

```python
import jax
import jax.numpy as jnp
from jax import lax
from jax.experimental import pallas as pl
from jax.experimental.pallas import tpu as pltpu
from jax.sharding import PartitionSpec as P

D = 512
FF = 2048
WIN = 256
ROWS = 512
F32 = jnp.float32
BF16 = jnp.bfloat16

HBM = pl.BlockSpec(memory_space=pltpu.HBM)
VM = pl.BlockSpec(memory_space=pltpu.VMEM)
SM = pl.BlockSpec(memory_space=pltpu.SMEM)
DMA = pltpu.SemaphoreType.DMA
SLIGHT = pl.CostEstimate(flops=1000, bytes_accessed=1000, transcendentals=0)
HEAVY = pl.CostEstimate(flops=35_000_000_000, bytes_accessed=1000, transcendentals=0)
EXTRA = 4096
FFN_PART = 128
ATT_PART = 80
CHUNK = FFN_PART + ATT_PART
WAY = ((16, 4, 1), (1, 16, 4))


def limit(mebibytes):
    return pltpu.CompilerParams(vmem_limit_bytes=mebibytes * 1024 * 1024)


def sds(shape, dtype):
    return jax.ShapeDtypeStruct(shape, dtype)


def nn(a, b):
    return lax.dot_general(a, b, (((1,), (0,)), ((), ())), preferred_element_type=F32)


def nt(a, b):
    return lax.dot_general(a, b, (((1,), (1,)), ((), ())), preferred_element_type=F32)


def tn(a, b):
    return lax.dot_general(a, b, (((0,), (0,)), ((), ())), preferred_element_type=F32)


def fetch(near, mine, other, dst, sem):
    @pl.when(near)
    def _():
        pltpu.make_async_copy(mine.at[0], dst, sem).start()

    @pl.when(jnp.logical_not(near))
    def _():
        pltpu.make_async_copy(other.at[0], dst, sem).start()

    return pltpu.make_async_copy(mine.at[0], dst, sem).wait


def copy(src, dst, sem):
    load = pltpu.make_async_copy(src, dst, sem)
    load.start()
    return load.wait


def chosen(near, mine, other):
    return jnp.where(near, mine[...].astype(F32), other[...].astype(F32))


def normalize(v):
    center = v - jnp.mean(v, -1, keepdims=True)
    inverse = lax.rsqrt(jnp.mean(center * center, -1, keepdims=True) + 1e-05)
    return center * inverse, inverse


def norm_backward(e, normed, inverse, gain):
    scaled = e * gain
    return inverse * (
        scaled
        - jnp.mean(scaled, -1, keepdims=True)
        - normed * jnp.mean(scaled * normed, -1, keepdims=True)
    )


def gelu_pair(v):
    c = 0.7978845608028654
    sq = v * v
    t = jnp.tanh(v * (c + (c * 0.044715) * sq))
    half = 0.5 + 0.5 * t
    slope = half + (0.5 * v) * (1.0 - t * t) * (c + (3.0 * c * 0.044715) * sq)
    return v * half, slope


def used(place_ref, window):
    return place_ref[2 + 2 * place_ref[0] + window]


def write_mask(place_ref, mask):
    rows = lax.broadcasted_iota(jnp.int32, (WIN, WIN), 0)
    cols = lax.broadcasted_iota(jnp.int32, (WIN, WIN), 1)
    for w in range(2):
        inside = (cols <= rows) & (cols < used(place_ref, w))
        mask[w] = jnp.where(inside, 0.0, -1e30)


def window_rows(w):
    return slice(w * WIN, (w + 1) * WIN)


def unused_zeroed(place_ref, w, part):
    at_row = lax.broadcasted_iota(jnp.int32, (WIN, D), 0)
    return jnp.where(at_row < used(place_ref, w), part, 0.0)


def project_rows(hidden_low, wq, project):
    for c in range(3):
        at = slice(c * D, (c + 1) * D)
        project[:, at] = nn(hidden_low, wq[:, at]).astype(BF16)


def attend(mask, project, probs, mixed):
    lanes = lax.broadcasted_iota(jnp.int32, (WIN, 128), 1)
    for step in range(8):
        w, p = step // 4, step % 4
        rows = window_rows(w)
        at = [slice(j * D + p * 128, j * D + (p + 1) * 128) for j in range(3)]
        q2 = project[rows, at[0]] * jnp.asarray(0.125, BF16)
        k2 = project[rows, at[1]]
        v2 = project[rows, at[2]]
        blocked = mask[w]
        parts = []
        for h in range(2):
            own = (lanes >= 64) if h else (lanes < 64)
            qm = jnp.where(own, q2, jnp.zeros_like(q2))
            scores = nt(qm, k2) + blocked
            raised = jnp.exp(scores - jnp.max(scores, -1, keepdims=True))
            soft = (raised * (1.0 / jnp.sum(raised, -1, keepdims=True))).astype(BF16)
            probs[step * 2 + h] = soft
            parts.append(nn(soft, v2))
        mixed[rows, at[0]] = jnp.where(lanes < 64, parts[0], parts[1]).astype(BF16)


def attend_back(project, probs, grad_mixed, grad_project):
    lanes = lax.broadcasted_iota(jnp.int32, (WIN, 128), 1)
    for step in range(8):
        w, p = step // 4, step % 4
        rows = window_rows(w)
        at = [slice(j * D + p * 128, j * D + (p + 1) * 128) for j in range(3)]
        q2 = project[rows, at[0]] * jnp.asarray(0.125, BF16)
        k2 = project[rows, at[1]]
        v2 = project[rows, at[2]]
        g2 = grad_mixed[rows, at[0]]
        grad_q, grad_k, grad_v = [], [], []
        for h in range(2):
            own = (lanes >= 64) if h else (lanes < 64)
            none = jnp.zeros_like(q2)
            gm = jnp.where(own, g2, none)
            qm = jnp.where(own, q2, none)
            soft_low = probs[step * 2 + h]
            soft = soft_low.astype(F32)
            product = soft * nt(gm, v2)
            grad_scores = (product - soft * jnp.sum(product, -1, keepdims=True)).astype(BF16)
            grad_q.append(nn(grad_scores, k2))
            grad_k.append(tn(grad_scores, qm))
            grad_v.append(tn(soft_low, gm))
        grad_project[rows, at[0]] = (
            jnp.where(lanes < 64, grad_q[0], grad_q[1]) * 0.125
        ).astype(BF16)
        grad_project[rows, at[1]] = (grad_k[0] + grad_k[1]).astype(BF16)
        grad_project[rows, at[2]] = (grad_v[0] + grad_v[1]).astype(BF16)


def feed(small, sum_one, wu, wd, acc, low_ref, active_ref, slope_ref):
    normed, _ = normalize(sum_one + small[0:1])
    after = normed * small[1:2] + small[2:3]
    acc[...] = after
    low = after.astype(BF16)
    low_ref[...] = low
    for c in range(4):
        block = slice(c * D, (c + 1) * D)
        value = nn(low, wu[:, block]) + small[6 + c : 7 + c]
        active, slope = gelu_pair(value)
        active = active.astype(BF16)
        active_ref[:, block] = active
        slope_ref[:, block] = slope.astype(BF16)
        acc[...] += nn(active, wd[block, :])
    return acc[...] + small[3:4]


def feed_back(
    sec, small, e, sum_two, wu, wd, acc, low_ref, active_ref, slope_ref, small_ref, grads, send
):
    normed, inverse = normalize(sum_two)
    small_ref[...] = jnp.zeros_like(small_ref)
    small_ref[1:2, :] = jnp.sum(e * normed, 0, keepdims=True)
    small_ref[2:3, :] = jnp.sum(e, 0, keepdims=True)
    grad_sum = norm_backward(e, normed, inverse, small[4:5])
    acc[...] = grad_sum
    grad_low = grad_sum.astype(BF16)
    small_ref[0:1, :] = jnp.sum(grad_low.astype(F32), 0, keepdims=True)
    for c in range(4):
        block = slice(c * D, (c + 1) * D)
        grad_up = nt(grad_low, wd[block, :]) * slope_ref[:, block].astype(F32)
        grad_up = grad_up.astype(BF16)
        small_ref[3 + c : 4 + c, :] = jnp.sum(grad_up.astype(F32), 0, keepdims=True)
        slope_ref[:, block] = grad_up
        grad_wu = tn(low_ref[...], grad_up).astype(BF16)
        grad_wd = tn(active_ref[:, block], grad_low).astype(BF16)
        for k in range(4):
            at = slice((c * 4 + k) * D, (c * 4 + k + 1) * D)
            grads[0, at, :] = grad_wu[:, k * 128 : (k + 1) * 128]
            grads[1, at, :] = grad_wd[:, k * 128 : (k + 1) * 128]
        at = slice(c * 2048, (c + 1) * 2048)
        send[at, :] = grads[1 - sec, at, :]
    acc[...] += nt(slope_ref[...], wu[...])


def input_back(
    sec, stream, pos, wq, grad_sum, grad_out, rows, grad_project, total, grads, send
):
    for c in range(4):
        grads[1, 2048 + c * D : 2048 + (c + 1) * D, :] = grad_out[:, c * 128 : (c + 1) * 128]
    position = pos[...].astype(F32)
    hidden_low = jnp.concatenate(
        [(stream[w].astype(F32) + position).astype(BF16) for w in range(2)], 0
    )
    total[...] = grad_sum[...]
    for j in range(3):
        block = slice(j * D, (j + 1) * D)
        part = grad_project[:, block]
        total[...] += nt(part, wq[:, block])
        grad_w = tn(hidden_low, part).astype(BF16)
        half, base = ((0, 0), (0, 2048), (1, 0))[j]
        for c in range(4):
            grads[half, base + c * D : base + (c + 1) * D, :] = grad_w[:, c * 128 : (c + 1) * 128]
    grad_pos = total[0:WIN, :] + total[WIN : 2 * WIN, :]
    small = rows[...].astype(F32)
    blank = jnp.zeros((8, 128), F32)
    for c in range(4):
        lanes_at = slice(c * 128, (c + 1) * 128)
        for half in range(2):
            extra = []
            for i in range(16):
                at = half * 128 + i * 8
                extra.append(grad_pos[at : at + 8, lanes_at])
                if c == 0 and i < 8:
                    extra.append(small[i % 2 * 8 : i % 2 * 8 + 8, i // 2 * 128 : i // 2 * 128 + 128])
                else:
                    extra.append(blank)
            at = EXTRA + c * WIN
            grads[half, at : at + WIN, :] = jnp.concatenate(extra, 0).astype(BF16)
    send[...] = grads[1 - sec]


def first_kernel(
    place_ref,
    tokens,
    pos_m,
    pos_o,
    wq_m,
    wq_o,
    wo_m,
    wo_o,
    project,
    probs,
    mixed,
    sum_one,
    stream,
    pos,
    wq,
    wo,
    hidden,
    mask,
    sems,
):
    sec = place_ref[0]
    wait_stream = copy(tokens.at[sec], stream, sems.at[0])
    wait_pos = fetch(sec == 0, pos_m, pos_o, pos, sems.at[1])
    wait_qkv = fetch(sec == 0, wq_m, wq_o, wq, sems.at[2])
    wait_out = fetch(sec == 0, wo_m, wo_o, wo, sems.at[3])
    write_mask(place_ref, mask)
    wait_stream()
    wait_pos()
    position = pos[...].astype(F32)
    for w in range(2):
        hidden[window_rows(w), :] = stream[w].astype(F32) + position
    wait_qkv()
    wait_out()
    project_rows(hidden[...].astype(BF16), wq, project)
    attend(mask, project, probs, mixed)
    sum_one[...] = hidden[...] + nn(mixed[...], wo[...])


ATTENTION_KEPT = [
    sds((ROWS, 3 * D), BF16),
    sds((16, WIN, WIN), BF16),
    sds((ROWS, D), BF16),
    sds((ROWS, D), F32),
]
FEED_KEPT = [
    sds((ROWS, D), BF16),
    sds((ROWS, FF), BF16),
    sds((ROWS, FF), BF16),
    sds((ROWS, D), F32),
]
FFN_GRADS = [
    sds((ROWS, D), F32),
    sds((8, D), F32),
    sds((2, 8192, 128), BF16),
    sds((8192, 128), BF16),
]
ATT_GRADS = [sds((2, 5120, 128), BF16), sds((5120, 128), BF16)]


def forward_first(place, tokens, mine, other):
    args = [place, tokens]
    for i in (0, 1, 2):
        args += [mine[i], other[i]]
    return pl.pallas_call(
        first_kernel,
        out_shape=ATTENTION_KEPT,
        in_specs=[SM] + [HBM] * 7,
        out_specs=[VM] * 4,
        scratch_shapes=[
            pltpu.VMEM((2, WIN, D), BF16),
            pltpu.VMEM((WIN, D), BF16),
            pltpu.VMEM((D, 3 * D), BF16),
            pltpu.VMEM((D, D), BF16),
            pltpu.VMEM((ROWS, D), F32),
            pltpu.VMEM((2, WIN, WIN), F32),
            DMA((4,)),
        ],
        compiler_params=limit(20),
        cost_estimate=HEAVY,
        name="forward_attention_0",
    )(*args)


def middle_kernel(
    place_ref,
    cotangent,
    pos_m,
    pos_o,
    wq_m,
    wq_o,
    wo_m,
    wo_o,
    wu_m,
    wu_o,
    wd_m,
    wd_o,
    vec_m,
    vec_o,
    sum_one_0,
    low_0,
    active_0,
    slope_0,
    sum_two_0,
    stream_1,
    project_1,
    probs_1,
    mixed_1,
    sum_one_1,
    output,
    grad_after,
    small_grads,
    grads,
    send,
    arriving,
    pos,
    wq,
    wo,
    wu,
    wd,
    hidden,
    mask,
    acc,
    low_1,
    active_1,
    slope_1,
    sems,
):
    sec = place_ref[0]
    near_0 = sec == 0
    near_1 = sec == 1
    wait_up = fetch(near_0, wu_m, wu_o, wu, sems.at[0])
    wait_down = fetch(near_0, wd_m, wd_o, wd, sems.at[1])
    wait_pos = fetch(near_1, pos_m, pos_o, pos, sems.at[2])
    wait_qkv = fetch(near_1, wq_m, wq_o, wq, sems.at[3])
    wait_out = fetch(near_1, wo_m, wo_o, wo, sems.at[4])
    wait_cotangent = copy(cotangent.at[sec], arriving, sems.at[5])
    write_mask(place_ref, mask)
    small_0 = chosen(near_0, vec_m, vec_o)
    small_1 = chosen(near_1, vec_m, vec_o)
    wait_up()
    wait_down()
    sum_two = feed(small_0, sum_one_0[...], wu, wd, acc, low_0, active_0, slope_0)
    sum_two_0[...] = sum_two
    wait_up = fetch(near_1, wu_m, wu_o, wu, sems.at[0])
    wait_down = fetch(near_1, wd_m, wd_o, wd, sems.at[1])
    wait_pos()
    wait_qkv()
    normed, _ = normalize(sum_two)
    result = (normed * small_0[4:5] + small_0[5:6]).astype(BF16)
    position = pos[...].astype(F32)
    for w in range(2):
        rows = window_rows(w)
        stream_1[w] = result[rows]
        hidden[rows, :] = result[rows].astype(F32) + position
    project_rows(hidden[...].astype(BF16), wq, project_1)
    attend(mask, project_1, probs_1, mixed_1)
    wait_out()
    wait_up()
    wait_down()
    wait_cotangent()
    sum_one = hidden[...] + nn(mixed_1[...], wo[...])
    sum_one_1[...] = sum_one
    sum_two = feed(small_1, sum_one, wu, wd, acc, low_1, active_1, slope_1)
    normed, _ = normalize(sum_two)
    result = normed * small_1[4:5] + small_1[5:6]
    upstream = []
    for w in range(2):
        output[w] = unused_zeroed(place_ref, w, result[window_rows(w)]).astype(BF16)
        upstream.append(unused_zeroed(place_ref, w, arriving[w].astype(F32)))
    e = jnp.concatenate(upstream, 0)
    feed_back(
        sec, small_1, e, sum_two, wu, wd, acc, low_1, active_1, slope_1, small_grads, grads, send
    )
    grad_after[...] = acc[...]


def forward_middle(place, cotangent, mine, other, sum_one):
    args = [place, cotangent]
    for a, b in zip(mine, other):
        args += [a, b]
    return pl.pallas_call(
        middle_kernel,
        out_shape=FEED_KEPT
        + [sds((2, WIN, D), BF16)]
        + ATTENTION_KEPT
        + [sds((2, WIN, D), BF16)]
        + FFN_GRADS,
        in_specs=[SM] + [HBM] * 11 + [VM] * 3,
        out_specs=[VM] * 14,
        scratch_shapes=[
            pltpu.VMEM((2, WIN, D), BF16),
            pltpu.VMEM((WIN, D), BF16),
            pltpu.VMEM((D, 3 * D), BF16),
            pltpu.VMEM((D, D), BF16),
            pltpu.VMEM((D, FF), BF16),
            pltpu.VMEM((FF, D), BF16),
            pltpu.VMEM((ROWS, D), F32),
            pltpu.VMEM((2, WIN, WIN), F32),
            pltpu.VMEM((ROWS, D), F32),
            pltpu.VMEM((ROWS, D), BF16),
            pltpu.VMEM((ROWS, FF), BF16),
            pltpu.VMEM((ROWS, FF), BF16),
            DMA((6,)),
        ],
        compiler_params=limit(MIDDLE_LIMIT),
        cost_estimate=HEAVY,
        name="feed_0_to_feed_backward_1",
    )(*args, sum_one)


MIDDLE_LIMIT = 32


def out_kernel(
    layer,
    place_ref,
    wo_m,
    wo_o,
    vec_m,
    vec_o,
    grad_after,
    sum_one,
    mixed,
    small_in,
    grad_sum_ref,
    grad_mixed,
    grad_out,
    rows_ref,
    wo,
    sem,
):
    near = place_ref[0] == layer
    wait_out = fetch(near, wo_m, wo_o, wo, sem)
    small = chosen(near, vec_m, vec_o)
    normed, inverse = normalize(sum_one[...] + small[0:1])
    e = grad_after[...]
    row_norm = jnp.sum(e * normed, 0, keepdims=True)
    row_shift = jnp.sum(e, 0, keepdims=True)
    grad_sum = norm_backward(e, normed, inverse, small[1:2])
    grad_sum_ref[...] = grad_sum
    branch = grad_sum.astype(BF16)
    row_out = jnp.sum(branch.astype(F32), 0, keepdims=True)
    rows = jnp.concatenate([row_out, row_norm, row_shift, jnp.zeros((5, D), F32)], 0)
    rows_ref[...] = jnp.concatenate([rows, small_in[...]], 0).astype(BF16)
    wait_out()
    grad_mixed[...] = nt(branch, wo[...]).astype(BF16)
    grad_out[...] = tn(mixed[...], branch).astype(BF16)


def out_back(layer, place, mine, other, grad_after, kept, small):
    def body(*refs):
        out_kernel(layer, *refs)

    return pl.pallas_call(
        body,
        out_shape=[
            sds((ROWS, D), F32),
            sds((ROWS, D), BF16),
            sds((D, D), BF16),
            sds((16, D), BF16),
        ],
        in_specs=[SM] + [HBM] * 2 + [VM] * 6,
        out_specs=[VM] * 4,
        scratch_shapes=[pltpu.VMEM((D, D), BF16), DMA],
        compiler_params=limit(16),
        cost_estimate=HEAVY,
        name=f"projection_backward_{layer}",
    )(place, mine[2], other[2], mine[5], other[5], grad_after, kept[3], kept[2], small)


def late_kernel(
    place_ref,
    pos_m,
    pos_o,
    wq_m,
    wq_o,
    wu_m,
    wu_o,
    wd_m,
    wd_o,
    vec_m,
    vec_o,
    stream_1,
    project_1,
    probs_1,
    grad_sum,
    grad_mixed,
    grad_out,
    rows_1,
    low_0,
    active_0,
    slope_0,
    sum_two_0,
    att_grads,
    att_send,
    grad_after,
    small_grads,
    ffn_grads,
    ffn_send,
    pos,
    wq,
    wu,
    wd,
    grad_project,
    total,
    sems,
):
    sec = place_ref[0]
    wait_qkv = fetch(sec == 1, wq_m, wq_o, wq, sems.at[0])
    wait_pos = fetch(sec == 1, pos_m, pos_o, pos, sems.at[1])
    wait_down = fetch(sec == 0, wd_m, wd_o, wd, sems.at[2])
    wait_up = fetch(sec == 0, wu_m, wu_o, wu, sems.at[3])
    small = chosen(sec == 0, vec_m, vec_o)
    attend_back(project_1, probs_1, grad_mixed, grad_project)
    wait_qkv()
    wait_pos()
    wait_down()
    wait_up()
    input_back(
        sec, stream_1, pos, wq, grad_sum, grad_out, rows_1, grad_project, total, att_grads, att_send
    )
    e = total[...].astype(BF16).astype(F32)
    feed_back(
        sec,
        small,
        e,
        sum_two_0[...],
        wu,
        wd,
        total,
        low_0,
        active_0,
        slope_0,
        small_grads,
        ffn_grads,
        ffn_send,
    )
    grad_after[...] = total[...]


def late_back(place, mine, other, stream, attention, before, feed_kept):
    args = [place]
    for i in (0, 1, 3, 4, 5):
        args += [mine[i], other[i]]
    return pl.pallas_call(
        late_kernel,
        out_shape=ATT_GRADS + FFN_GRADS,
        in_specs=[SM] + [HBM] * 8 + [VM] * 13,
        out_specs=[VM] * 6,
        scratch_shapes=[
            pltpu.VMEM((WIN, D), BF16),
            pltpu.VMEM((D, 3 * D), BF16),
            pltpu.VMEM((D, FF), BF16),
            pltpu.VMEM((FF, D), BF16),
            pltpu.VMEM((ROWS, 3 * D), BF16),
            pltpu.VMEM((ROWS, D), F32),
            DMA((4,)),
        ],
        compiler_params=limit(24),
        cost_estimate=HEAVY,
        name="attention_backward_1_and_feed_backward_0",
    )(*args, stream, attention[0], attention[1], *before, *feed_kept)


def last_kernel(
    place_ref,
    tokens,
    pos_m,
    pos_o,
    wq_m,
    wq_o,
    project,
    probs,
    grad_sum,
    grad_mixed,
    grad_out,
    rows,
    grad_low,
    grads,
    send,
    stream,
    pos,
    wq,
    grad_project,
    total,
    sems,
):
    sec = place_ref[0]
    wait_qkv = fetch(sec == 0, wq_m, wq_o, wq, sems.at[0])
    wait_pos = fetch(sec == 0, pos_m, pos_o, pos, sems.at[1])
    wait_stream = copy(tokens.at[sec], stream, sems.at[2])
    attend_back(project, probs, grad_mixed, grad_project)
    wait_qkv()
    wait_pos()
    wait_stream()
    input_back(
        sec, stream, pos, wq, grad_sum, grad_out, rows, grad_project, total, grads, send
    )
    for w in range(2):
        grad_low[w] = total[window_rows(w), :].astype(BF16)


def last_back(place, tokens, mine, other, attention, before):
    args = [place, tokens]
    for i in (0, 1):
        args += [mine[i], other[i]]
    return pl.pallas_call(
        last_kernel,
        out_shape=[sds((2, WIN, D), BF16)] + ATT_GRADS,
        in_specs=[SM] + [HBM] * 5 + [VM] * 6,
        out_specs=[VM] * 3,
        scratch_shapes=[
            pltpu.VMEM((2, WIN, D), BF16),
            pltpu.VMEM((WIN, D), BF16),
            pltpu.VMEM((D, 3 * D), BF16),
            pltpu.VMEM((ROWS, 3 * D), BF16),
            pltpu.VMEM((ROWS, D), F32),
            DMA((3,)),
        ],
        compiler_params=limit(20),
        cost_estimate=HEAVY,
        name="attention_backward_0",
    )(*args, attention[0], attention[1], *before)


def pack_vectors(b_out, gain_one, shift_one, b_down, gain_two, shift_two, b_up):
    def body(*refs):
        out = refs[-1]
        rows = [ref[...].astype(F32) for ref in refs[:6]]
        wide = refs[6][...].astype(F32)
        rows += [wide[:, c * D : (c + 1) * D] for c in range(4)]
        rows += [jnp.zeros((6, D), F32)]
        out[...] = jnp.concatenate(rows, 0).astype(BF16)

    return pl.pallas_call(
        body,
        out_shape=sds((16, D), BF16),
        in_specs=[VM] * 7,
        out_specs=VM,
        name="pack_vectors",
    )(b_out, gain_one, shift_one, b_down, gain_two, shift_two, b_up)


def plain(body, shapes, args, name, specs=None):
    return pl.pallas_call(
        body,
        out_shape=[sds(shape, BF16) for shape in shapes],
        in_specs=specs or [VM] * len(args),
        out_specs=[VM] * len(shapes),
        compiler_params=limit(24),
        cost_estimate=SLIGHT,
        name=name,
    )(*args)


def stage_order(place_ref):
    first = place_ref[0] == 0
    strides = [jnp.where(first, a, b) for a, b in zip(*WAY)]
    coords = [lax.rem(lax.div(place_ref[1], stride), 4) for stride in strides]

    def owner(*distances):
        return sum(
            lax.rem(coord + r, 4) * stride
            for coord, r, stride in zip(coords, distances, strides)
        )

    return owner


def pair_sum(place, *arrays):
    ranges = []
    for i in range(len(arrays) // 2):
        if arrays[2 * i + 1].shape[0] == 8192:
            ranges += [(i, 0, FFN_PART)]
        else:
            ranges += [(i, 0, 64), (i, EXTRA, 16)]
    part = sum(rows for _, _, rows in ranges)

    def body(place_ref, *refs):
        outs = refs[len(arrays) :]
        owner = stage_order(place_ref)
        sec = place_ref[0]
        for third in range(4):
            for second in range(4):
                for first in range(4):
                    dev = owner(first, second, third)
                    at = (second * 4 + first) * part
                    for i, base, rows in ranges:
                        src = pl.ds(pl.multiple_of(base + dev * rows, 16), rows)
                        total = refs[2 * i][sec, src, :].astype(F32)
                        total += refs[2 * i + 1][src, :].astype(F32)
                        outs[third][at : at + rows, :] = total.astype(BF16)
                        at += rows

    specs = [SM] + [VM] * len(arrays)
    return plain(body, [(16 * part, 128)] * 4, (place,) + arrays, "sum_of_two_cores", specs)


def add_four(refs, at):
    return sum(ref[at].astype(F32) for ref in refs)


def line_sum(*arrivals):
    rows = arrivals[0][0].shape[0] // 16
    count = len(arrivals)

    def body(*refs):
        outs = refs[4 * count :]
        for r in range(4):
            for first in range(4):
                at = (r * 4 + first) * rows
                for i in range(count):
                    total = add_four(refs[4 * i : 4 * i + 4], (slice(at, at + rows), slice(None)))
                    outs[r][first, i] = total.astype(BF16)

    args = sum(arrivals, [])
    return plain(body, [(4, count, rows, 128)] * 4, args, "sum_over_line")


def early_line_sum(late_ffn, mixed):
    def body(*refs):
        outs = refs[8:]
        for r in range(4):
            for first in range(4):
                i = r * 4 + first
                at = slice(i * FFN_PART, (i + 1) * FFN_PART)
                total = add_four(refs[0:4], (at, slice(None)))
                outs[r][first, 0:FFN_PART, :] = total.astype(BF16)
                at = slice(i * CHUNK, (i + 1) * CHUNK)
                total = add_four(refs[4:8], (at, slice(None)))
                outs[r][first, FFN_PART:, :] = total.astype(BF16)

    return plain(
        body, [(4, FFN_PART + CHUNK, 128)] * 4, late_ffn + mixed, "sum_over_line_early"
    )


def plane_sum(early, last):
    def body(*refs):
        outs = refs[8:]
        for first in range(4):
            total = add_four(refs[0:4], first).astype(BF16)
            outs[first][1, 0:FFN_PART, :] = total[0:FFN_PART]
            outs[first][0, 0:FFN_PART, :] = total[FFN_PART : 2 * FFN_PART]
            outs[first][1, FFN_PART:, :] = total[2 * FFN_PART :]
            outs[first][0, FFN_PART:, :] = add_four(refs[4:8], (first, 0)).astype(BF16)

    return plain(body, [(2, CHUNK, 128)] * 4, early + last, "sum_over_plane")


def cube_sum(place, pieces):
    def body(place_ref, *refs):
        sec = place_ref[0]
        refs[4][...] = add_four(refs[:4], sec).astype(BF16)
        refs[5][...] = add_four(refs[:4], 1 - sec).astype(BF16)

    specs = [SM] + [VM] * 4
    return plain(body, [(CHUNK, 128)] * 2, [place] + pieces, "sum_over_cube", specs)


def place_parts(place_ref, sources, targets, pos, small, ready, sems):
    wu_ref, wd_ref, wq_ref, wo_ref = targets
    sec = place_ref[0]
    owner = stage_order(place_ref)
    waits = []
    for n, (ref, third, second) in enumerate(sources):
        for step in range(8):
            dev = owner(step % 4, second + step // 4, third)
            slot = n * 8 + step

            def write(kind, rows, base, half, n=n, step=step, slot=slot, ref=ref):
                side = sec if half == 0 else 1 - sec
                ready[kind][slot] = ref[step, side, base : base + rows, :].astype(F32)
                return ready[kind].at[slot]

            def send(kind, src, dst, slot=slot):
                return pltpu.make_async_copy(src, dst, sems.at[kind, slot])

            def lanes(start):
                return pl.ds(pl.multiple_of(start * 128, 128), 128)

            block = lax.div(dev, 4)
            r = pl.multiple_of(lax.rem(dev, 4) * 128, 128)
            up = send(
                0, write(0, FFN_PART, 0, 0), wu_ref.at[0, pl.ds(r, FFN_PART), lanes(block)]
            )
            up.start()
            r = pl.multiple_of(lax.div(block, 4) * D + r, 128)
            down = send(
                1,
                write(1, FFN_PART, 0, 1),
                wd_ref.at[0, pl.ds(r, FFN_PART), lanes(lax.rem(block, 4))],
            )
            down.start()
            block = lax.div(dev, 8)
            rows = pl.ds(pl.multiple_of(lax.rem(dev, 8) * 64, 64), 64)
            first = send(2, write(2, 64, FFN_PART, 0), wq_ref.at[0, rows, lanes(block)])
            first.start()
            src = write(3, 64, FFN_PART, 1)

            @pl.when(block < 4)
            def _(src=src, rows=rows, block=block, send=send, lanes=lanes):
                send(3, src, wq_ref.at[0, rows, lanes(block + 8)]).start()

            @pl.when(block >= 4)
            def _(src=src, rows=rows, block=block, send=send, lanes=lanes):
                send(3, src, wo_ref.at[0, rows, lanes(block - 4)]).start()

            waits += [up, down, first, send(3, src, wq_ref.at[0, rows, lanes(block)])]
            for half in range(2):
                side = sec if half == 0 else 1 - sec
                extra = ref[step, side, FFN_PART + 64 : CHUNK, :].astype(F32)
                at = pl.multiple_of(half * 128 + lax.rem(dev, 16) * 8, 8)
                pos[pl.ds(at, 8), lanes(lax.div(dev, 16))] = extra[0:8]
                if half == 0:
                    small[pl.ds(pl.multiple_of(dev * 8, 8), 8), :] = extra[8:16]
    for copy_out in waits:
        copy_out.wait()


WEIGHT_GRADS = [
    sds((1, D, FF), F32),
    sds((1, FF, D), F32),
    sds((1, D, 3 * D), F32),
    sds((1, D, D), F32),
]
PLACED = [sds((WIN, D), F32), sds((64 * 8, 128), F32)]
READY = [
    pltpu.VMEM((32, FFN_PART, 128), F32),
    pltpu.VMEM((32, FFN_PART, 128), F32),
    pltpu.VMEM((32, 64, 128), F32),
    pltpu.VMEM((32, 64, 128), F32),
    DMA((4, 32)),
]


def place_early(place, own_a, own_b, next_a, prev_b):
    def body(place_ref, own_a, own_b, next_a, prev_b, *refs):
        targets, (pos, small), ready, sems = refs[:4], refs[4:6], refs[6:10], refs[10]
        sources = [(own_a, 0, 0), (own_b, 0, 2), (next_a, 1, 0), (prev_b, 3, 2)]
        place_parts(place_ref, sources, targets, pos, small, ready, sems)

    return pl.pallas_call(
        body,
        out_shape=WEIGHT_GRADS + PLACED,
        in_specs=[SM] + [VM] * 4,
        out_specs=[HBM] * 4 + [VM] * 2,
        scratch_shapes=READY,
        compiler_params=limit(16),
        cost_estimate=HEAVY,
        name="place_gradients_early",
    )(place, own_a, own_b, next_a, prev_b)


def place_late(place, next_b, prev_a, far_a, far_b, placed):
    def body(place_ref, next_b, prev_a, far_a, far_b, *refs):
        pos_in, small_in = refs[4:6]
        targets, (pos, bo, g1, s1, bu, bd, g2, s2) = refs[6:10], refs[10:18]
        small, ready, sems = refs[18], refs[19:23], refs[23]
        pos[0] = pos_in[...]
        small[...] = small_in[...]
        sources = [(next_b, 1, 2), (prev_a, 3, 0), (far_a, 2, 0), (far_b, 2, 2)]
        place_parts(place_ref, sources, targets, pos.at[0], small, ready, sems)
        for c in range(4):
            lane = slice(c * 128, (c + 1) * 128)
            at = c * 16
            for ref, row in ((bo, 0), (g1, 1), (s1, 2), (bd, 8), (g2, 9), (s2, 10)):
                ref[:, lane] = small[at + row : at + row + 1, :]
            for j in range(4):
                row = at + 11 + j
                bu[:, j * D + c * 128 : j * D + (c + 1) * 128] = small[row : row + 1, :]

    vector = sds((1, D), F32)
    return pl.pallas_call(
        body,
        out_shape=WEIGHT_GRADS
        + [sds((1, WIN, D), F32), vector, vector, vector, sds((1, FF), F32)]
        + [vector] * 3,
        in_specs=[SM] + [VM] * 4 + [HBM] * 4 + [VM] * 2,
        out_specs=[HBM] * 4 + [VM] * 8,
        scratch_shapes=[pltpu.VMEM((64 * 8, 128), F32)] + READY,
        input_output_aliases={5: 0, 6: 1, 7: 2, 8: 3},
        compiler_params=limit(16),
        cost_estimate=HEAVY,
        name="place_gradients_late",
    )(place, next_b, prev_a, far_a, far_b, *placed)


def swap(value):
    return lax.ppermute(value, "section", [(0, 1), (1, 0)])


def from_ahead(value, stage, distance):
    pairs = []
    for section in range(2):
        stride = WAY[section][stage]
        for dst in range(64):
            at = dst // stride % 4
            src = dst + ((at + distance) % 4 - at) * stride
            pairs.append((section * 64 + src, section * 64 + dst))
    return lax.ppermute(value, ("section", "dp"), pairs)


def send_ahead(pieces, stage):
    return [pieces[0]] + [from_ahead(pieces[r], stage, 4 - r) for r in (1, 3, 2)]


def gather(chunk):
    line = jnp.stack([chunk] + [from_ahead(chunk, 0, r) for r in (1, 2, 3)])
    ahead = [from_ahead(line, 1, r) for r in (1, 2, 3)]
    own_a = jnp.concatenate([line, ahead[0]], 0)
    own_b = jnp.concatenate([ahead[1], ahead[2]], 0)
    next_a = from_ahead(own_a, 2, 1)
    prev_b = from_ahead(own_b, 2, 3)
    next_b = from_ahead(own_b, 2, 1)
    prev_a = from_ahead(own_a, 2, 3)
    far_a = from_ahead(next_a, 2, 1)
    far_b = from_ahead(prev_b, 2, 3)
    return own_a, own_b, next_a, next_b, far_a, far_b, prev_a, prev_b


def hold(*values):
    return tuple(pltpu.with_memory_space_constraint(value, pltpu.HBM) for value in values)


def shards(
    tokens,
    lengths,
    out_cotangent,
    pos_table,
    w_qkv,
    w_out,
    b_out,
    norm1_gain,
    norm1_bias,
    w_up,
    b_up,
    w_down,
    b_down,
    norm2_gain,
    norm2_bias,
):
    section = lax.axis_index("section")
    place = jnp.stack([section, lax.axis_index("dp")]).astype(jnp.int32)
    place = jnp.concatenate([place, lengths.reshape(4)])
    vec = pack_vectors(b_out, norm1_gain, norm1_bias, b_down, norm2_gain, norm2_bias, b_up)
    got_qkv = swap(w_qkv)
    got_pos = swap(pos_table)
    got_out = swap(w_out)
    late_up, late_down, got_qkv = lax.optimization_barrier((w_up, w_down, got_qkv))
    mine = hold(pos_table, w_qkv, w_out, w_up, w_down) + (vec,)
    other = hold(got_pos, got_qkv, got_out, swap(late_up), swap(late_down)) + (swap(vec),)
    tokens, out_cotangent = hold(tokens, out_cotangent)
    attention_0 = forward_first(place, tokens, mine, other)
    middle = forward_middle(place, out_cotangent, mine, other, attention_0[3])
    feed_0, stream, attention_1, output = middle[0:4], middle[4], middle[5:9], middle[9]
    after, small, ffn_both, ffn_send = middle[10:14]

    def tie(*values):
        return lax.optimization_barrier(values)

    ffn_got = swap(ffn_send)
    before = out_back(1, place, mine, other, after, attention_1, small)
    pieces = pair_sum(place, ffn_both, ffn_got)
    before, pieces = tie(before, pieces)
    late_ffn = send_ahead(pieces, 2)
    att_both, att_send, after, small, ffn_both, ffn_send = late_back(
        place, mine, other, stream, attention_1, before, feed_0
    )
    after, late_ffn = tie(after, late_ffn)
    att_got = swap(att_send)
    ffn_got = swap(ffn_send)
    before = out_back(0, place, mine, other, after, attention_0, small)
    pieces = pair_sum(place, ffn_both, ffn_got, att_both, att_got)
    before, pieces = tie(before, pieces)
    mixed = send_ahead(pieces, 2)
    arriving, att_both, att_send = last_back(place, tokens, mine, other, attention_0, before)
    att_send, mixed = tie(att_send, mixed)
    pieces = pair_sum(place, att_both, swap(att_send))
    early = send_ahead(early_line_sum(late_ffn, mixed), 1)
    last = send_ahead(line_sum(send_ahead(pieces, 2)), 1)
    pieces = plane_sum(early, last)
    own, others = cube_sum(place, send_ahead(pieces, 0))
    chunk = jnp.stack([own, swap(others)])
    own_a, own_b, next_a, next_b, far_a, far_b, prev_a, prev_b = gather(chunk)
    placed = place_early(place, own_a, own_b, next_a, prev_b)
    up, down, qkv, out, position, bias, gain_one, shift_one, bias_up, bias_down, gain_two, shift_two = (
        place_late(place, next_b, prev_a, far_a, far_b, placed)
    )
    return (
        output[None],
        arriving[None],
        position,
        qkv,
        out,
        bias,
        gain_one,
        shift_one,
        up,
        bias_up,
        down,
        bias_down,
        gain_two,
        shift_two,
    )


def solution(mesh):
    placed = (
        P(None, "dp", None, None),
        P(None, "dp"),
        P(None, "dp", None, None),
        P("section", None, None),
        P("section", None, None),
        P("section", None, None),
        P("section", None),
        P("section", None),
        P("section", None),
        P("section", None, None),
        P("section", None),
        P("section", None, None),
        P("section", None),
        P("section", None),
        P("section", None),
    )
    return jax.shard_map(
        shards,
        mesh=mesh,
        in_specs=placed,
        out_specs=(
            P("section", "dp", None, None),
            P("section", "dp", None, None),
            P("section", None, None),
            P("section", None, None),
            P("section", None, None),
            P("section", None),
            P("section", None),
            P("section", None),
            P("section", None, None),
            P("section", None),
            P("section", None, None),
            P("section", None),
            P("section", None),
            P("section", None),
        ),
        check_vma=False,
    )
```

```python
import jax
import jax.numpy as jnp
from jax import lax
from jax.experimental import pallas as pl
from jax.experimental.pallas import tpu as pltpu
from jax.sharding import PartitionSpec as P

D = 512
FF = 2048
WIN = 256
ROWS = 512
F32 = jnp.float32
BF16 = jnp.bfloat16

HBM = pl.BlockSpec(memory_space=pltpu.HBM)
ANY = pl.BlockSpec(memory_space=pl.ANY)
VM = pl.BlockSpec(memory_space=pltpu.VMEM)
SM = pl.BlockSpec(memory_space=pltpu.SMEM)
DMA = pltpu.SemaphoreType.DMA
SLIGHT = pl.CostEstimate(flops=1000, bytes_accessed=1000, transcendentals=0)
HEAVY = pl.CostEstimate(flops=35_000_000_000, bytes_accessed=1000, transcendentals=0)
EXTRA = 4096
FFN_PART = 128
ATT_PART = 80
CHUNK = FFN_PART + ATT_PART
WAY = ((16, 4, 1), (1, 16, 4))


def limit(mebibytes):
    return pltpu.CompilerParams(vmem_limit_bytes=mebibytes * 1024 * 1024)


def sds(shape, dtype):
    return jax.ShapeDtypeStruct(shape, dtype)


def nn(a, b):
    return lax.dot_general(a, b, (((1,), (0,)), ((), ())), preferred_element_type=F32)


def nt(a, b):
    return lax.dot_general(a, b, (((1,), (1,)), ((), ())), preferred_element_type=F32)


def tn(a, b):
    return lax.dot_general(a, b, (((0,), (0,)), ((), ())), preferred_element_type=F32)


def fetch(near, mine, other, dst, sem):
    @pl.when(near)
    def _():
        pltpu.make_async_copy(mine.at[0], dst, sem).start()

    @pl.when(jnp.logical_not(near))
    def _():
        pltpu.make_async_copy(other.at[0], dst, sem).start()

    return pltpu.make_async_copy(mine.at[0], dst, sem).wait


def copy(src, dst, sem):
    load = pltpu.make_async_copy(src, dst, sem)
    load.start()
    return load.wait


def chosen(near, mine, other):
    return jnp.where(near, mine[...].astype(F32), other[...].astype(F32))


def normalize(v):
    center = v - jnp.mean(v, -1, keepdims=True)
    inverse = lax.rsqrt(jnp.mean(center * center, -1, keepdims=True) + 1e-05)
    return center * inverse, inverse


def norm_backward(e, normed, inverse, gain):
    scaled = e * gain
    return inverse * (
        scaled
        - jnp.mean(scaled, -1, keepdims=True)
        - normed * jnp.mean(scaled * normed, -1, keepdims=True)
    )


def gelu_pair(v):
    c = 0.7978845608028654
    sq = v * v
    t = jnp.tanh(v * (c + (c * 0.044715) * sq))
    half = 0.5 + 0.5 * t
    slope = half + (0.5 * v) * (1.0 - t * t) * (c + (3.0 * c * 0.044715) * sq)
    return v * half, slope


def used(place_ref, window):
    return place_ref[2 + 2 * place_ref[0] + window]


def write_mask(place_ref, mask):
    rows = lax.broadcasted_iota(jnp.int32, (WIN, WIN), 0)
    cols = lax.broadcasted_iota(jnp.int32, (WIN, WIN), 1)
    for w in range(2):
        inside = (cols <= rows) & (cols < used(place_ref, w))
        mask[w] = jnp.where(inside, 0.0, -1e30)


def window_rows(w):
    return slice(w * WIN, (w + 1) * WIN)


def unused_zeroed(place_ref, w, part):
    at_row = lax.broadcasted_iota(jnp.int32, (WIN, D), 0)
    return jnp.where(at_row < used(place_ref, w), part, 0.0)


def project_rows(hidden_low, wq, project):
    for c in range(3):
        at = slice(c * D, (c + 1) * D)
        project[:, at] = nn(hidden_low, wq[:, at]).astype(BF16)


def attend(mask, project, probs, mixed):
    lanes = lax.broadcasted_iota(jnp.int32, (WIN, 128), 1)
    for step in range(8):
        w, p = step // 4, step % 4
        rows = window_rows(w)
        at = [slice(j * D + p * 128, j * D + (p + 1) * 128) for j in range(3)]
        q2 = project[rows, at[0]] * jnp.asarray(0.125, BF16)
        k2 = project[rows, at[1]]
        v2 = project[rows, at[2]]
        blocked = mask[w]
        parts = []
        for h in range(2):
            own = (lanes >= 64) if h else (lanes < 64)
            qm = jnp.where(own, q2, jnp.zeros_like(q2))
            scores = nt(qm, k2) + blocked
            raised = jnp.exp(scores - jnp.max(scores, -1, keepdims=True))
            soft = (raised * (1.0 / jnp.sum(raised, -1, keepdims=True))).astype(BF16)
            probs[step * 2 + h] = soft
            parts.append(nn(soft, v2))
        mixed[rows, at[0]] = jnp.where(lanes < 64, parts[0], parts[1]).astype(BF16)


def attend_back(project, probs, grad_mixed, grad_project):
    lanes = lax.broadcasted_iota(jnp.int32, (WIN, 128), 1)
    for step in range(8):
        w, p = step // 4, step % 4
        rows = window_rows(w)
        at = [slice(j * D + p * 128, j * D + (p + 1) * 128) for j in range(3)]
        q2 = project[rows, at[0]] * jnp.asarray(0.125, BF16)
        k2 = project[rows, at[1]]
        v2 = project[rows, at[2]]
        g2 = grad_mixed[rows, at[0]]
        grad_q, grad_k, grad_v = [], [], []
        for h in range(2):
            own = (lanes >= 64) if h else (lanes < 64)
            none = jnp.zeros_like(q2)
            gm = jnp.where(own, g2, none)
            qm = jnp.where(own, q2, none)
            soft_low = probs[step * 2 + h]
            soft = soft_low.astype(F32)
            product = soft * nt(gm, v2)
            grad_scores = (product - soft * jnp.sum(product, -1, keepdims=True)).astype(BF16)
            grad_q.append(nn(grad_scores, k2))
            grad_k.append(tn(grad_scores, qm))
            grad_v.append(tn(soft_low, gm))
        grad_project[rows, at[0]] = (
            jnp.where(lanes < 64, grad_q[0], grad_q[1]) * 0.125
        ).astype(BF16)
        grad_project[rows, at[1]] = (grad_k[0] + grad_k[1]).astype(BF16)
        grad_project[rows, at[2]] = (grad_v[0] + grad_v[1]).astype(BF16)


def feed(small, sum_one, wu, wd, acc, low_ref, active_ref, slope_ref, wait_up, wait_down):
    normed, _ = normalize(sum_one + small[0:1])
    after = normed * small[1:2] + small[2:3]
    acc[...] = after
    low = after.astype(BF16)
    low_ref[...] = low
    wait_up()
    for c in range(4):
        block = slice(c * D, (c + 1) * D)
        value = nn(low, wu[:, block]) + small[6 + c : 7 + c]
        active, slope = gelu_pair(value)
        active = active.astype(BF16)
        active_ref[:, block] = active
        slope_ref[:, block] = slope.astype(BF16)
    wait_down()
    return acc[...] + (nn(active_ref[...], wd[...]) + small[3:4])


def feed_back(
    sec, small, e, sum_two, wu, wd, acc, low_ref, active_ref, slope_ref, small_ref, grads, send
):
    normed, inverse = normalize(sum_two)
    small_ref[...] = jnp.zeros_like(small_ref)
    small_ref[1:2, :] = jnp.sum(e * normed, 0, keepdims=True)
    small_ref[2:3, :] = jnp.sum(e, 0, keepdims=True)
    grad_sum = norm_backward(e, normed, inverse, small[4:5])
    acc[...] = grad_sum
    grad_low = grad_sum.astype(BF16)
    small_ref[0:1, :] = jnp.sum(grad_low.astype(F32), 0, keepdims=True)
    for c in range(4):
        block = slice(c * D, (c + 1) * D)
        grad_up = nt(grad_low, wd[block, :]) * slope_ref[:, block].astype(F32)
        grad_up = grad_up.astype(BF16)
        small_ref[3 + c : 4 + c, :] = jnp.sum(grad_up.astype(F32), 0, keepdims=True)
        slope_ref[:, block] = grad_up
        grad_wu = tn(low_ref[...], grad_up).astype(BF16)
        grad_wd = tn(active_ref[:, block], grad_low).astype(BF16)
        for k in range(4):
            at = slice((c * 4 + k) * D, (c * 4 + k + 1) * D)
            grads[0, at, :] = grad_wu[:, k * 128 : (k + 1) * 128]
            grads[1, at, :] = grad_wd[:, k * 128 : (k + 1) * 128]
    acc[...] += nt(slope_ref[...], wu[...])
    send[...] = grads[1 - sec]


def input_back(
    sec, stream, pos, wq, grad_sum, grad_out, rows, grad_project, total, grads, send
):
    for c in range(4):
        grads[1, 2048 + c * D : 2048 + (c + 1) * D, :] = grad_out[:, c * 128 : (c + 1) * 128]
    position = pos[...].astype(F32)
    hidden_low = jnp.concatenate(
        [(stream[w].astype(F32) + position).astype(BF16) for w in range(2)], 0
    )
    total[...] = grad_sum[...]
    for j in range(3):
        block = slice(j * D, (j + 1) * D)
        part = grad_project[:, block]
        total[...] += nt(part, wq[:, block])
        grad_w = tn(hidden_low, part).astype(BF16)
        half, base = ((0, 0), (0, 2048), (1, 0))[j]
        for c in range(4):
            grads[half, base + c * D : base + (c + 1) * D, :] = grad_w[:, c * 128 : (c + 1) * 128]
    grad_pos = total[0:WIN, :] + total[WIN : 2 * WIN, :]
    small = rows[...].astype(F32)
    blank = jnp.zeros((8, 128), F32)
    for c in range(4):
        lanes_at = slice(c * 128, (c + 1) * 128)
        for half in range(2):
            extra = []
            for i in range(16):
                at = half * 128 + i * 8
                extra.append(grad_pos[at : at + 8, lanes_at])
                if c == 0 and i < 8:
                    extra.append(small[i % 2 * 8 : i % 2 * 8 + 8, i // 2 * 128 : i // 2 * 128 + 128])
                else:
                    extra.append(blank)
            at = EXTRA + c * WIN
            grads[half, at : at + WIN, :] = jnp.concatenate(extra, 0).astype(BF16)
    send[...] = grads[1 - sec]


def first_kernel(
    place_ref,
    tokens,
    pos_m,
    pos_o,
    wq_m,
    wq_o,
    wo_m,
    wo_o,
    project,
    probs,
    mixed,
    sum_one,
    stream,
    pos,
    wq,
    wo,
    hidden,
    mask,
    sems,
):
    sec = place_ref[0]
    wait_stream = copy(tokens.at[sec], stream, sems.at[0])
    wait_pos = fetch(sec == 0, pos_m, pos_o, pos, sems.at[1])
    wait_qkv = fetch(sec == 0, wq_m, wq_o, wq, sems.at[2])
    wait_out = fetch(sec == 0, wo_m, wo_o, wo, sems.at[3])
    write_mask(place_ref, mask)
    wait_stream()
    wait_pos()
    position = pos[...].astype(F32)
    for w in range(2):
        hidden[window_rows(w), :] = stream[w].astype(F32) + position
    wait_qkv()
    wait_out()
    project_rows(hidden[...].astype(BF16), wq, project)
    attend(mask, project, probs, mixed)
    sum_one[...] = hidden[...] + nn(mixed[...], wo[...])


ATTENTION_KEPT = [
    sds((ROWS, 3 * D), BF16),
    sds((16, WIN, WIN), BF16),
    sds((ROWS, D), BF16),
    sds((ROWS, D), F32),
]
FEED_KEPT = [
    sds((ROWS, D), BF16),
    sds((ROWS, FF), BF16),
    sds((ROWS, FF), BF16),
    sds((ROWS, D), F32),
]
FFN_GRADS = [
    sds((ROWS, D), F32),
    sds((8, D), F32),
    sds((2, 8192, 128), BF16),
    sds((8192, 128), BF16),
]
ATT_GRADS = [sds((2, 5120, 128), BF16), sds((5120, 128), BF16)]


def forward_first(place, tokens, mine, other):
    args = [place, tokens]
    for i in (0, 1, 2):
        args += [mine[i], other[i]]
    return pl.pallas_call(
        first_kernel,
        out_shape=ATTENTION_KEPT,
        in_specs=[SM, HBM] + [HBM, ANY] * 3,
        out_specs=[VM] * 4,
        scratch_shapes=[
            pltpu.VMEM((2, WIN, D), BF16),
            pltpu.VMEM((WIN, D), BF16),
            pltpu.VMEM((D, 3 * D), BF16),
            pltpu.VMEM((D, D), BF16),
            pltpu.VMEM((ROWS, D), F32),
            pltpu.VMEM((2, WIN, WIN), F32),
            DMA((4,)),
        ],
        compiler_params=limit(12),
        cost_estimate=HEAVY,
        name="forward_attention_0",
    )(*args)


def middle_kernel(
    place_ref,
    cotangent,
    pos_m,
    pos_o,
    wq_m,
    wq_o,
    wo_m,
    wo_o,
    wu_m,
    wu_o,
    wd_m,
    wd_o,
    vec_m,
    vec_o,
    sum_one_0,
    low_0,
    active_0,
    slope_0,
    sum_two_0,
    stream_1,
    project_1,
    probs_1,
    mixed_1,
    sum_one_1,
    output,
    grad_after,
    small_grads,
    grads,
    send,
    arriving,
    pos,
    wq,
    wo,
    wu,
    wd,
    hidden,
    mask,
    acc,
    low_1,
    active_1,
    slope_1,
    sems,
):
    sec = place_ref[0]
    near_0 = sec == 0
    near_1 = sec == 1
    wait_up = fetch(near_0, wu_m, wu_o, wu, sems.at[0])
    wait_down = fetch(near_0, wd_m, wd_o, wd, sems.at[1])
    wait_pos = fetch(near_1, pos_m, pos_o, pos, sems.at[2])
    wait_qkv = fetch(near_1, wq_m, wq_o, wq, sems.at[3])
    wait_out = fetch(near_1, wo_m, wo_o, wo, sems.at[4])
    wait_cotangent = copy(cotangent.at[sec], arriving, sems.at[5])
    write_mask(place_ref, mask)
    small_0 = chosen(near_0, vec_m, vec_o)
    small_1 = chosen(near_1, vec_m, vec_o)
    sum_two = feed(
        small_0, sum_one_0[...], wu, wd, acc, low_0, active_0, slope_0, wait_up, wait_down
    )
    sum_two_0[...] = sum_two
    wait_up = fetch(near_1, wu_m, wu_o, wu, sems.at[0])
    wait_down = fetch(near_1, wd_m, wd_o, wd, sems.at[1])
    wait_pos()
    wait_qkv()
    normed, _ = normalize(sum_two)
    result = (normed * small_0[4:5] + small_0[5:6]).astype(BF16)
    position = pos[...].astype(F32)
    for w in range(2):
        rows = window_rows(w)
        stream_1[w] = result[rows]
        hidden[rows, :] = result[rows].astype(F32) + position
    project_rows(hidden[...].astype(BF16), wq, project_1)
    attend(mask, project_1, probs_1, mixed_1)
    wait_out()
    wait_cotangent()
    sum_one = hidden[...] + nn(mixed_1[...], wo[...])
    sum_one_1[...] = sum_one
    sum_two = feed(
        small_1, sum_one, wu, wd, acc, low_1, active_1, slope_1, wait_up, wait_down
    )
    normed, _ = normalize(sum_two)
    result = normed * small_1[4:5] + small_1[5:6]
    upstream = []
    for w in range(2):
        output[w] = unused_zeroed(place_ref, w, result[window_rows(w)]).astype(BF16)
        upstream.append(unused_zeroed(place_ref, w, arriving[w].astype(F32)))
    e = jnp.concatenate(upstream, 0)
    feed_back(
        sec, small_1, e, sum_two, wu, wd, acc, low_1, active_1, slope_1, small_grads, grads, send
    )
    grad_after[...] = acc[...]


def forward_middle(place, cotangent, mine, other, sum_one):
    args = [place, cotangent]
    for a, b in zip(mine, other):
        args += [a, b]
    return pl.pallas_call(
        middle_kernel,
        out_shape=FEED_KEPT
        + [sds((2, WIN, D), BF16)]
        + ATTENTION_KEPT
        + [sds((2, WIN, D), BF16)]
        + FFN_GRADS,
        in_specs=[SM, HBM] + [HBM, ANY] * 5 + [VM] * 3,
        out_specs=[VM] * 14,
        scratch_shapes=[
            pltpu.VMEM((2, WIN, D), BF16),
            pltpu.VMEM((WIN, D), BF16),
            pltpu.VMEM((D, 3 * D), BF16),
            pltpu.VMEM((D, D), BF16),
            pltpu.VMEM((D, FF), BF16),
            pltpu.VMEM((FF, D), BF16),
            pltpu.VMEM((ROWS, D), F32),
            pltpu.VMEM((2, WIN, WIN), F32),
            pltpu.VMEM((ROWS, D), F32),
            pltpu.VMEM((ROWS, D), BF16),
            pltpu.VMEM((ROWS, FF), BF16),
            pltpu.VMEM((ROWS, FF), BF16),
            DMA((6,)),
        ],
        compiler_params=limit(MIDDLE_LIMIT),
        cost_estimate=HEAVY,
        name="feed_0_to_feed_backward_1",
    )(*args, sum_one)


MIDDLE_LIMIT = 23


def out_kernel(
    layer,
    place_ref,
    wo_m,
    wo_o,
    vec_m,
    vec_o,
    grad_after,
    sum_one,
    mixed,
    small_in,
    grad_sum_ref,
    grad_mixed,
    grad_out,
    rows_ref,
    wo,
    sem,
):
    near = place_ref[0] == layer
    wait_out = fetch(near, wo_m, wo_o, wo, sem)
    small = chosen(near, vec_m, vec_o)
    normed, inverse = normalize(sum_one[...] + small[0:1])
    e = grad_after[...]
    row_norm = jnp.sum(e * normed, 0, keepdims=True)
    row_shift = jnp.sum(e, 0, keepdims=True)
    grad_sum = norm_backward(e, normed, inverse, small[1:2])
    grad_sum_ref[...] = grad_sum
    branch = grad_sum.astype(BF16)
    row_out = jnp.sum(branch.astype(F32), 0, keepdims=True)
    rows = jnp.concatenate([row_out, row_norm, row_shift, jnp.zeros((5, D), F32)], 0)
    rows_ref[...] = jnp.concatenate([rows, small_in[...]], 0).astype(BF16)
    wait_out()
    grad_mixed[...] = nt(branch, wo[...]).astype(BF16)
    grad_out[...] = tn(mixed[...], branch).astype(BF16)


def out_back(layer, place, mine, other, grad_after, kept, small):
    def body(*refs):
        out_kernel(layer, *refs)

    return pl.pallas_call(
        body,
        out_shape=[
            sds((ROWS, D), F32),
            sds((ROWS, D), BF16),
            sds((D, D), BF16),
            sds((16, D), BF16),
        ],
        in_specs=[SM, HBM, ANY] + [VM] * 6,
        out_specs=[VM] * 4,
        scratch_shapes=[pltpu.VMEM((D, D), BF16), DMA],
        compiler_params=limit(8),
        cost_estimate=HEAVY,
        name=f"projection_backward_{layer}",
    )(place, mine[2], other[2], mine[5], other[5], grad_after, kept[3], kept[2], small)


def late_kernel(
    place_ref,
    pos_m,
    pos_o,
    wq_m,
    wq_o,
    wu_m,
    wu_o,
    wd_m,
    wd_o,
    vec_m,
    vec_o,
    stream_1,
    project_1,
    probs_1,
    grad_sum,
    grad_mixed,
    grad_out,
    rows_1,
    low_0,
    active_0,
    slope_0,
    sum_two_0,
    att_grads,
    att_send,
    grad_after,
    small_grads,
    ffn_grads,
    ffn_send,
    pos,
    wq,
    wu,
    wd,
    grad_project,
    total,
    sems,
):
    sec = place_ref[0]
    wait_qkv = fetch(sec == 1, wq_m, wq_o, wq, sems.at[0])
    wait_pos = fetch(sec == 1, pos_m, pos_o, pos, sems.at[1])
    wait_down = fetch(sec == 0, wd_m, wd_o, wd, sems.at[2])
    wait_up = fetch(sec == 0, wu_m, wu_o, wu, sems.at[3])
    small = chosen(sec == 0, vec_m, vec_o)
    attend_back(project_1, probs_1, grad_mixed, grad_project)
    wait_qkv()
    wait_pos()
    wait_down()
    wait_up()
    input_back(
        sec, stream_1, pos, wq, grad_sum, grad_out, rows_1, grad_project, total, att_grads, att_send
    )
    e = total[...].astype(BF16).astype(F32)
    feed_back(
        sec,
        small,
        e,
        sum_two_0[...],
        wu,
        wd,
        total,
        low_0,
        active_0,
        slope_0,
        small_grads,
        ffn_grads,
        ffn_send,
    )
    grad_after[...] = total[...]


def late_back(place, mine, other, stream, attention, before, feed_kept):
    args = [place]
    for i in (0, 1, 3, 4, 5):
        args += [mine[i], other[i]]
    return pl.pallas_call(
        late_kernel,
        out_shape=ATT_GRADS + FFN_GRADS,
        in_specs=[SM] + [HBM, ANY] * 4 + [VM] * 13,
        out_specs=[VM] * 6,
        scratch_shapes=[
            pltpu.VMEM((WIN, D), BF16),
            pltpu.VMEM((D, 3 * D), BF16),
            pltpu.VMEM((D, FF), BF16),
            pltpu.VMEM((FF, D), BF16),
            pltpu.VMEM((ROWS, 3 * D), BF16),
            pltpu.VMEM((ROWS, D), F32),
            DMA((4,)),
        ],
        compiler_params=limit(21),
        cost_estimate=HEAVY,
        name="attention_backward_1_and_feed_backward_0",
    )(*args, stream, attention[0], attention[1], *before, *feed_kept)


def last_kernel(
    place_ref,
    tokens,
    pos_m,
    pos_o,
    wq_m,
    wq_o,
    project,
    probs,
    grad_sum,
    grad_mixed,
    grad_out,
    rows,
    grad_low,
    grads,
    send,
    stream,
    pos,
    wq,
    grad_project,
    total,
    sems,
):
    sec = place_ref[0]
    wait_qkv = fetch(sec == 0, wq_m, wq_o, wq, sems.at[0])
    wait_pos = fetch(sec == 0, pos_m, pos_o, pos, sems.at[1])
    wait_stream = copy(tokens.at[sec], stream, sems.at[2])
    attend_back(project, probs, grad_mixed, grad_project)
    wait_qkv()
    wait_pos()
    wait_stream()
    input_back(
        sec, stream, pos, wq, grad_sum, grad_out, rows, grad_project, total, grads, send
    )
    for w in range(2):
        grad_low[w] = total[window_rows(w), :].astype(BF16)


def last_back(place, tokens, mine, other, attention, before):
    args = [place, tokens]
    for i in (0, 1):
        args += [mine[i], other[i]]
    return pl.pallas_call(
        last_kernel,
        out_shape=[sds((2, WIN, D), BF16)] + ATT_GRADS,
        in_specs=[SM, HBM] + [HBM, ANY] * 2 + [VM] * 6,
        out_specs=[VM] * 3,
        scratch_shapes=[
            pltpu.VMEM((2, WIN, D), BF16),
            pltpu.VMEM((WIN, D), BF16),
            pltpu.VMEM((D, 3 * D), BF16),
            pltpu.VMEM((ROWS, 3 * D), BF16),
            pltpu.VMEM((ROWS, D), F32),
            DMA((3,)),
        ],
        compiler_params=limit(14),
        cost_estimate=HEAVY,
        name="attention_backward_0",
    )(*args, attention[0], attention[1], *before)


def pack_vectors(b_out, gain_one, shift_one, b_down, gain_two, shift_two, b_up):
    def body(*refs):
        out = refs[-1]
        rows = [ref[...].astype(F32) for ref in refs[:6]]
        wide = refs[6][...].astype(F32)
        rows += [wide[:, c * D : (c + 1) * D] for c in range(4)]
        rows += [jnp.zeros((6, D), F32)]
        out[...] = jnp.concatenate(rows, 0).astype(BF16)

    return pl.pallas_call(
        body,
        out_shape=sds((16, D), BF16),
        in_specs=[VM] * 7,
        out_specs=VM,
        name="pack_vectors",
    )(b_out, gain_one, shift_one, b_down, gain_two, shift_two, b_up)


def plain(body, shapes, args, name, specs=None):
    return pl.pallas_call(
        body,
        out_shape=[sds(shape, BF16) for shape in shapes],
        in_specs=specs or [VM] * len(args),
        out_specs=[VM] * len(shapes),
        compiler_params=limit(8),
        cost_estimate=SLIGHT,
        name=name,
    )(*args)


def stage_order(place_ref):
    first = place_ref[0] == 0
    strides = [jnp.where(first, a, b) for a, b in zip(*WAY)]
    coords = [lax.rem(lax.div(place_ref[1], stride), 4) for stride in strides]

    def owner(*distances):
        return sum(
            lax.rem(coord + r, 4) * stride
            for coord, r, stride in zip(coords, distances, strides)
        )

    return owner


def pair_sum(place, *arrays):
    ranges = []
    for i in range(len(arrays) // 2):
        if arrays[2 * i + 1].shape[0] == 8192:
            ranges += [(i, 0, FFN_PART)]
        else:
            ranges += [(i, 0, 64), (i, EXTRA, 16)]
    part = sum(rows for _, _, rows in ranges)

    def body(place_ref, *refs):
        outs = refs[len(arrays) :]
        owner = stage_order(place_ref)
        sec = place_ref[0]
        for third in range(4):
            for second in range(4):
                for first in range(4):
                    dev = owner(first, second, third)
                    at = (second * 4 + first) * part
                    for i, base, rows in ranges:
                        src = pl.ds(pl.multiple_of(base + dev * rows, 16), rows)
                        total = refs[2 * i][sec, src, :].astype(F32)
                        total += refs[2 * i + 1][src, :].astype(F32)
                        outs[third][at : at + rows, :] = total.astype(BF16)
                        at += rows

    specs = [SM] + [VM] * len(arrays)
    return plain(body, [(16 * part, 128)] * 4, (place,) + arrays, "sum_of_two_cores", specs)


def add_four(refs, at):
    return sum(ref[at].astype(F32) for ref in refs)


def line_sum(*arrivals):
    rows = arrivals[0][0].shape[0] // 16
    count = len(arrivals)

    def body(*refs):
        outs = refs[4 * count :]
        for r in range(4):
            for first in range(4):
                at = (r * 4 + first) * rows
                for i in range(count):
                    total = add_four(refs[4 * i : 4 * i + 4], (slice(at, at + rows), slice(None)))
                    outs[r][first, i] = total.astype(BF16)

    args = sum(arrivals, [])
    return plain(body, [(4, count, rows, 128)] * 4, args, "sum_over_line")


def early_line_sum(late_ffn, mixed):
    def body(*refs):
        outs = refs[8:]
        for r in range(4):
            for first in range(4):
                i = r * 4 + first
                at = slice(i * FFN_PART, (i + 1) * FFN_PART)
                total = add_four(refs[0:4], (at, slice(None)))
                outs[r][first, 0:FFN_PART, :] = total.astype(BF16)
                at = slice(i * CHUNK, (i + 1) * CHUNK)
                total = add_four(refs[4:8], (at, slice(None)))
                outs[r][first, FFN_PART:, :] = total.astype(BF16)

    return plain(
        body, [(4, FFN_PART + CHUNK, 128)] * 4, late_ffn + mixed, "sum_over_line_early"
    )


def plane_sum(early, last):
    def body(*refs):
        outs = refs[8:]
        for first in range(4):
            total = add_four(refs[0:4], first).astype(BF16)
            outs[first][1, 0:FFN_PART, :] = total[0:FFN_PART]
            outs[first][0, 0:FFN_PART, :] = total[FFN_PART : 2 * FFN_PART]
            outs[first][1, FFN_PART:, :] = total[2 * FFN_PART :]
            outs[first][0, FFN_PART:, :] = add_four(refs[4:8], (first, 0)).astype(BF16)

    return plain(body, [(2, CHUNK, 128)] * 4, early + last, "sum_over_plane")


def cube_sum(place, pieces):
    def body(place_ref, *refs):
        sec = place_ref[0]
        refs[4][...] = add_four(refs[:4], sec).astype(BF16)
        refs[5][...] = add_four(refs[:4], 1 - sec).astype(BF16)

    specs = [SM] + [VM] * 4
    return plain(body, [(CHUNK, 128)] * 2, [place] + pieces, "sum_over_cube", specs)


def place_parts(place_ref, sources, targets, pos, small, ready, sems):
    wu_ref, wd_ref, wq_ref, wo_ref = targets
    sec = place_ref[0]
    owner = stage_order(place_ref)
    waits = []
    for n, (ref, third, second) in enumerate(sources):
        for step in range(8):
            dev = owner(step % 4, second + step // 4, third)
            slot = n * 8 + step

            def write(kind, rows, base, half, n=n, step=step, slot=slot, ref=ref):
                side = sec if half == 0 else 1 - sec
                ready[kind][slot] = ref[step, side, base : base + rows, :].astype(F32)
                return ready[kind].at[slot]

            def send(kind, src, dst, slot=slot):
                return pltpu.make_async_copy(src, dst, sems.at[kind, slot])

            def lanes(start):
                return pl.ds(pl.multiple_of(start * 128, 128), 128)

            block = lax.div(dev, 4)
            r = pl.multiple_of(lax.rem(dev, 4) * 128, 128)
            up = send(
                0, write(0, FFN_PART, 0, 0), wu_ref.at[0, pl.ds(r, FFN_PART), lanes(block)]
            )
            up.start()
            r = pl.multiple_of(lax.div(block, 4) * D + r, 128)
            down = send(
                1,
                write(1, FFN_PART, 0, 1),
                wd_ref.at[0, pl.ds(r, FFN_PART), lanes(lax.rem(block, 4))],
            )
            down.start()
            block = lax.div(dev, 8)
            rows = pl.ds(pl.multiple_of(lax.rem(dev, 8) * 64, 64), 64)
            first = send(2, write(2, 64, FFN_PART, 0), wq_ref.at[0, rows, lanes(block)])
            first.start()
            src = write(3, 64, FFN_PART, 1)

            @pl.when(block < 4)
            def _(src=src, rows=rows, block=block, send=send, lanes=lanes):
                send(3, src, wq_ref.at[0, rows, lanes(block + 8)]).start()

            @pl.when(block >= 4)
            def _(src=src, rows=rows, block=block, send=send, lanes=lanes):
                send(3, src, wo_ref.at[0, rows, lanes(block - 4)]).start()

            waits += [up, down, first, send(3, src, wq_ref.at[0, rows, lanes(block)])]
            for half in range(2):
                side = sec if half == 0 else 1 - sec
                extra = ref[step, side, FFN_PART + 64 : CHUNK, :].astype(F32)
                at = pl.multiple_of(half * 128 + lax.rem(dev, 16) * 8, 8)
                pos[pl.ds(at, 8), lanes(lax.div(dev, 16))] = extra[0:8]
                if half == 0:
                    small[pl.ds(pl.multiple_of(dev * 8, 8), 8), :] = extra[8:16]
    for copy_out in waits:
        copy_out.wait()


WEIGHT_GRADS = [
    sds((1, D, FF), F32),
    sds((1, FF, D), F32),
    sds((1, D, 3 * D), F32),
    sds((1, D, D), F32),
]
PLACED = [sds((WIN, D), F32), sds((64 * 8, 128), F32)]
VECTOR = sds((1, D), F32)
LAST = [sds((1, WIN, D), F32)] + [VECTOR] * 3 + [sds((1, FF), F32)] + [VECTOR] * 3


def place_gradients(place, sources, placed=(), final=False):
    count = len(sources)

    def body(place_ref, *refs):
        gathered = [(refs[i],) + sources[i][1:] for i in range(count)]
        refs = refs[count:]
        before, refs = refs[: len(placed)], refs[len(placed) :]
        targets, refs = refs[:4], refs[4:]
        if final:
            pos, bo, g1, s1, bu, bd, g2, s2, small = refs[:9]
            pos = pos.at[0]
            refs = refs[9:]
        else:
            pos, small = refs[:2]
            refs = refs[2:]
        if before:
            pos[...] = before[4][...]
            small[...] = before[5][...]
        place_parts(place_ref, gathered, targets, pos, small, refs[:4], refs[4])
        if not final:
            return
        for c in range(4):
            lane = slice(c * 128, (c + 1) * 128)
            at = c * 16
            for ref, row in ((bo, 0), (g1, 1), (s1, 2), (bd, 8), (g2, 9), (s2, 10)):
                ref[:, lane] = small[at + row : at + row + 1, :]
            for j in range(4):
                row = at + 11 + j
                bu[:, j * D + c * 128 : j * D + (c + 1) * 128] = small[row : row + 1, :]

    slots = 8 * count
    ready = [
        pltpu.VMEM((slots, FFN_PART, 128), F32),
        pltpu.VMEM((slots, FFN_PART, 128), F32),
        pltpu.VMEM((slots, 64, 128), F32),
        pltpu.VMEM((slots, 64, 128), F32),
        DMA((4, slots)),
    ]
    if final:
        ready = [pltpu.VMEM((64 * 8, 128), F32)] + ready
    outs = LAST if final else PLACED
    return pl.pallas_call(
        body,
        out_shape=WEIGHT_GRADS + outs,
        in_specs=[SM] + [VM] * count + ([HBM] * 4 + [VM] * 2 if placed else []),
        out_specs=[HBM] * 4 + [VM] * len(outs),
        scratch_shapes=ready,
        input_output_aliases={1 + count + i: i for i in range(4)} if placed else {},
        compiler_params=limit(12),
        cost_estimate=HEAVY,
        name="place_gradients",
    )(place, *[source[0] for source in sources], *placed)


def swap(value):
    return lax.ppermute(value, "section", [(0, 1), (1, 0)])


def from_ahead(value, stage, distance):
    pairs = []
    for section in range(2):
        stride = WAY[section][stage]
        for dst in range(64):
            at = dst // stride % 4
            src = dst + ((at + distance) % 4 - at) * stride
            pairs.append((section * 64 + src, section * 64 + dst))
    return lax.ppermute(value, ("section", "dp"), pairs)


def send_ahead(pieces, stage):
    return [pieces[0]] + [from_ahead(pieces[r], stage, 4 - r) for r in (1, 3, 2)]


def gather(chunk):
    line = jnp.stack([chunk] + [from_ahead(chunk, 0, r) for r in (1, 2, 3)])
    ahead = [from_ahead(line, 1, r) for r in (1, 2, 3)]
    own_a = jnp.concatenate([line, ahead[0]], 0)
    own_b = jnp.concatenate([ahead[1], ahead[2]], 0)
    next_a = from_ahead(own_a, 2, 1)
    prev_b = from_ahead(own_b, 2, 3)
    next_b = from_ahead(own_b, 2, 1)
    prev_a = from_ahead(own_a, 2, 3)
    far_a = from_ahead(next_a, 2, 1)
    far_b = from_ahead(prev_b, 2, 3)
    return own_a, own_b, next_a, next_b, far_a, far_b, prev_a, prev_b


def hold(*values):
    return tuple(pltpu.with_memory_space_constraint(value, pltpu.HBM) for value in values)


def shards(
    tokens,
    lengths,
    out_cotangent,
    pos_table,
    w_qkv,
    w_out,
    b_out,
    norm1_gain,
    norm1_bias,
    w_up,
    b_up,
    w_down,
    b_down,
    norm2_gain,
    norm2_bias,
):
    section = lax.axis_index("section")
    place = jnp.stack([section, lax.axis_index("dp")]).astype(jnp.int32)
    place = jnp.concatenate([place, lengths.reshape(4)])
    vec = pack_vectors(b_out, norm1_gain, norm1_bias, b_down, norm2_gain, norm2_bias, b_up)
    got_qkv = swap(w_qkv)
    got_pos = swap(pos_table)
    got_out = swap(w_out)
    late_up, late_down, got_qkv = lax.optimization_barrier((w_up, w_down, got_qkv))
    mine = hold(pos_table, w_qkv, w_out, w_up, w_down) + (vec,)
    other = (got_pos, got_qkv, got_out, swap(late_up), swap(late_down), swap(vec))
    tokens, out_cotangent = hold(tokens, out_cotangent)
    attention_0 = forward_first(place, tokens, mine, other)
    middle = forward_middle(place, out_cotangent, mine, other, attention_0[3])
    feed_0, stream, attention_1, output = middle[0:4], middle[4], middle[5:9], middle[9]
    after, small, ffn_both, ffn_send = middle[10:14]

    def tie(*values):
        return lax.optimization_barrier(values)

    ffn_got = swap(ffn_send)
    before = out_back(1, place, mine, other, after, attention_1, small)
    pieces = pair_sum(place, ffn_both, ffn_got)
    before, pieces = tie(before, pieces)
    late_ffn = send_ahead(pieces, 2)
    att_both, att_send, after, small, ffn_both, ffn_send = late_back(
        place, mine, other, stream, attention_1, before, feed_0
    )
    after, late_ffn = tie(after, late_ffn)
    att_got = swap(att_send)
    ffn_got = swap(ffn_send)
    before = out_back(0, place, mine, other, after, attention_0, small)
    pieces = pair_sum(place, ffn_both, ffn_got, att_both, att_got)
    before, pieces = tie(before, pieces)
    mixed = send_ahead(pieces, 2)
    arriving, att_both, att_send = last_back(place, tokens, mine, other, attention_0, before)
    att_send, mixed = tie(att_send, mixed)
    pieces = pair_sum(place, att_both, swap(att_send))
    early = send_ahead(early_line_sum(late_ffn, mixed), 1)
    last = send_ahead(line_sum(send_ahead(pieces, 2)), 1)
    pieces = plane_sum(early, last)
    own, others = cube_sum(place, send_ahead(pieces, 0))
    chunk = jnp.stack([own, swap(others)])
    own_a, own_b, next_a, next_b, far_a, far_b, prev_a, prev_b = gather(chunk)
    sources = [(own_a, 0, 0), (own_b, 0, 2), (next_a, 1, 0), (prev_b, 3, 2)]
    placed = place_gradients(place, sources)
    placed = place_gradients(place, [(next_b, 1, 2), (prev_a, 3, 0)], placed)
    up, down, qkv, out, position, bias, gain_one, shift_one, bias_up, bias_down, gain_two, shift_two = (
        place_gradients(place, [(far_a, 2, 0), (far_b, 2, 2)], placed, True)
    )
    return (
        output[None],
        arriving[None],
        position,
        qkv,
        out,
        bias,
        gain_one,
        shift_one,
        up,
        bias_up,
        down,
        bias_down,
        gain_two,
        shift_two,
    )


def solution(mesh):
    placed = (
        P(None, "dp", None, None),
        P(None, "dp"),
        P(None, "dp", None, None),
        P("section", None, None),
        P("section", None, None),
        P("section", None, None),
        P("section", None),
        P("section", None),
        P("section", None),
        P("section", None, None),
        P("section", None),
        P("section", None, None),
        P("section", None),
        P("section", None),
        P("section", None),
    )
    return jax.shard_map(
        shards,
        mesh=mesh,
        in_specs=placed,
        out_specs=(
            P("section", "dp", None, None),
            P("section", "dp", None, None),
            P("section", None, None),
            P("section", None, None),
            P("section", None, None),
            P("section", None),
            P("section", None),
            P("section", None),
            P("section", None, None),
            P("section", None),
            P("section", None, None),
            P("section", None),
            P("section", None),
            P("section", None),
        ),
        check_vma=False,
    )
```

```python
import jax
import jax.numpy as jnp
from jax import lax
from jax.experimental import pallas as pl
from jax.experimental.pallas import tpu as pltpu
from jax.sharding import PartitionSpec as P

D = 512
FF = 2048
WIN = 256
ROWS = 512
F32 = jnp.float32
BF16 = jnp.bfloat16

HBM = pl.BlockSpec(memory_space=pltpu.HBM)
ANY = pl.BlockSpec(memory_space=pl.ANY)
VM = pl.BlockSpec(memory_space=pltpu.VMEM)
SM = pl.BlockSpec(memory_space=pltpu.SMEM)
DMA = pltpu.SemaphoreType.DMA
SLIGHT = pl.CostEstimate(flops=1000, bytes_accessed=1000, transcendentals=0)
HEAVY = pl.CostEstimate(flops=35_000_000_000, bytes_accessed=1000, transcendentals=0)
EXTRA = 4096
FFN_PART = 128
ATT_PART = 80
CHUNK = FFN_PART + ATT_PART
WAY = ((16, 4, 1), (1, 16, 4))


def limit(mebibytes):
    return pltpu.CompilerParams(vmem_limit_bytes=mebibytes * 1024 * 1024)


def sds(shape, dtype):
    return jax.ShapeDtypeStruct(shape, dtype)


def nn(a, b):
    return lax.dot_general(a, b, (((1,), (0,)), ((), ())), preferred_element_type=F32)


def nt(a, b):
    return lax.dot_general(a, b, (((1,), (1,)), ((), ())), preferred_element_type=F32)


def tn(a, b):
    return lax.dot_general(a, b, (((0,), (0,)), ((), ())), preferred_element_type=F32)


def fetch(near, mine, other, dst, sem):
    @pl.when(near)
    def _():
        pltpu.make_async_copy(mine.at[0], dst, sem).start()

    @pl.when(jnp.logical_not(near))
    def _():
        pltpu.make_async_copy(other.at[0], dst, sem).start()

    return pltpu.make_async_copy(mine.at[0], dst, sem).wait


def copy(src, dst, sem):
    load = pltpu.make_async_copy(src, dst, sem)
    load.start()
    return load.wait


def chosen(near, mine, other):
    return jnp.where(near, mine[...].astype(F32), other[...].astype(F32))


def normalize(v):
    center = v - jnp.mean(v, -1, keepdims=True)
    inverse = lax.rsqrt(jnp.mean(center * center, -1, keepdims=True) + 1e-05)
    return center * inverse, inverse


def norm_backward(e, normed, inverse, gain):
    scaled = e * gain
    return inverse * (
        scaled
        - jnp.mean(scaled, -1, keepdims=True)
        - normed * jnp.mean(scaled * normed, -1, keepdims=True)
    )


def gelu_pair(v):
    c = 0.7978845608028654
    poly = c + (c * 0.044715) * (v * v)
    t = jnp.tanh(v * poly)
    half = 0.5 + 0.5 * t
    active = v * half
    return active, half + (active - active * t) * (3.0 * poly - 2.0 * c)


def used(place_ref, window):
    return place_ref[2 + 2 * place_ref[0] + window]


def write_mask(place_ref, mask):
    rows = lax.broadcasted_iota(jnp.int32, (WIN, WIN), 0)
    cols = lax.broadcasted_iota(jnp.int32, (WIN, WIN), 1)
    for w in range(2):
        inside = (cols <= rows) & (cols < used(place_ref, w))
        mask[w] = jnp.where(inside, 0.0, -1e30)


def window_rows(w):
    return slice(w * WIN, (w + 1) * WIN)


def unused_zeroed(place_ref, w, part):
    at_row = lax.broadcasted_iota(jnp.int32, (WIN, D), 0)
    return jnp.where(at_row < used(place_ref, w), part, 0.0)


def project_rows(hidden_low, wq, project):
    for c in range(3):
        at = slice(c * D, (c + 1) * D)
        project[:, at] = nn(hidden_low, wq[:, at]).astype(BF16)


def attend(mask, project, probs, mixed):
    lanes = lax.broadcasted_iota(jnp.int32, (WIN, 128), 1)
    for step in range(8):
        w, p = step // 4, step % 4
        rows = window_rows(w)
        at = [slice(j * D + p * 128, j * D + (p + 1) * 128) for j in range(3)]
        q2 = project[rows, at[0]] * jnp.asarray(0.125, BF16)
        k2 = project[rows, at[1]]
        v2 = project[rows, at[2]]
        blocked = mask[w]
        parts = []
        for h in range(2):
            own = (lanes >= 64) if h else (lanes < 64)
            qm = jnp.where(own, q2, jnp.zeros_like(q2))
            scores = nt(qm, k2) + blocked
            raised = jnp.exp(scores - jnp.max(scores, -1, keepdims=True))
            soft = (raised * (1.0 / jnp.sum(raised, -1, keepdims=True))).astype(BF16)
            probs[step * 2 + h] = soft
            parts.append(nn(soft, v2))
        mixed[rows, at[0]] = jnp.where(lanes < 64, parts[0], parts[1]).astype(BF16)


def attend_back(project, probs, grad_mixed, grad_project):
    lanes = lax.broadcasted_iota(jnp.int32, (WIN, 128), 1)
    for step in range(8):
        w, p = step // 4, step % 4
        rows = window_rows(w)
        at = [slice(j * D + p * 128, j * D + (p + 1) * 128) for j in range(3)]
        q2 = project[rows, at[0]] * jnp.asarray(0.125, BF16)
        k2 = project[rows, at[1]]
        v2 = project[rows, at[2]]
        g2 = grad_mixed[rows, at[0]]
        grad_q, grad_k, grad_v = [], [], []
        for h in range(2):
            own = (lanes >= 64) if h else (lanes < 64)
            none = jnp.zeros_like(q2)
            gm = jnp.where(own, g2, none)
            qm = jnp.where(own, q2, none)
            soft_low = probs[step * 2 + h]
            soft = soft_low.astype(F32)
            product = soft * nt(gm, v2)
            grad_scores = (product - soft * jnp.sum(product, -1, keepdims=True)).astype(BF16)
            grad_q.append(nn(grad_scores, k2))
            grad_k.append(tn(grad_scores, qm))
            grad_v.append(tn(soft_low, gm))
        grad_project[rows, at[0]] = (
            jnp.where(lanes < 64, grad_q[0], grad_q[1]) * 0.125
        ).astype(BF16)
        grad_project[rows, at[1]] = (grad_k[0] + grad_k[1]).astype(BF16)
        grad_project[rows, at[2]] = (grad_v[0] + grad_v[1]).astype(BF16)


def feed(small, sum_one, wu, wd, acc, low_ref, active_ref, slope_ref, wait_up, wait_down):
    normed, _ = normalize(sum_one + small[0:1])
    after = normed * small[1:2] + small[2:3]
    acc[...] = after
    low = after.astype(BF16)
    low_ref[...] = low
    wait_up()
    for c in range(4):
        block = slice(c * D, (c + 1) * D)
        value = nn(low, wu[:, block]) + small[6 + c : 7 + c]
        active, slope = gelu_pair(value)
        active = active.astype(BF16)
        active_ref[:, block] = active
        slope_ref[:, block] = slope.astype(BF16)
    wait_down()
    return acc[...] + (nn(active_ref[...], wd[...]) + small[3:4])


def feed_back(
    sec, small, e, sum_two, wu, wd, acc, low_ref, active_ref, slope_ref, small_ref, grads, send
):
    normed, inverse = normalize(sum_two)
    small_ref[...] = jnp.zeros_like(small_ref)
    small_ref[1:2, :] = jnp.sum(e * normed, 0, keepdims=True)
    small_ref[2:3, :] = jnp.sum(e, 0, keepdims=True)
    grad_sum = norm_backward(e, normed, inverse, small[4:5])
    acc[...] = grad_sum
    grad_low = grad_sum.astype(BF16)
    small_ref[0:1, :] = jnp.sum(grad_low.astype(F32), 0, keepdims=True)
    for c in range(4):
        block = slice(c * D, (c + 1) * D)
        grad_up = nt(grad_low, wd[block, :]) * slope_ref[:, block].astype(F32)
        grad_up = grad_up.astype(BF16)
        small_ref[3 + c : 4 + c, :] = jnp.sum(grad_up.astype(F32), 0, keepdims=True)
        slope_ref[:, block] = grad_up
        grad_wu = tn(low_ref[...], grad_up).astype(BF16)
        grad_wd = tn(active_ref[:, block], grad_low).astype(BF16)
        for k in range(4):
            at = slice((c * 4 + k) * D, (c * 4 + k + 1) * D)
            grads[0, at, :] = grad_wu[:, k * 128 : (k + 1) * 128]
            grads[1, at, :] = grad_wd[:, k * 128 : (k + 1) * 128]
    acc[...] += nt(slope_ref[...], wu[...])
    send[...] = grads[1 - sec]


def input_back(
    sec, stream, pos, wq, grad_sum, grad_out, rows, grad_project, total, grads, send
):
    for c in range(4):
        grads[1, 2048 + c * D : 2048 + (c + 1) * D, :] = grad_out[:, c * 128 : (c + 1) * 128]
    position = pos[...].astype(F32)
    hidden_low = jnp.concatenate(
        [(stream[w].astype(F32) + position).astype(BF16) for w in range(2)], 0
    )
    total[...] = grad_sum[...]
    for j in range(3):
        block = slice(j * D, (j + 1) * D)
        part = grad_project[:, block]
        total[...] += nt(part, wq[:, block])
        grad_w = tn(hidden_low, part).astype(BF16)
        half, base = ((0, 0), (0, 2048), (1, 0))[j]
        for c in range(4):
            grads[half, base + c * D : base + (c + 1) * D, :] = grad_w[:, c * 128 : (c + 1) * 128]
    grad_pos = total[0:WIN, :] + total[WIN : 2 * WIN, :]
    small = rows[...].astype(F32)
    blank = jnp.zeros((8, 128), F32)
    for c in range(4):
        lanes_at = slice(c * 128, (c + 1) * 128)
        for half in range(2):
            extra = []
            for i in range(16):
                at = half * 128 + i * 8
                extra.append(grad_pos[at : at + 8, lanes_at])
                if c == 0 and i < 8:
                    extra.append(small[i % 2 * 8 : i % 2 * 8 + 8, i // 2 * 128 : i // 2 * 128 + 128])
                else:
                    extra.append(blank)
            at = EXTRA + c * WIN
            grads[half, at : at + WIN, :] = jnp.concatenate(extra, 0).astype(BF16)
    send[...] = grads[1 - sec]


def first_kernel(
    place_ref,
    tokens,
    pos_m,
    pos_o,
    wq_m,
    wq_o,
    wo_m,
    wo_o,
    project,
    probs,
    mixed,
    sum_one,
    stream,
    pos,
    wq,
    wo,
    hidden,
    mask,
    sems,
):
    sec = place_ref[0]
    wait_stream = copy(tokens.at[sec], stream, sems.at[0])
    wait_pos = fetch(sec == 0, pos_m, pos_o, pos, sems.at[1])
    wait_qkv = fetch(sec == 0, wq_m, wq_o, wq, sems.at[2])
    wait_out = fetch(sec == 0, wo_m, wo_o, wo, sems.at[3])
    write_mask(place_ref, mask)
    wait_stream()
    wait_pos()
    position = pos[...].astype(F32)
    for w in range(2):
        hidden[window_rows(w), :] = stream[w].astype(F32) + position
    wait_qkv()
    wait_out()
    project_rows(hidden[...].astype(BF16), wq, project)
    attend(mask, project, probs, mixed)
    sum_one[...] = hidden[...] + nn(mixed[...], wo[...])


ATTENTION_KEPT = [
    sds((ROWS, 3 * D), BF16),
    sds((16, WIN, WIN), BF16),
    sds((ROWS, D), BF16),
    sds((ROWS, D), F32),
]
FEED_KEPT = [
    sds((ROWS, D), BF16),
    sds((ROWS, FF), BF16),
    sds((ROWS, FF), BF16),
    sds((ROWS, D), F32),
]
FFN_GRADS = [
    sds((ROWS, D), F32),
    sds((8, D), F32),
    sds((2, 8192, 128), BF16),
    sds((8192, 128), BF16),
]
ATT_GRADS = [sds((2, 5120, 128), BF16), sds((5120, 128), BF16)]


def forward_first(place, tokens, mine, other):
    args = [place, tokens]
    for i in (0, 1, 2):
        args += [mine[i], other[i]]
    return pl.pallas_call(
        first_kernel,
        out_shape=ATTENTION_KEPT,
        in_specs=[SM, HBM] + [HBM, ANY] * 3,
        out_specs=[VM] * 4,
        scratch_shapes=[
            pltpu.VMEM((2, WIN, D), BF16),
            pltpu.VMEM((WIN, D), BF16),
            pltpu.VMEM((D, 3 * D), BF16),
            pltpu.VMEM((D, D), BF16),
            pltpu.VMEM((ROWS, D), F32),
            pltpu.VMEM((2, WIN, WIN), F32),
            DMA((4,)),
        ],
        compiler_params=limit(12),
        cost_estimate=HEAVY,
        name="forward_attention_0",
    )(*args)


def middle_kernel(
    place_ref,
    cotangent,
    pos_m,
    pos_o,
    wq_m,
    wq_o,
    wo_m,
    wo_o,
    wu_m,
    wu_o,
    wd_m,
    wd_o,
    vec_m,
    vec_o,
    sum_one_0,
    low_0,
    active_0,
    slope_0,
    sum_two_0,
    stream_1,
    project_1,
    probs_1,
    mixed_1,
    sum_one_1,
    output,
    grad_after,
    small_grads,
    grads,
    send,
    arriving,
    pos,
    wq,
    wo,
    wu,
    wd,
    hidden,
    mask,
    acc,
    low_1,
    active_1,
    slope_1,
    sems,
):
    sec = place_ref[0]
    near_0 = sec == 0
    near_1 = sec == 1
    wait_up = fetch(near_0, wu_m, wu_o, wu, sems.at[0])
    wait_down = fetch(near_0, wd_m, wd_o, wd, sems.at[1])
    wait_pos = fetch(near_1, pos_m, pos_o, pos, sems.at[2])
    wait_qkv = fetch(near_1, wq_m, wq_o, wq, sems.at[3])
    wait_out = fetch(near_1, wo_m, wo_o, wo, sems.at[4])
    wait_cotangent = copy(cotangent.at[sec], arriving, sems.at[5])
    write_mask(place_ref, mask)
    small_0 = chosen(near_0, vec_m, vec_o)
    small_1 = chosen(near_1, vec_m, vec_o)
    sum_two = feed(
        small_0, sum_one_0[...], wu, wd, acc, low_0, active_0, slope_0, wait_up, wait_down
    )
    sum_two_0[...] = sum_two
    wait_up = fetch(near_1, wu_m, wu_o, wu, sems.at[0])
    wait_down = fetch(near_1, wd_m, wd_o, wd, sems.at[1])
    wait_pos()
    wait_qkv()
    normed, _ = normalize(sum_two)
    result = (normed * small_0[4:5] + small_0[5:6]).astype(BF16)
    position = pos[...].astype(F32)
    for w in range(2):
        rows = window_rows(w)
        stream_1[w] = result[rows]
        hidden[rows, :] = result[rows].astype(F32) + position
    project_rows(hidden[...].astype(BF16), wq, project_1)
    attend(mask, project_1, probs_1, mixed_1)
    wait_out()
    wait_cotangent()
    sum_one = hidden[...] + nn(mixed_1[...], wo[...])
    sum_one_1[...] = sum_one
    sum_two = feed(
        small_1, sum_one, wu, wd, acc, low_1, active_1, slope_1, wait_up, wait_down
    )
    normed, _ = normalize(sum_two)
    result = normed * small_1[4:5] + small_1[5:6]
    upstream = []
    for w in range(2):
        output[w] = unused_zeroed(place_ref, w, result[window_rows(w)]).astype(BF16)
        upstream.append(unused_zeroed(place_ref, w, arriving[w].astype(F32)))
    e = jnp.concatenate(upstream, 0)
    feed_back(
        sec, small_1, e, sum_two, wu, wd, acc, low_1, active_1, slope_1, small_grads, grads, send
    )
    grad_after[...] = acc[...]


def forward_middle(place, cotangent, mine, other, sum_one):
    args = [place, cotangent]
    for a, b in zip(mine, other):
        args += [a, b]
    return pl.pallas_call(
        middle_kernel,
        out_shape=FEED_KEPT
        + [sds((2, WIN, D), BF16)]
        + ATTENTION_KEPT
        + [sds((2, WIN, D), BF16)]
        + FFN_GRADS,
        in_specs=[SM, HBM] + [HBM, ANY] * 5 + [VM] * 3,
        out_specs=[VM] * 14,
        scratch_shapes=[
            pltpu.VMEM((2, WIN, D), BF16),
            pltpu.VMEM((WIN, D), BF16),
            pltpu.VMEM((D, 3 * D), BF16),
            pltpu.VMEM((D, D), BF16),
            pltpu.VMEM((D, FF), BF16),
            pltpu.VMEM((FF, D), BF16),
            pltpu.VMEM((ROWS, D), F32),
            pltpu.VMEM((2, WIN, WIN), F32),
            pltpu.VMEM((ROWS, D), F32),
            pltpu.VMEM((ROWS, D), BF16),
            pltpu.VMEM((ROWS, FF), BF16),
            pltpu.VMEM((ROWS, FF), BF16),
            DMA((6,)),
        ],
        compiler_params=limit(MIDDLE_LIMIT),
        cost_estimate=HEAVY,
        name="feed_0_to_feed_backward_1",
    )(*args, sum_one)


MIDDLE_LIMIT = 23


def out_kernel(
    layer,
    place_ref,
    wo_m,
    wo_o,
    vec_m,
    vec_o,
    grad_after,
    sum_one,
    mixed,
    small_in,
    grad_sum_ref,
    grad_mixed,
    grad_out,
    rows_ref,
    wo,
    sem,
):
    near = place_ref[0] == layer
    wait_out = fetch(near, wo_m, wo_o, wo, sem)
    small = chosen(near, vec_m, vec_o)
    normed, inverse = normalize(sum_one[...] + small[0:1])
    e = grad_after[...]
    row_norm = jnp.sum(e * normed, 0, keepdims=True)
    row_shift = jnp.sum(e, 0, keepdims=True)
    grad_sum = norm_backward(e, normed, inverse, small[1:2])
    grad_sum_ref[...] = grad_sum
    branch = grad_sum.astype(BF16)
    row_out = jnp.sum(branch.astype(F32), 0, keepdims=True)
    rows = jnp.concatenate([row_out, row_norm, row_shift, jnp.zeros((5, D), F32)], 0)
    rows_ref[...] = jnp.concatenate([rows, small_in[...]], 0).astype(BF16)
    wait_out()
    grad_mixed[...] = nt(branch, wo[...]).astype(BF16)
    grad_out[...] = tn(mixed[...], branch).astype(BF16)


def out_back(layer, place, mine, other, grad_after, kept, small):
    def body(*refs):
        out_kernel(layer, *refs)

    return pl.pallas_call(
        body,
        out_shape=[
            sds((ROWS, D), F32),
            sds((ROWS, D), BF16),
            sds((D, D), BF16),
            sds((16, D), BF16),
        ],
        in_specs=[SM, HBM, ANY] + [VM] * 6,
        out_specs=[VM] * 4,
        scratch_shapes=[pltpu.VMEM((D, D), BF16), DMA],
        compiler_params=limit(8),
        cost_estimate=HEAVY,
        name=f"projection_backward_{layer}",
    )(place, mine[2], other[2], mine[5], other[5], grad_after, kept[3], kept[2], small)


def late_kernel(
    place_ref,
    pos_m,
    pos_o,
    wq_m,
    wq_o,
    wu_m,
    wu_o,
    wd_m,
    wd_o,
    vec_m,
    vec_o,
    stream_1,
    project_1,
    probs_1,
    grad_sum,
    grad_mixed,
    grad_out,
    rows_1,
    low_0,
    active_0,
    slope_0,
    sum_two_0,
    att_grads,
    att_send,
    grad_after,
    small_grads,
    ffn_grads,
    ffn_send,
    pos,
    wq,
    wu,
    wd,
    grad_project,
    total,
    sems,
):
    sec = place_ref[0]
    wait_qkv = fetch(sec == 1, wq_m, wq_o, wq, sems.at[0])
    wait_pos = fetch(sec == 1, pos_m, pos_o, pos, sems.at[1])
    wait_down = fetch(sec == 0, wd_m, wd_o, wd, sems.at[2])
    wait_up = fetch(sec == 0, wu_m, wu_o, wu, sems.at[3])
    small = chosen(sec == 0, vec_m, vec_o)
    attend_back(project_1, probs_1, grad_mixed, grad_project)
    wait_qkv()
    wait_pos()
    wait_down()
    wait_up()
    input_back(
        sec, stream_1, pos, wq, grad_sum, grad_out, rows_1, grad_project, total, att_grads, att_send
    )
    e = total[...].astype(BF16).astype(F32)
    feed_back(
        sec,
        small,
        e,
        sum_two_0[...],
        wu,
        wd,
        total,
        low_0,
        active_0,
        slope_0,
        small_grads,
        ffn_grads,
        ffn_send,
    )
    grad_after[...] = total[...]


def late_back(place, mine, other, stream, attention, before, feed_kept):
    args = [place]
    for i in (0, 1, 3, 4, 5):
        args += [mine[i], other[i]]
    return pl.pallas_call(
        late_kernel,
        out_shape=ATT_GRADS + FFN_GRADS,
        in_specs=[SM] + [HBM, ANY] * 4 + [VM] * 13,
        out_specs=[VM] * 6,
        scratch_shapes=[
            pltpu.VMEM((WIN, D), BF16),
            pltpu.VMEM((D, 3 * D), BF16),
            pltpu.VMEM((D, FF), BF16),
            pltpu.VMEM((FF, D), BF16),
            pltpu.VMEM((ROWS, 3 * D), BF16),
            pltpu.VMEM((ROWS, D), F32),
            DMA((4,)),
        ],
        compiler_params=limit(21),
        cost_estimate=HEAVY,
        name="attention_backward_1_and_feed_backward_0",
    )(*args, stream, attention[0], attention[1], *before, *feed_kept)


def last_kernel(
    place_ref,
    tokens,
    pos_m,
    pos_o,
    wq_m,
    wq_o,
    project,
    probs,
    grad_sum,
    grad_mixed,
    grad_out,
    rows,
    grad_low,
    grads,
    send,
    stream,
    pos,
    wq,
    grad_project,
    total,
    sems,
):
    sec = place_ref[0]
    wait_qkv = fetch(sec == 0, wq_m, wq_o, wq, sems.at[0])
    wait_pos = fetch(sec == 0, pos_m, pos_o, pos, sems.at[1])
    wait_stream = copy(tokens.at[sec], stream, sems.at[2])
    attend_back(project, probs, grad_mixed, grad_project)
    wait_qkv()
    wait_pos()
    wait_stream()
    input_back(
        sec, stream, pos, wq, grad_sum, grad_out, rows, grad_project, total, grads, send
    )
    for w in range(2):
        grad_low[w] = total[window_rows(w), :].astype(BF16)


def last_back(place, tokens, mine, other, attention, before):
    args = [place, tokens]
    for i in (0, 1):
        args += [mine[i], other[i]]
    return pl.pallas_call(
        last_kernel,
        out_shape=[sds((2, WIN, D), BF16)] + ATT_GRADS,
        in_specs=[SM, HBM] + [HBM, ANY] * 2 + [VM] * 6,
        out_specs=[VM] * 3,
        scratch_shapes=[
            pltpu.VMEM((2, WIN, D), BF16),
            pltpu.VMEM((WIN, D), BF16),
            pltpu.VMEM((D, 3 * D), BF16),
            pltpu.VMEM((ROWS, 3 * D), BF16),
            pltpu.VMEM((ROWS, D), F32),
            DMA((3,)),
        ],
        compiler_params=limit(14),
        cost_estimate=HEAVY,
        name="attention_backward_0",
    )(*args, attention[0], attention[1], *before)


def pack_vectors(b_out, gain_one, shift_one, b_down, gain_two, shift_two, b_up):
    def body(*refs):
        out = refs[-1]
        rows = [ref[...].astype(F32) for ref in refs[:6]]
        wide = refs[6][...].astype(F32)
        rows += [wide[:, c * D : (c + 1) * D] for c in range(4)]
        rows += [jnp.zeros((6, D), F32)]
        out[...] = jnp.concatenate(rows, 0).astype(BF16)

    return pl.pallas_call(
        body,
        out_shape=sds((16, D), BF16),
        in_specs=[VM] * 7,
        out_specs=VM,
        name="pack_vectors",
    )(b_out, gain_one, shift_one, b_down, gain_two, shift_two, b_up)


def plain(body, shapes, args, name, specs=None):
    return pl.pallas_call(
        body,
        out_shape=[sds(shape, BF16) for shape in shapes],
        in_specs=specs or [VM] * len(args),
        out_specs=[VM] * len(shapes),
        compiler_params=limit(8),
        cost_estimate=SLIGHT,
        name=name,
    )(*args)


def stage_order(place_ref):
    first = place_ref[0] == 0
    strides = [jnp.where(first, a, b) for a, b in zip(*WAY)]
    coords = [lax.rem(lax.div(place_ref[1], stride), 4) for stride in strides]

    def owner(*distances):
        return sum(
            lax.rem(coord + r, 4) * stride
            for coord, r, stride in zip(coords, distances, strides)
        )

    return owner


def pair_sum(place, *arrays):
    ranges = []
    for i in range(len(arrays) // 2):
        if arrays[2 * i + 1].shape[0] == 8192:
            ranges += [(i, 0, FFN_PART)]
        else:
            ranges += [(i, 0, 64), (i, EXTRA, 16)]
    part = sum(rows for _, _, rows in ranges)

    def body(place_ref, *refs):
        outs = refs[len(arrays) :]
        owner = stage_order(place_ref)
        sec = place_ref[0]
        for third in range(4):
            for second in range(4):
                for first in range(4):
                    dev = owner(first, second, third)
                    at = (second * 4 + first) * part
                    for i, base, rows in ranges:
                        src = pl.ds(pl.multiple_of(base + dev * rows, 16), rows)
                        total = refs[2 * i][sec, src, :].astype(F32)
                        total += refs[2 * i + 1][src, :].astype(F32)
                        outs[third][at : at + rows, :] = total.astype(BF16)
                        at += rows

    specs = [SM] + [VM] * len(arrays)
    return plain(body, [(16 * part, 128)] * 4, (place,) + arrays, "sum_of_two_cores", specs)


def add_four(refs, at):
    return sum(ref[at].astype(F32) for ref in refs)


def line_sum(*arrivals):
    rows = arrivals[0][0].shape[0] // 16
    count = len(arrivals)

    def body(*refs):
        outs = refs[4 * count :]
        for r in range(4):
            for first in range(4):
                at = (r * 4 + first) * rows
                for i in range(count):
                    total = add_four(refs[4 * i : 4 * i + 4], (slice(at, at + rows), slice(None)))
                    outs[r][first, i] = total.astype(BF16)

    args = sum(arrivals, [])
    return plain(body, [(4, count, rows, 128)] * 4, args, "sum_over_line")


def early_line_sum(late_ffn, mixed):
    def body(*refs):
        outs = refs[8:]
        for r in range(4):
            for first in range(4):
                i = r * 4 + first
                at = slice(i * FFN_PART, (i + 1) * FFN_PART)
                total = add_four(refs[0:4], (at, slice(None)))
                outs[r][first, 0:FFN_PART, :] = total.astype(BF16)
                at = slice(i * CHUNK, (i + 1) * CHUNK)
                total = add_four(refs[4:8], (at, slice(None)))
                outs[r][first, FFN_PART:, :] = total.astype(BF16)

    return plain(
        body, [(4, FFN_PART + CHUNK, 128)] * 4, late_ffn + mixed, "sum_over_line_early"
    )


def plane_sum(early, last):
    def body(*refs):
        outs = refs[8:]
        for first in range(4):
            total = add_four(refs[0:4], first).astype(BF16)
            outs[first][1, 0:FFN_PART, :] = total[0:FFN_PART]
            outs[first][0, 0:FFN_PART, :] = total[FFN_PART : 2 * FFN_PART]
            outs[first][1, FFN_PART:, :] = total[2 * FFN_PART :]
            outs[first][0, FFN_PART:, :] = add_four(refs[4:8], (first, 0)).astype(BF16)

    return plain(body, [(2, CHUNK, 128)] * 4, early + last, "sum_over_plane")


def cube_sum(place, pieces):
    def body(place_ref, *refs):
        sec = place_ref[0]
        refs[4][...] = add_four(refs[:4], sec).astype(BF16)
        refs[5][...] = add_four(refs[:4], 1 - sec).astype(BF16)

    specs = [SM] + [VM] * 4
    return plain(body, [(CHUNK, 128)] * 2, [place] + pieces, "sum_over_cube", specs)


def place_parts(place_ref, sources, targets, pos, small, ready, sems):
    wu_ref, wd_ref, wq_ref, wo_ref = targets
    sec = place_ref[0]
    owner = stage_order(place_ref)
    waits = []
    for n, (ref, third, second) in enumerate(sources):
        for step in range(8):
            dev = owner(step % 4, second + step // 4, third)
            slot = n * 8 + step

            def write(kind, rows, base, half, n=n, step=step, slot=slot, ref=ref):
                side = sec if half == 0 else 1 - sec
                ready[kind][slot] = ref[step, side, base : base + rows, :].astype(F32)
                return ready[kind].at[slot]

            def send(kind, src, dst, slot=slot):
                return pltpu.make_async_copy(src, dst, sems.at[kind, slot])

            def lanes(start):
                return pl.ds(pl.multiple_of(start * 128, 128), 128)

            block = lax.div(dev, 4)
            r = pl.multiple_of(lax.rem(dev, 4) * 128, 128)
            up = send(
                0, write(0, FFN_PART, 0, 0), wu_ref.at[0, pl.ds(r, FFN_PART), lanes(block)]
            )
            up.start()
            r = pl.multiple_of(lax.div(block, 4) * D + r, 128)
            down = send(
                1,
                write(1, FFN_PART, 0, 1),
                wd_ref.at[0, pl.ds(r, FFN_PART), lanes(lax.rem(block, 4))],
            )
            down.start()
            block = lax.div(dev, 8)
            rows = pl.ds(pl.multiple_of(lax.rem(dev, 8) * 64, 64), 64)
            first = send(2, write(2, 64, FFN_PART, 0), wq_ref.at[0, rows, lanes(block)])
            first.start()
            src = write(3, 64, FFN_PART, 1)

            @pl.when(block < 4)
            def _(src=src, rows=rows, block=block, send=send, lanes=lanes):
                send(3, src, wq_ref.at[0, rows, lanes(block + 8)]).start()

            @pl.when(block >= 4)
            def _(src=src, rows=rows, block=block, send=send, lanes=lanes):
                send(3, src, wo_ref.at[0, rows, lanes(block - 4)]).start()

            waits += [up, down, first, send(3, src, wq_ref.at[0, rows, lanes(block)])]
            for half in range(2):
                side = sec if half == 0 else 1 - sec
                extra = ref[step, side, FFN_PART + 64 : CHUNK, :].astype(F32)
                at = pl.multiple_of(half * 128 + lax.rem(dev, 16) * 8, 8)
                pos[pl.ds(at, 8), lanes(lax.div(dev, 16))] = extra[0:8]
                if half == 0:
                    small[pl.ds(pl.multiple_of(dev * 8, 8), 8), :] = extra[8:16]
    for copy_out in waits:
        copy_out.wait()


WEIGHT_GRADS = [
    sds((1, D, FF), F32),
    sds((1, FF, D), F32),
    sds((1, D, 3 * D), F32),
    sds((1, D, D), F32),
]
PLACED = [sds((WIN, D), F32), sds((64 * 8, 128), F32)]
VECTOR = sds((1, D), F32)
LAST = [sds((1, WIN, D), F32)] + [VECTOR] * 3 + [sds((1, FF), F32)] + [VECTOR] * 3


def place_gradients(place, sources, placed=(), final=False):
    count = len(sources)

    def body(place_ref, *refs):
        gathered = [(refs[i],) + sources[i][1:] for i in range(count)]
        refs = refs[count:]
        before, refs = refs[: len(placed)], refs[len(placed) :]
        targets, refs = refs[:4], refs[4:]
        if final:
            pos, bo, g1, s1, bu, bd, g2, s2, small = refs[:9]
            pos = pos.at[0]
            refs = refs[9:]
        else:
            pos, small = refs[:2]
            refs = refs[2:]
        if before:
            pos[...] = before[4][...]
            small[...] = before[5][...]
        place_parts(place_ref, gathered, targets, pos, small, refs[:4], refs[4])
        if not final:
            return
        for c in range(4):
            lane = slice(c * 128, (c + 1) * 128)
            at = c * 16
            for ref, row in ((bo, 0), (g1, 1), (s1, 2), (bd, 8), (g2, 9), (s2, 10)):
                ref[:, lane] = small[at + row : at + row + 1, :]
            for j in range(4):
                row = at + 11 + j
                bu[:, j * D + c * 128 : j * D + (c + 1) * 128] = small[row : row + 1, :]

    slots = 8 * count
    ready = [
        pltpu.VMEM((slots, FFN_PART, 128), F32),
        pltpu.VMEM((slots, FFN_PART, 128), F32),
        pltpu.VMEM((slots, 64, 128), F32),
        pltpu.VMEM((slots, 64, 128), F32),
        DMA((4, slots)),
    ]
    if final:
        ready = [pltpu.VMEM((64 * 8, 128), F32)] + ready
    outs = LAST if final else PLACED
    return pl.pallas_call(
        body,
        out_shape=WEIGHT_GRADS + outs,
        in_specs=[SM] + [VM] * count + ([HBM] * 4 + [VM] * 2 if placed else []),
        out_specs=[HBM] * 4 + [VM] * len(outs),
        scratch_shapes=ready,
        input_output_aliases={1 + count + i: i for i in range(4)} if placed else {},
        compiler_params=limit(12),
        cost_estimate=HEAVY,
        name="place_gradients",
    )(place, *[source[0] for source in sources], *placed)


def swap(value):
    return lax.ppermute(value, "section", [(0, 1), (1, 0)])


def from_ahead(value, stage, distance):
    pairs = []
    for section in range(2):
        stride = WAY[section][stage]
        for dst in range(64):
            at = dst // stride % 4
            src = dst + ((at + distance) % 4 - at) * stride
            pairs.append((section * 64 + src, section * 64 + dst))
    return lax.ppermute(value, ("section", "dp"), pairs)


def send_ahead(pieces, stage):
    return [pieces[0]] + [from_ahead(pieces[r], stage, 4 - r) for r in (1, 3, 2)]


def gather(chunk):
    line = jnp.stack([chunk] + [from_ahead(chunk, 0, r) for r in (1, 2, 3)])
    ahead = [from_ahead(line, 1, r) for r in (1, 2, 3)]
    own_a = jnp.concatenate([line, ahead[0]], 0)
    own_b = jnp.concatenate([ahead[1], ahead[2]], 0)
    next_a = from_ahead(own_a, 2, 1)
    prev_b = from_ahead(own_b, 2, 3)
    next_b = from_ahead(own_b, 2, 1)
    prev_a = from_ahead(own_a, 2, 3)
    far_a = from_ahead(next_a, 2, 1)
    far_b = from_ahead(prev_b, 2, 3)
    return own_a, own_b, next_a, next_b, far_a, far_b, prev_a, prev_b


def hold(*values):
    return tuple(pltpu.with_memory_space_constraint(value, pltpu.HBM) for value in values)


def shards(
    tokens,
    lengths,
    out_cotangent,
    pos_table,
    w_qkv,
    w_out,
    b_out,
    norm1_gain,
    norm1_bias,
    w_up,
    b_up,
    w_down,
    b_down,
    norm2_gain,
    norm2_bias,
):
    section = lax.axis_index("section")
    place = jnp.stack([section, lax.axis_index("dp")]).astype(jnp.int32)
    place = jnp.concatenate([place, lengths.reshape(4)])
    vec = pack_vectors(b_out, norm1_gain, norm1_bias, b_down, norm2_gain, norm2_bias, b_up)
    got_qkv = swap(w_qkv)
    got_pos = swap(pos_table)
    got_out = swap(w_out)
    late_up, late_down, got_qkv = lax.optimization_barrier((w_up, w_down, got_qkv))
    mine = hold(pos_table, w_qkv, w_out, w_up, w_down) + (vec,)
    other = (got_pos, got_qkv, got_out, swap(late_up), swap(late_down), swap(vec))
    tokens, out_cotangent = hold(tokens, out_cotangent)
    attention_0 = forward_first(place, tokens, mine, other)
    middle = forward_middle(place, out_cotangent, mine, other, attention_0[3])
    feed_0, stream, attention_1, output = middle[0:4], middle[4], middle[5:9], middle[9]
    after, small, ffn_both, ffn_send = middle[10:14]

    def tie(*values):
        return lax.optimization_barrier(values)

    ffn_got = swap(ffn_send)
    before = out_back(1, place, mine, other, after, attention_1, small)
    pieces = pair_sum(place, ffn_both, ffn_got)
    before, pieces = tie(before, pieces)
    late_ffn = send_ahead(pieces, 2)
    att_both, att_send, after, small, ffn_both, ffn_send = late_back(
        place, mine, other, stream, attention_1, before, feed_0
    )
    after, late_ffn = tie(after, late_ffn)
    att_got = swap(att_send)
    ffn_got = swap(ffn_send)
    before = out_back(0, place, mine, other, after, attention_0, small)
    pieces = pair_sum(place, ffn_both, ffn_got, att_both, att_got)
    before, pieces = tie(before, pieces)
    mixed = send_ahead(pieces, 2)
    arriving, att_both, att_send = last_back(place, tokens, mine, other, attention_0, before)
    att_send, mixed = tie(att_send, mixed)
    pieces = pair_sum(place, att_both, swap(att_send))
    early = send_ahead(early_line_sum(late_ffn, mixed), 1)
    last = send_ahead(line_sum(send_ahead(pieces, 2)), 1)
    pieces = plane_sum(early, last)
    own, others = cube_sum(place, send_ahead(pieces, 0))
    chunk = jnp.stack([own, swap(others)])
    own_a, own_b, next_a, next_b, far_a, far_b, prev_a, prev_b = gather(chunk)
    sources = [(own_a, 0, 0), (own_b, 0, 2), (next_a, 1, 0), (prev_b, 3, 2)]
    placed = place_gradients(place, sources)
    placed = place_gradients(place, [(next_b, 1, 2), (prev_a, 3, 0)], placed)
    up, down, qkv, out, position, bias, gain_one, shift_one, bias_up, bias_down, gain_two, shift_two = (
        place_gradients(place, [(far_a, 2, 0), (far_b, 2, 2)], placed, True)
    )
    return (
        output[None],
        arriving[None],
        position,
        qkv,
        out,
        bias,
        gain_one,
        shift_one,
        up,
        bias_up,
        down,
        bias_down,
        gain_two,
        shift_two,
    )


def solution(mesh):
    placed = (
        P(None, "dp", None, None),
        P(None, "dp"),
        P(None, "dp", None, None),
        P("section", None, None),
        P("section", None, None),
        P("section", None, None),
        P("section", None),
        P("section", None),
        P("section", None),
        P("section", None, None),
        P("section", None),
        P("section", None, None),
        P("section", None),
        P("section", None),
        P("section", None),
    )
    return jax.shard_map(
        shards,
        mesh=mesh,
        in_specs=placed,
        out_specs=(
            P("section", "dp", None, None),
            P("section", "dp", None, None),
            P("section", None, None),
            P("section", None, None),
            P("section", None, None),
            P("section", None),
            P("section", None),
            P("section", None),
            P("section", None, None),
            P("section", None),
            P("section", None, None),
            P("section", None),
            P("section", None),
            P("section", None),
        ),
        check_vma=False,
    )
```

```python
import jax
import jax.numpy as jnp
from jax import lax
from jax.experimental import pallas as pl
from jax.experimental.pallas import tpu as pltpu
from jax.sharding import PartitionSpec as P

D = 512
FF = 2048
WIN = 256
ROWS = 512
F32 = jnp.float32
BF16 = jnp.bfloat16

HBM = pl.BlockSpec(memory_space=pltpu.HBM)
ANY = pl.BlockSpec(memory_space=pl.ANY)
VM = pl.BlockSpec(memory_space=pltpu.VMEM)
SM = pl.BlockSpec(memory_space=pltpu.SMEM)
DMA = pltpu.SemaphoreType.DMA
SLIGHT = pl.CostEstimate(flops=1000, bytes_accessed=1000, transcendentals=0)
HEAVY = pl.CostEstimate(flops=35_000_000_000, bytes_accessed=1000, transcendentals=0)
EXTRA = 4096
FFN_PART = 128
ATT_PART = 80
CHUNK = FFN_PART + ATT_PART
WAY = ((16, 4, 1), (1, 16, 4))


def limit(mebibytes):
    return pltpu.CompilerParams(vmem_limit_bytes=mebibytes * 1024 * 1024)


def sds(shape, dtype):
    return jax.ShapeDtypeStruct(shape, dtype)


def nn(a, b):
    return lax.dot_general(a, b, (((1,), (0,)), ((), ())), preferred_element_type=F32)


def nt(a, b):
    return lax.dot_general(a, b, (((1,), (1,)), ((), ())), preferred_element_type=F32)


def tn(a, b):
    return lax.dot_general(a, b, (((0,), (0,)), ((), ())), preferred_element_type=F32)


def fetch(near, mine, other, dst, sem):
    @pl.when(near)
    def _():
        pltpu.make_async_copy(mine.at[0], dst, sem).start()

    @pl.when(jnp.logical_not(near))
    def _():
        pltpu.make_async_copy(other.at[0], dst, sem).start()

    return pltpu.make_async_copy(mine.at[0], dst, sem).wait


def copy(src, dst, sem):
    load = pltpu.make_async_copy(src, dst, sem)
    load.start()
    return load.wait


def chosen(near, mine, other):
    return jnp.where(near, mine[...].astype(F32), other[...].astype(F32))


def normalize(v):
    center = v - jnp.mean(v, -1, keepdims=True)
    inverse = lax.rsqrt(jnp.mean(center * center, -1, keepdims=True) + 1e-05)
    return center * inverse, inverse


def norm_backward(e, normed, inverse, gain):
    scaled = e * gain
    return inverse * (
        scaled
        - jnp.mean(scaled, -1, keepdims=True)
        - normed * jnp.mean(scaled * normed, -1, keepdims=True)
    )


def gelu_pair(v):
    c = 0.7978845608028654
    poly = c + (c * 0.044715) * (v * v)
    t = jnp.tanh(v * poly)
    half = 0.5 + 0.5 * t
    active = v * half
    return active, half + (active - active * t) * (3.0 * poly - 2.0 * c)


def used(place_ref, window):
    return place_ref[2 + 2 * place_ref[0] + window]


def write_mask(place_ref, mask):
    rows = lax.broadcasted_iota(jnp.int32, (WIN, WIN), 0)
    cols = lax.broadcasted_iota(jnp.int32, (WIN, WIN), 1)
    for w in range(2):
        inside = (cols <= rows) & (cols < used(place_ref, w))
        mask[w] = jnp.where(inside, 0.0, -1e30)


def window_rows(w):
    return slice(w * WIN, (w + 1) * WIN)


def unused_zeroed(place_ref, w, part):
    at_row = lax.broadcasted_iota(jnp.int32, (WIN, D), 0)
    return jnp.where(at_row < used(place_ref, w), part, 0.0)


def project_rows(hidden_low, wq, project):
    for c in range(3):
        at = slice(c * D, (c + 1) * D)
        project[:, at] = nn(hidden_low, wq[:, at]).astype(BF16)


def attend(mask, project, probs, mixed):
    lanes = lax.broadcasted_iota(jnp.int32, (WIN, 128), 1)
    for step in range(8):
        w, p = step // 4, step % 4
        rows = window_rows(w)
        at = [slice(j * D + p * 128, j * D + (p + 1) * 128) for j in range(3)]
        q2 = project[rows, at[0]] * jnp.asarray(0.125, BF16)
        k2 = project[rows, at[1]]
        v2 = project[rows, at[2]]
        blocked = mask[w]
        parts = []
        for h in range(2):
            own = (lanes >= 64) if h else (lanes < 64)
            qm = jnp.where(own, q2, jnp.zeros_like(q2))
            scores = nt(qm, k2) + blocked
            raised = jnp.exp(scores - jnp.max(scores, -1, keepdims=True))
            soft = (raised * (1.0 / jnp.sum(raised, -1, keepdims=True))).astype(BF16)
            probs[step * 2 + h] = soft
            parts.append(nn(soft, v2))
        mixed[rows, at[0]] = jnp.where(lanes < 64, parts[0], parts[1]).astype(BF16)


def attend_back(project, probs, grad_mixed, grad_project):
    lanes = lax.broadcasted_iota(jnp.int32, (WIN, 128), 1)
    for step in range(8):
        w, p = step // 4, step % 4
        rows = window_rows(w)
        at = [slice(j * D + p * 128, j * D + (p + 1) * 128) for j in range(3)]
        q2 = project[rows, at[0]] * jnp.asarray(0.125, BF16)
        k2 = project[rows, at[1]]
        v2 = project[rows, at[2]]
        g2 = grad_mixed[rows, at[0]]
        grad_q, grad_k, grad_v = [], [], []
        for h in range(2):
            own = (lanes >= 64) if h else (lanes < 64)
            none = jnp.zeros_like(q2)
            gm = jnp.where(own, g2, none)
            qm = jnp.where(own, q2, none)
            soft_low = probs[step * 2 + h]
            soft = soft_low.astype(F32)
            product = soft * nt(gm, v2)
            grad_scores = (product - soft * jnp.sum(product, -1, keepdims=True)).astype(BF16)
            grad_q.append(nn(grad_scores, k2))
            grad_k.append(tn(grad_scores, qm))
            grad_v.append(tn(soft_low, gm))
        grad_project[rows, at[0]] = (
            jnp.where(lanes < 64, grad_q[0], grad_q[1]) * 0.125
        ).astype(BF16)
        grad_project[rows, at[1]] = (grad_k[0] + grad_k[1]).astype(BF16)
        grad_project[rows, at[2]] = (grad_v[0] + grad_v[1]).astype(BF16)


def feed(small, sum_one, wu, wd, acc, low_ref, active_ref, slope_ref, wait_up, wait_down):
    normed, _ = normalize(sum_one + small[0:1])
    after = normed * small[1:2] + small[2:3]
    acc[...] = after
    low = after.astype(BF16)
    low_ref[...] = low
    wait_up()
    for c in range(4):
        block = slice(c * D, (c + 1) * D)
        value = nn(low, wu[:, block]) + small[6 + c : 7 + c]
        active, slope = gelu_pair(value)
        active = active.astype(BF16)
        active_ref[:, block] = active
        slope_ref[:, block] = slope.astype(BF16)
    wait_down()
    return acc[...] + (nn(active_ref[...], wd[...]) + small[3:4])


def feed_back(
    sec, small, e, sum_two, wu, wd, acc, low_ref, active_ref, slope_ref, small_ref, grads, send
):
    normed, inverse = normalize(sum_two)
    small_ref[...] = jnp.zeros_like(small_ref)
    small_ref[1:2, :] = jnp.sum(e * normed, 0, keepdims=True)
    small_ref[2:3, :] = jnp.sum(e, 0, keepdims=True)
    grad_sum = norm_backward(e, normed, inverse, small[4:5])
    acc[...] = grad_sum
    grad_low = grad_sum.astype(BF16)
    small_ref[0:1, :] = jnp.sum(grad_low.astype(F32), 0, keepdims=True)
    for c in range(4):
        block = slice(c * D, (c + 1) * D)
        grad_up = nt(grad_low, wd[block, :]) * slope_ref[:, block].astype(F32)
        grad_up = grad_up.astype(BF16)
        small_ref[3 + c : 4 + c, :] = jnp.sum(grad_up.astype(F32), 0, keepdims=True)
        slope_ref[:, block] = grad_up
        grad_wu = tn(low_ref[...], grad_up).astype(BF16)
        grad_wd = tn(active_ref[:, block], grad_low).astype(BF16)
        for k in range(4):
            at = slice((c * 4 + k) * D, (c * 4 + k + 1) * D)
            grads[0, at, :] = grad_wu[:, k * 128 : (k + 1) * 128]
            grads[1, at, :] = grad_wd[:, k * 128 : (k + 1) * 128]
    acc[...] += nt(slope_ref[...], wu[...])
    send[...] = grads[1 - sec]


def input_back(
    sec, stream, pos, wq, grad_sum, grad_out, rows, grad_project, total, grads, send
):
    for c in range(4):
        grads[1, 2048 + c * D : 2048 + (c + 1) * D, :] = grad_out[:, c * 128 : (c + 1) * 128]
    position = pos[...].astype(F32)
    hidden_low = jnp.concatenate(
        [(stream[w].astype(F32) + position).astype(BF16) for w in range(2)], 0
    )
    total[...] = grad_sum[...]
    for j in range(3):
        block = slice(j * D, (j + 1) * D)
        part = grad_project[:, block]
        total[...] += nt(part, wq[:, block])
        grad_w = tn(hidden_low, part).astype(BF16)
        half, base = ((0, 0), (0, 2048), (1, 0))[j]
        for c in range(4):
            grads[half, base + c * D : base + (c + 1) * D, :] = grad_w[:, c * 128 : (c + 1) * 128]
    grad_pos = total[0:WIN, :] + total[WIN : 2 * WIN, :]
    small = rows[...].astype(F32)
    blank = jnp.zeros((8, 128), F32)
    for c in range(4):
        lanes_at = slice(c * 128, (c + 1) * 128)
        for half in range(2):
            extra = []
            for i in range(16):
                at = half * 128 + i * 8
                extra.append(grad_pos[at : at + 8, lanes_at])
                if c == 0 and i < 8:
                    extra.append(small[i % 2 * 8 : i % 2 * 8 + 8, i // 2 * 128 : i // 2 * 128 + 128])
                else:
                    extra.append(blank)
            at = EXTRA + c * WIN
            grads[half, at : at + WIN, :] = jnp.concatenate(extra, 0).astype(BF16)
    send[...] = grads[1 - sec]


def first_kernel(
    place_ref,
    tokens,
    pos_m,
    pos_o,
    wq_m,
    wq_o,
    wo_m,
    wo_o,
    project,
    probs,
    mixed,
    sum_one,
    stream,
    pos,
    wq,
    wo,
    hidden,
    mask,
    sems,
):
    sec = place_ref[0]
    wait_stream = copy(tokens.at[sec], stream, sems.at[0])
    wait_pos = fetch(sec == 0, pos_m, pos_o, pos, sems.at[1])
    wait_qkv = fetch(sec == 0, wq_m, wq_o, wq, sems.at[2])
    wait_out = fetch(sec == 0, wo_m, wo_o, wo, sems.at[3])
    write_mask(place_ref, mask)
    wait_stream()
    wait_pos()
    position = pos[...].astype(F32)
    for w in range(2):
        hidden[window_rows(w), :] = stream[w].astype(F32) + position
    wait_qkv()
    wait_out()
    project_rows(hidden[...].astype(BF16), wq, project)
    attend(mask, project, probs, mixed)
    sum_one[...] = hidden[...] + nn(mixed[...], wo[...])


ATTENTION_KEPT = [
    sds((ROWS, 3 * D), BF16),
    sds((16, WIN, WIN), BF16),
    sds((ROWS, D), BF16),
    sds((ROWS, D), F32),
]
FEED_KEPT = [
    sds((ROWS, D), BF16),
    sds((ROWS, FF), BF16),
    sds((ROWS, FF), BF16),
    sds((ROWS, D), F32),
]
FFN_GRADS = [
    sds((ROWS, D), F32),
    sds((8, D), F32),
    sds((2, 8192, 128), BF16),
    sds((8192, 128), BF16),
]
ATT_GRADS = [sds((2, 5120, 128), BF16), sds((5120, 128), BF16)]


def forward_first(place, tokens, mine, other):
    args = [place, tokens]
    for i in (0, 1, 2):
        args += [mine[i], other[i]]
    return pl.pallas_call(
        first_kernel,
        out_shape=ATTENTION_KEPT,
        in_specs=[SM, HBM] + [HBM, ANY] * 3,
        out_specs=[VM] * 4,
        scratch_shapes=[
            pltpu.VMEM((2, WIN, D), BF16),
            pltpu.VMEM((WIN, D), BF16),
            pltpu.VMEM((D, 3 * D), BF16),
            pltpu.VMEM((D, D), BF16),
            pltpu.VMEM((ROWS, D), F32),
            pltpu.VMEM((2, WIN, WIN), F32),
            DMA((4,)),
        ],
        compiler_params=limit(12),
        cost_estimate=HEAVY,
        name="forward_attention_0",
    )(*args)


def middle_kernel(
    place_ref,
    cotangent,
    pos_m,
    pos_o,
    wq_m,
    wq_o,
    wo_m,
    wo_o,
    wu_m,
    wu_o,
    wd_m,
    wd_o,
    vec_m,
    vec_o,
    sum_one_0,
    low_0,
    active_0,
    slope_0,
    sum_two_0,
    stream_1,
    project_1,
    probs_1,
    mixed_1,
    sum_one_1,
    output,
    grad_after,
    small_grads,
    grads,
    send,
    arriving,
    pos,
    wq,
    wo,
    wu,
    wd,
    hidden,
    mask,
    acc,
    low_1,
    active_1,
    slope_1,
    sems,
):
    sec = place_ref[0]
    near_0 = sec == 0
    near_1 = sec == 1
    wait_up = fetch(near_0, wu_m, wu_o, wu, sems.at[0])
    wait_down = fetch(near_0, wd_m, wd_o, wd, sems.at[1])
    wait_pos = fetch(near_1, pos_m, pos_o, pos, sems.at[2])
    wait_qkv = fetch(near_1, wq_m, wq_o, wq, sems.at[3])
    wait_out = fetch(near_1, wo_m, wo_o, wo, sems.at[4])
    wait_cotangent = copy(cotangent.at[sec], arriving, sems.at[5])
    write_mask(place_ref, mask)
    small_0 = chosen(near_0, vec_m, vec_o)
    small_1 = chosen(near_1, vec_m, vec_o)
    sum_two = feed(
        small_0, sum_one_0[...], wu, wd, acc, low_0, active_0, slope_0, wait_up, wait_down
    )
    sum_two_0[...] = sum_two
    wait_up = fetch(near_1, wu_m, wu_o, wu, sems.at[0])
    wait_down = fetch(near_1, wd_m, wd_o, wd, sems.at[1])
    wait_pos()
    wait_qkv()
    normed, _ = normalize(sum_two)
    result = (normed * small_0[4:5] + small_0[5:6]).astype(BF16)
    position = pos[...].astype(F32)
    for w in range(2):
        rows = window_rows(w)
        stream_1[w] = result[rows]
        hidden[rows, :] = result[rows].astype(F32) + position
    project_rows(hidden[...].astype(BF16), wq, project_1)
    attend(mask, project_1, probs_1, mixed_1)
    wait_out()
    wait_cotangent()
    sum_one = hidden[...] + nn(mixed_1[...], wo[...])
    sum_one_1[...] = sum_one
    sum_two = feed(
        small_1, sum_one, wu, wd, acc, low_1, active_1, slope_1, wait_up, wait_down
    )
    normed, _ = normalize(sum_two)
    result = normed * small_1[4:5] + small_1[5:6]
    upstream = []
    for w in range(2):
        output[w] = unused_zeroed(place_ref, w, result[window_rows(w)]).astype(BF16)
        upstream.append(unused_zeroed(place_ref, w, arriving[w].astype(F32)))
    e = jnp.concatenate(upstream, 0)
    feed_back(
        sec, small_1, e, sum_two, wu, wd, acc, low_1, active_1, slope_1, small_grads, grads, send
    )
    grad_after[...] = acc[...]


def forward_middle(place, cotangent, mine, other, sum_one):
    args = [place, cotangent]
    for a, b in zip(mine, other):
        args += [a, b]
    return pl.pallas_call(
        middle_kernel,
        out_shape=FEED_KEPT
        + [sds((2, WIN, D), BF16)]
        + ATTENTION_KEPT
        + [sds((2, WIN, D), BF16)]
        + FFN_GRADS,
        in_specs=[SM, HBM] + [HBM, ANY] * 5 + [VM] * 3,
        out_specs=[VM] * 14,
        scratch_shapes=[
            pltpu.VMEM((2, WIN, D), BF16),
            pltpu.VMEM((WIN, D), BF16),
            pltpu.VMEM((D, 3 * D), BF16),
            pltpu.VMEM((D, D), BF16),
            pltpu.VMEM((D, FF), BF16),
            pltpu.VMEM((FF, D), BF16),
            pltpu.VMEM((ROWS, D), F32),
            pltpu.VMEM((2, WIN, WIN), F32),
            pltpu.VMEM((ROWS, D), F32),
            pltpu.VMEM((ROWS, D), BF16),
            pltpu.VMEM((ROWS, FF), BF16),
            pltpu.VMEM((ROWS, FF), BF16),
            DMA((6,)),
        ],
        compiler_params=limit(MIDDLE_LIMIT),
        cost_estimate=HEAVY,
        name="feed_0_to_feed_backward_1",
    )(*args, sum_one)


MIDDLE_LIMIT = 23


def out_kernel(
    layer,
    place_ref,
    wo_m,
    wo_o,
    vec_m,
    vec_o,
    grad_after,
    sum_one,
    mixed,
    small_in,
    grad_sum_ref,
    grad_mixed,
    grad_out,
    rows_ref,
    wo,
    sem,
):
    near = place_ref[0] == layer
    wait_out = fetch(near, wo_m, wo_o, wo, sem)
    small = chosen(near, vec_m, vec_o)
    normed, inverse = normalize(sum_one[...] + small[0:1])
    e = grad_after[...]
    row_norm = jnp.sum(e * normed, 0, keepdims=True)
    row_shift = jnp.sum(e, 0, keepdims=True)
    grad_sum = norm_backward(e, normed, inverse, small[1:2])
    grad_sum_ref[...] = grad_sum
    branch = grad_sum.astype(BF16)
    row_out = jnp.sum(branch.astype(F32), 0, keepdims=True)
    rows = jnp.concatenate([row_out, row_norm, row_shift, jnp.zeros((5, D), F32)], 0)
    rows_ref[...] = jnp.concatenate([rows, small_in[...]], 0).astype(BF16)
    wait_out()
    grad_mixed[...] = nt(branch, wo[...]).astype(BF16)
    grad_out[...] = tn(mixed[...], branch).astype(BF16)


def out_back(layer, place, mine, other, grad_after, kept, small):
    def body(*refs):
        out_kernel(layer, *refs)

    return pl.pallas_call(
        body,
        out_shape=[
            sds((ROWS, D), F32),
            sds((ROWS, D), BF16),
            sds((D, D), BF16),
            sds((16, D), BF16),
        ],
        in_specs=[SM, HBM, ANY] + [VM] * 6,
        out_specs=[VM] * 4,
        scratch_shapes=[pltpu.VMEM((D, D), BF16), DMA],
        compiler_params=limit(8),
        cost_estimate=HEAVY,
        name=f"projection_backward_{layer}",
    )(place, mine[2], other[2], mine[5], other[5], grad_after, kept[3], kept[2], small)


def late_kernel(
    place_ref,
    pos_m,
    pos_o,
    wq_m,
    wq_o,
    wu_m,
    wu_o,
    wd_m,
    wd_o,
    vec_m,
    vec_o,
    stream_1,
    project_1,
    probs_1,
    grad_sum,
    grad_mixed,
    grad_out,
    rows_1,
    low_0,
    active_0,
    slope_0,
    sum_two_0,
    att_grads,
    att_send,
    grad_after,
    small_grads,
    ffn_grads,
    ffn_send,
    pos,
    wq,
    wu,
    wd,
    grad_project,
    total,
    sems,
):
    sec = place_ref[0]
    wait_qkv = fetch(sec == 1, wq_m, wq_o, wq, sems.at[0])
    wait_pos = fetch(sec == 1, pos_m, pos_o, pos, sems.at[1])
    wait_down = fetch(sec == 0, wd_m, wd_o, wd, sems.at[2])
    wait_up = fetch(sec == 0, wu_m, wu_o, wu, sems.at[3])
    small = chosen(sec == 0, vec_m, vec_o)
    attend_back(project_1, probs_1, grad_mixed, grad_project)
    wait_qkv()
    wait_pos()
    wait_down()
    wait_up()
    input_back(
        sec, stream_1, pos, wq, grad_sum, grad_out, rows_1, grad_project, total, att_grads, att_send
    )
    e = total[...].astype(BF16).astype(F32)
    feed_back(
        sec,
        small,
        e,
        sum_two_0[...],
        wu,
        wd,
        total,
        low_0,
        active_0,
        slope_0,
        small_grads,
        ffn_grads,
        ffn_send,
    )
    grad_after[...] = total[...]


def late_back(place, mine, other, stream, attention, before, feed_kept):
    args = [place]
    for i in (0, 1, 3, 4, 5):
        args += [mine[i], other[i]]
    return pl.pallas_call(
        late_kernel,
        out_shape=ATT_GRADS + FFN_GRADS,
        in_specs=[SM] + [HBM, ANY] * 4 + [VM] * 13,
        out_specs=[VM] * 6,
        scratch_shapes=[
            pltpu.VMEM((WIN, D), BF16),
            pltpu.VMEM((D, 3 * D), BF16),
            pltpu.VMEM((D, FF), BF16),
            pltpu.VMEM((FF, D), BF16),
            pltpu.VMEM((ROWS, 3 * D), BF16),
            pltpu.VMEM((ROWS, D), F32),
            DMA((4,)),
        ],
        compiler_params=limit(21),
        cost_estimate=HEAVY,
        name="attention_backward_1_and_feed_backward_0",
    )(*args, stream, attention[0], attention[1], *before, *feed_kept)


def last_kernel(
    place_ref,
    tokens,
    pos_m,
    pos_o,
    wq_m,
    wq_o,
    project,
    probs,
    grad_sum,
    grad_mixed,
    grad_out,
    rows,
    grad_low,
    grads,
    send,
    stream,
    pos,
    wq,
    grad_project,
    total,
    sems,
):
    sec = place_ref[0]
    wait_qkv = fetch(sec == 0, wq_m, wq_o, wq, sems.at[0])
    wait_pos = fetch(sec == 0, pos_m, pos_o, pos, sems.at[1])
    wait_stream = copy(tokens.at[sec], stream, sems.at[2])
    attend_back(project, probs, grad_mixed, grad_project)
    wait_qkv()
    wait_pos()
    wait_stream()
    input_back(
        sec, stream, pos, wq, grad_sum, grad_out, rows, grad_project, total, grads, send
    )
    for w in range(2):
        grad_low[w] = total[window_rows(w), :].astype(BF16)


def last_back(place, tokens, mine, other, attention, before):
    args = [place, tokens]
    for i in (0, 1):
        args += [mine[i], other[i]]
    return pl.pallas_call(
        last_kernel,
        out_shape=[sds((2, WIN, D), BF16)] + ATT_GRADS,
        in_specs=[SM, HBM] + [HBM, ANY] * 2 + [VM] * 6,
        out_specs=[VM] * 3,
        scratch_shapes=[
            pltpu.VMEM((2, WIN, D), BF16),
            pltpu.VMEM((WIN, D), BF16),
            pltpu.VMEM((D, 3 * D), BF16),
            pltpu.VMEM((ROWS, 3 * D), BF16),
            pltpu.VMEM((ROWS, D), F32),
            DMA((3,)),
        ],
        compiler_params=limit(14),
        cost_estimate=HEAVY,
        name="attention_backward_0",
    )(*args, attention[0], attention[1], *before)


def pack_vectors(b_out, gain_one, shift_one, b_down, gain_two, shift_two, b_up):
    def body(*refs):
        out = refs[-1]
        rows = [ref[...].astype(F32) for ref in refs[:6]]
        wide = refs[6][...].astype(F32)
        rows += [wide[:, c * D : (c + 1) * D] for c in range(4)]
        rows += [jnp.zeros((6, D), F32)]
        out[...] = jnp.concatenate(rows, 0).astype(BF16)

    return pl.pallas_call(
        body,
        out_shape=sds((16, D), BF16),
        in_specs=[VM] * 7,
        out_specs=VM,
        name="pack_vectors",
    )(b_out, gain_one, shift_one, b_down, gain_two, shift_two, b_up)


def plain(body, shapes, args, name, specs=None):
    return pl.pallas_call(
        body,
        out_shape=[sds(shape, BF16) for shape in shapes],
        in_specs=specs or [VM] * len(args),
        out_specs=[VM] * len(shapes),
        compiler_params=limit(8),
        cost_estimate=SLIGHT,
        name=name,
    )(*args)


def stage_order(place_ref):
    first = place_ref[0] == 0
    strides = [jnp.where(first, a, b) for a, b in zip(*WAY)]
    coords = [lax.rem(lax.div(place_ref[1], stride), 4) for stride in strides]

    def owner(*distances):
        return sum(
            lax.rem(coord + r, 4) * stride
            for coord, r, stride in zip(coords, distances, strides)
        )

    return owner


def pair_sum(place, *arrays):
    ranges = []
    for i in range(len(arrays) // 2):
        if arrays[2 * i + 1].shape[0] == 8192:
            ranges += [(i, 0, FFN_PART)]
        else:
            ranges += [(i, 0, 64), (i, EXTRA, 16)]
    part = sum(rows for _, _, rows in ranges)

    def body(place_ref, *refs):
        outs = refs[len(arrays) :]
        owner = stage_order(place_ref)
        sec = place_ref[0]
        for third in range(4):
            for second in range(4):
                for first in range(4):
                    dev = owner(first, second, third)
                    at = (second * 4 + first) * part
                    for i, base, rows in ranges:
                        src = pl.ds(pl.multiple_of(base + dev * rows, 16), rows)
                        total = refs[2 * i][sec, src, :].astype(F32)
                        total += refs[2 * i + 1][src, :].astype(F32)
                        outs[third][at : at + rows, :] = total.astype(BF16)
                        at += rows

    specs = [SM] + [VM] * len(arrays)
    return plain(body, [(16 * part, 128)] * 4, (place,) + arrays, "sum_of_two_cores", specs)


def add_four(refs, at):
    return sum(ref[at].astype(F32) for ref in refs)


def line_sum(*arrivals):
    rows = arrivals[0][0].shape[0] // 16
    count = len(arrivals)

    def body(*refs):
        outs = refs[4 * count :]
        for r in range(4):
            for first in range(4):
                at = (r * 4 + first) * rows
                for i in range(count):
                    total = add_four(refs[4 * i : 4 * i + 4], (slice(at, at + rows), slice(None)))
                    outs[r][first, i] = total.astype(BF16)

    args = sum(arrivals, [])
    return plain(body, [(4, count, rows, 128)] * 4, args, "sum_over_line")


def early_line_sum(late_ffn, mixed):
    def body(*refs):
        outs = refs[8:]
        for r in range(4):
            for first in range(4):
                i = r * 4 + first
                at = slice(i * FFN_PART, (i + 1) * FFN_PART)
                total = add_four(refs[0:4], (at, slice(None)))
                outs[r][first, 0:FFN_PART, :] = total.astype(BF16)
                at = slice(i * CHUNK, (i + 1) * CHUNK)
                total = add_four(refs[4:8], (at, slice(None)))
                outs[r][first, FFN_PART:, :] = total.astype(BF16)

    return plain(
        body, [(4, FFN_PART + CHUNK, 128)] * 4, late_ffn + mixed, "sum_over_line_early"
    )


def plane_sum(early, last):
    def body(*refs):
        outs = refs[8:]
        for first in range(4):
            total = add_four(refs[0:4], first).astype(BF16)
            outs[first][1, 0:FFN_PART, :] = total[0:FFN_PART]
            outs[first][0, 0:FFN_PART, :] = total[FFN_PART : 2 * FFN_PART]
            outs[first][1, FFN_PART:, :] = total[2 * FFN_PART :]
            outs[first][0, FFN_PART:, :] = add_four(refs[4:8], (first, 0)).astype(BF16)

    return plain(body, [(2, CHUNK, 128)] * 4, early + last, "sum_over_plane")


def cube_sum(place, pieces):
    def body(place_ref, *refs):
        sec = place_ref[0]
        refs[4][...] = add_four(refs[:4], sec).astype(BF16)
        refs[5][...] = add_four(refs[:4], 1 - sec).astype(BF16)

    specs = [SM] + [VM] * 4
    return plain(body, [(CHUNK, 128)] * 2, [place] + pieces, "sum_over_cube", specs)


def place_parts(place_ref, sources, targets, pos, small, ready, sems):
    wu_ref, wd_ref, wq_ref, wo_ref = targets
    sec = place_ref[0]
    owner = stage_order(place_ref)
    waits = []
    for n, (ref, third, second) in enumerate(sources):
        for step in range(8):
            dev = owner(step % 4, second + step // 4, third)
            slot = n * 8 + step

            def write(kind, rows, base, half, n=n, step=step, slot=slot, ref=ref):
                side = sec if half == 0 else 1 - sec
                ready[kind][slot] = ref[step, side, base : base + rows, :].astype(F32)
                return ready[kind].at[slot]

            def send(kind, src, dst, slot=slot):
                return pltpu.make_async_copy(src, dst, sems.at[kind, slot])

            def lanes(start):
                return pl.ds(pl.multiple_of(start * 128, 128), 128)

            block = lax.div(dev, 4)
            r = pl.multiple_of(lax.rem(dev, 4) * 128, 128)
            up = send(
                0, write(0, FFN_PART, 0, 0), wu_ref.at[0, pl.ds(r, FFN_PART), lanes(block)]
            )
            up.start()
            r = pl.multiple_of(lax.div(block, 4) * D + r, 128)
            down = send(
                1,
                write(1, FFN_PART, 0, 1),
                wd_ref.at[0, pl.ds(r, FFN_PART), lanes(lax.rem(block, 4))],
            )
            down.start()
            block = lax.div(dev, 8)
            rows = pl.ds(pl.multiple_of(lax.rem(dev, 8) * 64, 64), 64)
            first = send(2, write(2, 64, FFN_PART, 0), wq_ref.at[0, rows, lanes(block)])
            first.start()
            src = write(3, 64, FFN_PART, 1)

            @pl.when(block < 4)
            def _(src=src, rows=rows, block=block, send=send, lanes=lanes):
                send(3, src, wq_ref.at[0, rows, lanes(block + 8)]).start()

            @pl.when(block >= 4)
            def _(src=src, rows=rows, block=block, send=send, lanes=lanes):
                send(3, src, wo_ref.at[0, rows, lanes(block - 4)]).start()

            waits += [up, down, first, send(3, src, wq_ref.at[0, rows, lanes(block)])]
            for half in range(2):
                side = sec if half == 0 else 1 - sec
                extra = ref[step, side, FFN_PART + 64 : CHUNK, :].astype(F32)
                at = pl.multiple_of(half * 128 + lax.rem(dev, 16) * 8, 8)
                pos[pl.ds(at, 8), lanes(lax.div(dev, 16))] = extra[0:8]
                if half == 0:
                    small[pl.ds(pl.multiple_of(dev * 8, 8), 8), :] = extra[8:16]
    for copy_out in waits:
        copy_out.wait()


WEIGHT_GRADS = [
    sds((1, D, FF), F32),
    sds((1, FF, D), F32),
    sds((1, D, 3 * D), F32),
    sds((1, D, D), F32),
]
PLACED = [sds((WIN, D), F32), sds((64 * 8, 128), F32)]
VECTOR = sds((1, D), F32)
LAST = [sds((1, WIN, D), F32)] + [VECTOR] * 3 + [sds((1, FF), F32)] + [VECTOR] * 3


def place_gradients(place, sources, placed=(), final=False):
    count = len(sources)

    def body(place_ref, *refs):
        gathered = [(refs[i],) + sources[i][1:] for i in range(count)]
        refs = refs[count:]
        before, refs = refs[: len(placed)], refs[len(placed) :]
        targets, refs = refs[:4], refs[4:]
        if final:
            pos, bo, g1, s1, bu, bd, g2, s2, small = refs[:9]
            pos = pos.at[0]
            refs = refs[9:]
        else:
            pos, small = refs[:2]
            refs = refs[2:]
        if before:
            pos[...] = before[4][...]
            small[...] = before[5][...]
        place_parts(place_ref, gathered, targets, pos, small, refs[:4], refs[4])
        if not final:
            return
        for c in range(4):
            lane = slice(c * 128, (c + 1) * 128)
            at = c * 16
            for ref, row in ((bo, 0), (g1, 1), (s1, 2), (bd, 8), (g2, 9), (s2, 10)):
                ref[:, lane] = small[at + row : at + row + 1, :]
            for j in range(4):
                row = at + 11 + j
                bu[:, j * D + c * 128 : j * D + (c + 1) * 128] = small[row : row + 1, :]

    slots = 8 * count
    ready = [
        pltpu.VMEM((slots, FFN_PART, 128), F32),
        pltpu.VMEM((slots, FFN_PART, 128), F32),
        pltpu.VMEM((slots, 64, 128), F32),
        pltpu.VMEM((slots, 64, 128), F32),
        DMA((4, slots)),
    ]
    if final:
        ready = [pltpu.VMEM((64 * 8, 128), F32)] + ready
    outs = LAST if final else PLACED
    return pl.pallas_call(
        body,
        out_shape=WEIGHT_GRADS + outs,
        in_specs=[SM] + [VM] * count + ([HBM] * 4 + [VM] * 2 if placed else []),
        out_specs=[HBM] * 4 + [VM] * len(outs),
        scratch_shapes=ready,
        input_output_aliases={1 + count + i: i for i in range(4)} if placed else {},
        compiler_params=limit(12),
        cost_estimate=HEAVY,
        name="place_gradients",
    )(place, *[source[0] for source in sources], *placed)


def swap(value):
    return lax.ppermute(value, "section", [(0, 1), (1, 0)])


def from_ahead(value, stage, distance):
    pairs = []
    for section in range(2):
        stride = WAY[section][stage]
        for dst in range(64):
            at = dst // stride % 4
            src = dst + ((at + distance) % 4 - at) * stride
            pairs.append((section * 64 + src, section * 64 + dst))
    return lax.ppermute(value, ("section", "dp"), pairs)


def send_ahead(pieces, stage):
    return [pieces[0]] + [from_ahead(pieces[r], stage, 4 - r) for r in (2, 1, 3)]


def gather(chunk):
    line = jnp.stack([chunk] + [from_ahead(chunk, 0, r) for r in (1, 2, 3)])
    ahead = [from_ahead(line, 1, r) for r in (1, 2, 3)]
    own_a = jnp.concatenate([line, ahead[0]], 0)
    own_b = jnp.concatenate([ahead[1], ahead[2]], 0)
    next_a = from_ahead(own_a, 2, 1)
    prev_b = from_ahead(own_b, 2, 3)
    next_b = from_ahead(own_b, 2, 1)
    prev_a = from_ahead(own_a, 2, 3)
    far_a = from_ahead(next_a, 2, 1)
    far_b = from_ahead(prev_b, 2, 3)
    return own_a, own_b, next_a, next_b, far_a, far_b, prev_a, prev_b


def hold(*values):
    return tuple(pltpu.with_memory_space_constraint(value, pltpu.HBM) for value in values)


def shards(
    tokens,
    lengths,
    out_cotangent,
    pos_table,
    w_qkv,
    w_out,
    b_out,
    norm1_gain,
    norm1_bias,
    w_up,
    b_up,
    w_down,
    b_down,
    norm2_gain,
    norm2_bias,
):
    section = lax.axis_index("section")
    place = jnp.stack([section, lax.axis_index("dp")]).astype(jnp.int32)
    place = jnp.concatenate([place, lengths.reshape(4)])
    vec = pack_vectors(b_out, norm1_gain, norm1_bias, b_down, norm2_gain, norm2_bias, b_up)
    got_qkv = swap(w_qkv)
    got_pos = swap(pos_table)
    got_out = swap(w_out)
    late_up, late_down, got_qkv = lax.optimization_barrier((w_up, w_down, got_qkv))
    mine = hold(pos_table, w_qkv, w_out, w_up, w_down) + (vec,)
    other = (got_pos, got_qkv, got_out, swap(late_up), swap(late_down), swap(vec))
    tokens, out_cotangent = hold(tokens, out_cotangent)
    attention_0 = forward_first(place, tokens, mine, other)
    middle = forward_middle(place, out_cotangent, mine, other, attention_0[3])
    feed_0, stream, attention_1, output = middle[0:4], middle[4], middle[5:9], middle[9]
    after, small, ffn_both, ffn_send = middle[10:14]

    def tie(*values):
        return lax.optimization_barrier(values)

    ffn_got = swap(ffn_send)
    before = out_back(1, place, mine, other, after, attention_1, small)
    pieces = pair_sum(place, ffn_both, ffn_got)
    before, pieces = tie(before, pieces)
    late_ffn = send_ahead(pieces, 2)
    att_both, att_send, after, small, ffn_both, ffn_send = late_back(
        place, mine, other, stream, attention_1, before, feed_0
    )
    after, late_ffn = tie(after, late_ffn)
    att_got = swap(att_send)
    ffn_got = swap(ffn_send)
    before = out_back(0, place, mine, other, after, attention_0, small)
    pieces = pair_sum(place, ffn_both, ffn_got, att_both, att_got)
    before, pieces = tie(before, pieces)
    mixed = send_ahead(pieces, 2)
    arriving, att_both, att_send = last_back(place, tokens, mine, other, attention_0, before)
    att_send, mixed = tie(att_send, mixed)
    pieces = pair_sum(place, att_both, swap(att_send))
    early = send_ahead(early_line_sum(late_ffn, mixed), 1)
    last = send_ahead(line_sum(send_ahead(pieces, 2)), 1)
    pieces = plane_sum(early, last)
    own, others = cube_sum(place, send_ahead(pieces, 0))
    chunk = jnp.stack([own, swap(others)])
    own_a, own_b, next_a, next_b, far_a, far_b, prev_a, prev_b = gather(chunk)
    sources = [(own_a, 0, 0), (own_b, 0, 2), (next_a, 1, 0), (prev_b, 3, 2)]
    placed = place_gradients(place, sources)
    placed = place_gradients(place, [(next_b, 1, 2), (prev_a, 3, 0)], placed)
    up, down, qkv, out, position, bias, gain_one, shift_one, bias_up, bias_down, gain_two, shift_two = (
        place_gradients(place, [(far_a, 2, 0), (far_b, 2, 2)], placed, True)
    )
    return (
        output[None],
        arriving[None],
        position,
        qkv,
        out,
        bias,
        gain_one,
        shift_one,
        up,
        bias_up,
        down,
        bias_down,
        gain_two,
        shift_two,
    )


def solution(mesh):
    placed = (
        P(None, "dp", None, None),
        P(None, "dp"),
        P(None, "dp", None, None),
        P("section", None, None),
        P("section", None, None),
        P("section", None, None),
        P("section", None),
        P("section", None),
        P("section", None),
        P("section", None, None),
        P("section", None),
        P("section", None, None),
        P("section", None),
        P("section", None),
        P("section", None),
    )
    return jax.shard_map(
        shards,
        mesh=mesh,
        in_specs=placed,
        out_specs=(
            P("section", "dp", None, None),
            P("section", "dp", None, None),
            P("section", None, None),
            P("section", None, None),
            P("section", None, None),
            P("section", None),
            P("section", None),
            P("section", None),
            P("section", None, None),
            P("section", None),
            P("section", None, None),
            P("section", None),
            P("section", None),
            P("section", None),
        ),
        check_vma=False,
    )
```
